32 devices in a mesh: batch: 4 (over z), col: 4 (over x, core), rep: 2 (over y).
Axes of the slice: x: 2, y: 2, z: 4, core: 2. Of those that a mesh axis runs over, the one named last changes fastest.
Arguments:
- lookups: bfloat16 [8192, 1024], P(('rep', 'batch'), 'col'), parts along dimension 0, may hold values from -6 to 6
- input_weight: bfloat16 [1024, 1024], replicated, may hold values from -0.1875 to 0.1875
- joined_weight: bfloat16 [1024, 2048], replicated, may hold values from -0.1875 to 0.1875
- output_weight: bfloat16 [512, 1024], replicated, may hold values from -0.25 to 0.25
- owner_counts: int32 [32, 4], P(('rep', 'batch', 'col')), parts along dimension 0, may hold values from 1 to 96, 256 in all within a row
- user_index: int32 [8192], P(('rep', 'batch', 'col')), parts along dimension 0, may hold values from 0 to 7
Outputs:
- layer_out: bfloat16 [8192, 1024], P(('rep', 'batch', 'col')), parts along dimension 0
The draws below stay inside these ranges and needn't reach their ends.
There are 2 independent parts, one for each index of `rep`. The reference program is written for one: setup_inputs(seed, part) draws one part's arguments, and reference() takes and returns one part's arrays. A program takes and returns all parts, laid end to end along the dimension named above; an argument that names none is the same for every part. Nothing has to cross between parts.
Inputs may be any that keep to these rules, and one draw needn't show every extreme that they name: `owner_counts`: each row sums to 256; every entry is 1 or more and each row reaches 96.
All inputs are finite; a program needn't handle non-finite values.
Results may differ from the reference program's by a relative error of at most 0.0071.
Values may be sent and summed in bfloat16 or wider, within the bound.
No kernel may reach another device: no remote copies, remote signals or barrier semaphores. Data moves between devices by JAX's collectives and lax.ppermute only.
A program may use at most 64 MiB of HBM per device.

```python
import math
import jax
import jax.numpy as jnp
import numpy as np
from jax import lax

D = 1024
HEADS = 4
HEAD_DIM = 128
USERS = 8
TOK_DEV = 256
CAP = 96
TOKENS = 4096
N_BATCH = 4
N_COL = 4


def plant(array, stream_key, least, high):
    longest = array.shape.index(max(array.shape))
    spots = []
    for shift in (0, 1):
        where = [jax.random.randint(jax.random.fold_in(stream_key, axis), (), 0, length) for axis, length in enumerate(array.shape)]
        where[longest] = (where[longest] + shift) % array.shape[longest]
        spots.append(tuple(where))
    return array.at[spots[0]].set(least).at[spots[1]].set(high)


def levels(rng, shape, pieces, smallest, high):
    def one(axis_at, parts):
        draws = jax.random.uniform(jax.random.fold_in(jax.random.fold_in(rng, 6), axis_at), (parts,), jnp.float32, smallest / len(pieces), high / len(pieces))
        return jnp.repeat(jnp.exp(draws), shape[axis_at] // parts).reshape((-1,) + (1,) * (len(shape) - axis_at - 1))

    level = one(*pieces[0])
    for cut in pieces[1:]:
        level = level * one(*cut)
    return level


def cumulative_ranks(number_of, lean):
    portions = [(1 << 20) // math.isqrt(standing ** lean) + 1 for standing in range(1, number_of + 1)]
    scale = 1 + sum(portions) // (1 << 30)
    return np.cumsum(np.array([max(1, weight // scale) for weight in portions]))


def ranked_ids(rng, extent, count, slope):
    listing = cumulative_ranks(count, slope)
    pick = jax.random.randint(jax.random.fold_in(rng, 1), extent, 0, int(listing[count - 1]))
    grade = jnp.searchsorted(jnp.asarray(listing, jnp.int32), pick, side="right")
    return jax.random.permutation(jax.random.fold_in(rng, 2), count)[grade].astype(jnp.int32)


def length_profile(count, total, reach, lean):
    weights = [(1 << 20) // math.isqrt(rank ** lean) + 1 for rank in range(2, count + 1)]
    rest, given = total - reach - (count - 1), [1] * (count - 1)
    while rest > 0:
        candidates = [i for i in range(count - 1) if given[i] < reach]
        whole, budget = sum([weights[i] for i in candidates]), rest
        for i in candidates:
            addition = min(reach - given[i], max(1, budget * weights[i] // whole), rest)
            given[i] = given[i] + addition
            rest = rest - addition
    return np.array([reach] + given)


def uneven_parts(key, number_of, total, limit, lean):
    if number_of == 2:
        one = jax.random.randint(key, (), max(1, total - limit), min(limit, total - 1) + 1)
        return jnp.stack([one, total - one])
    lengths = jnp.asarray(length_profile(number_of, total, limit, lean), jnp.int32)
    pairs = (number_of - 1) // 2
    donor, taker = lengths[1:1 + 2 * pairs:2], lengths[2:2 + 2 * pairs:2]
    room = jnp.minimum(donor - 1, limit - taker)
    shifted = jax.random.randint(jax.random.fold_in(key, 1), (pairs,), 0, 1 << 20) % (room + 1)
    lengths = lengths.at[1:1 + 2 * pairs:2].set(donor - shifted).at[2:2 + 2 * pairs:2].set(taker + shifted)
    return lengths[jax.random.permutation(jax.random.fold_in(key, 2), number_of)]


def gaussian(stream_key, dims, deviation, most, cuts=(), kind=jnp.bfloat16):
    array = deviation * jax.random.normal(stream_key, dims, jnp.float32)
    if cuts:
        array = array * levels(stream_key, dims, cuts, -0.22, 0.18)
    return jnp.clip(array, -most, most).astype(kind)


def setup_inputs(seed: int = 0, part: int = 0) -> dict:
    splits = jax.random.split(jax.random.key(seed), 7)
    own_keys = jax.random.split(jax.random.fold_in(splits[6], part), 7)
    lookups = gaussian(own_keys[0], (TOKENS, D), 1.0, 6.0, ((0, 4), (1, 4)))
    input_weight = gaussian(splits[1], (D, D), D ** -0.5, 0.1875)
    joined_weight = gaussian(splits[2], (D, 4 * HEADS * HEAD_DIM), D ** -0.5, 0.1875)
    output_weight = gaussian(splits[3], (HEADS * HEAD_DIM, D), (HEADS * HEAD_DIM) ** -0.5, 0.25)
    owner_counts = jax.vmap(lambda own: uneven_parts(own, N_BATCH, TOK_DEV, CAP, 1))(jax.random.split(own_keys[4], (N_BATCH * N_COL))).reshape((N_BATCH * N_COL, N_BATCH)).astype(jnp.int32)
    user_index = plant(ranked_ids(own_keys[5], (TOKENS,), USERS, 2), jax.random.fold_in(own_keys[5], 3), 0, USERS - 1).astype(jnp.int32)
    return dict(lookups=lookups, input_weight=input_weight, joined_weight=joined_weight, output_weight=output_weight, owner_counts=owner_counts, user_index=user_index)


eps_norm = 1e-06

def layer_norm(values):
    row_mean = lax.optimization_barrier(jnp.mean(values, axis=-1, keepdims=True))
    centered = values - row_mean
    row_var = lax.optimization_barrier(jnp.mean(centered * centered, axis=-1, keepdims=True))
    return centered * lax.rsqrt(row_var + eps_norm)

def attend(joined_rows, seg_ids):
    width = HEADS * HEAD_DIM
    total = joined_rows.shape[0]
    gate_part = joined_rows[:, :width].astype(jnp.float32)
    value_part = joined_rows[:, width:2 * width].astype(jnp.float32).reshape(total, HEADS, HEAD_DIM)
    query_part = joined_rows[:, 2 * width:3 * width].astype(jnp.float32).reshape(total, HEADS, HEAD_DIM)
    key_part = joined_rows[:, 3 * width:].astype(jnp.float32).reshape(total, HEADS, HEAD_DIM)
    scores = jnp.einsum('ihd,jhd->hij', query_part, key_part) * HEAD_DIM ** (-0.5)
    positions = jnp.arange(total, dtype=jnp.int32)
    allowed = (positions[None, :] <= positions[:, None]) & (seg_ids[None, :] == seg_ids[:, None])
    weights = jnp.where(allowed[None], jax.nn.silu(scores), 0.0).astype(jnp.bfloat16)
    mixed = jnp.einsum('hij,jhd->ihd', weights.astype(jnp.float32), value_part).reshape(total, width)
    return (layer_norm(mixed) * gate_part).astype(jnp.bfloat16)

def reference(lookups, input_weight, joined_weight, output_weight, owner_counts, user_index):
    hidden = jnp.dot(lookups, input_weight, preferred_element_type=jnp.float32).astype(jnp.bfloat16)
    normed = layer_norm(hidden.astype(jnp.float32)).astype(jnp.bfloat16)
    joined = jax.nn.silu(jnp.dot(normed, joined_weight, preferred_element_type=jnp.float32)).astype(jnp.bfloat16)
    bin_starts = (jnp.cumsum(owner_counts, axis=1) - owner_counts).astype(jnp.int32)
    slot_ids = jnp.arange(CAP, dtype=jnp.int32)

    def owner_slots(owner_index):
        col_index = owner_index % N_COL
        dest_owner = owner_index // N_COL
        sources = (jnp.arange(N_BATCH, dtype=jnp.int32) * N_COL + col_index).astype(jnp.int32)
        counts = owner_counts[sources, dest_owner]
        offsets = bin_starts[sources, dest_owner]
        token_rows = (sources * TOK_DEV + offsets)[:, None] + slot_ids[None, :]
        filled = slot_ids[None, :] < counts[:, None]
        return (token_rows.reshape(-1).astype(jnp.int32), filled.reshape(-1))

    def per_owner(owner_index):
        token_rows, filled = owner_slots(owner_index)
        safe_rows = jnp.where(filled, token_rows, 0).astype(jnp.int32)
        seg_ids = jnp.where(filled, user_index[safe_rows], -1).astype(jnp.int32)
        gated = attend(joined[safe_rows], seg_ids)
        return jnp.dot(gated, output_weight, preferred_element_type=jnp.float32).astype(jnp.bfloat16)
    owner_ids = jnp.arange(N_BATCH * N_COL, dtype=jnp.int32)
    branches = lax.map(per_owner, owner_ids)
    token_rows, filled = jax.vmap(owner_slots)(owner_ids)
    targets = jnp.where(filled, token_rows, TOKENS).reshape(-1).astype(jnp.int32)
    placed = jnp.zeros((TOKENS, D), jnp.bfloat16).at[targets].set(branches.reshape(-1, D), mode='drop')
    return (hidden.astype(jnp.float32) + placed.astype(jnp.float32)).astype(jnp.bfloat16)
```

```python
import functools

import jax
import jax.numpy as jnp
from jax import lax
from jax.experimental import pallas as pl
from jax.experimental.pallas import tpu as pltpu
from jax.sharding import PartitionSpec as P

HEADS = 4
HEAD_DIM = 128
SEG_ROWS = 8

eps_norm = 1e-06

F32 = jnp.float32
BF16 = jnp.bfloat16


def layer_norm(values):
    row_mean = jnp.mean(values, axis=-1, keepdims=True)
    centered = values - row_mean
    row_var = jnp.mean(centered * centered, axis=-1, keepdims=True)
    return centered * lax.rsqrt(row_var + eps_norm)


def project(hidden_rows, joined_weight):
    normed = layer_norm(hidden_rows.astype(F32)).astype(BF16)
    return jax.nn.silu(jnp.dot(normed, joined_weight, preferred_element_type=F32)).astype(BF16)


def attend(joined_rows, seg_ids):
    width = HEADS * HEAD_DIM
    total = joined_rows.shape[0]
    gate_part = joined_rows[:, :width]
    value_part = joined_rows[:, width : 2 * width].reshape(total, HEADS, HEAD_DIM)
    query_part = joined_rows[:, 2 * width : 3 * width].reshape(total, HEADS, HEAD_DIM)
    key_part = joined_rows[:, 3 * width :].reshape(total, HEADS, HEAD_DIM)
    scores = jnp.einsum(
        "ihd,jhd->hij", query_part, key_part, preferred_element_type=F32
    ) * HEAD_DIM ** (-0.5)
    positions = jnp.arange(total, dtype=jnp.int32)
    allowed = (positions[None, :] <= positions[:, None]) & (seg_ids[None, :] == seg_ids[:, None])
    weights = jnp.where(allowed[None], jax.nn.silu(scores), 0.0).astype(BF16)
    mixed = jnp.einsum(
        "hij,jhd->ihd", weights, value_part, preferred_element_type=F32
    ).reshape(total, width)
    return (layer_norm(mixed) * gate_part.astype(F32)).astype(BF16)


def owners_plan(lookups, input_weight, joined_weight, output_weight, owner_counts, user_index):
    token_block = lax.all_to_all(lookups, "col", split_axis=0, concat_axis=1, tiled=True)
    hidden = jnp.dot(token_block, input_weight, preferred_element_type=F32).astype(BF16)
    local_rows = hidden.shape[0]
    owners = lax.axis_size("batch")
    capacity = local_rows // owners + local_rows // (2 * owners)
    counts = owner_counts[0]
    bin_ends = jnp.cumsum(counts)
    bin_starts = bin_ends - counts
    slot_ids = jnp.arange(capacity, dtype=jnp.int32)
    filled = slot_ids[None, :] < counts[:, None]
    gather_rows = jnp.where(filled, bin_starts[:, None] + slot_ids[None, :], 0).reshape(-1)
    seg_send = jnp.where(filled.reshape(-1), user_index[gather_rows], -1).reshape(owners, capacity)
    payload = hidden[gather_rows].reshape(owners, capacity, -1)
    received, seg_ids = (
        lax.all_to_all(payload, "batch", split_axis=0, concat_axis=0, tiled=True),
        lax.all_to_all(seg_send, "batch", split_axis=0, concat_axis=0, tiled=True),
    )
    joined_rows = project(received.reshape(owners * capacity, -1), joined_weight)
    gated_rows = attend(joined_rows, seg_ids.reshape(-1))
    token_pos = jnp.arange(local_rows, dtype=jnp.int32)
    owner_ids = jnp.arange(owners, dtype=jnp.int32)
    dest_owner = jnp.sum((token_pos[:, None] >= bin_ends[None, :]).astype(jnp.int32), axis=1)
    onehot = dest_owner[:, None] == owner_ids[None, :]
    first_slot = jnp.sum(jnp.where(onehot, bin_starts[None, :], 0), axis=1)
    back_rows = dest_owner * capacity + token_pos - first_slot
    returned = lax.all_to_all(
        gated_rows.reshape(owners, capacity, -1), "batch", split_axis=0, concat_axis=0, tiled=True
    )
    own_gated = returned.reshape(owners * capacity, -1)[back_rows]
    branch_rows = jnp.dot(own_gated, output_weight, preferred_element_type=F32).astype(BF16)
    return (hidden.astype(F32) + branch_rows.astype(F32)).astype(BF16)


def silu_of(values):
    half = 0.5 * values
    return half + half * jnp.tanh(half)


def head_weights(query, key, allowed):
    scores = lax.dot_general(query, key, (((1,), (1,)), ((), ())), preferred_element_type=F32)
    half = scores * (0.5 * HEAD_DIM ** (-0.5))
    return jnp.where(allowed, half + half * jnp.tanh(half), 0.0).astype(BF16)


def seg_column(seg_row):
    wide = jnp.broadcast_to(seg_row, (128, seg_row.shape[1]))
    return wide.T[:, :1]


def project_kernel(
    place, counts, own, part1, part2, part3, w_in, w_joined, users,
    hidden_out, gate_out, qkv_out, seg_out, send_a, send_b, send_c, normed,
):
    batch_at, col_at = place[0], place[1]
    rows, piece = own.shape
    group = qkv_out.shape[2] // 3
    total = None
    for shift, part in enumerate((own, part1, part2, part3)):
        start = pl.multiple_of((col_at ^ shift) * piece, piece)
        term = jnp.dot(part[...], w_in[pl.ds(start, piece), :], preferred_element_type=F32)
        total = term if total is None else total + term
    hidden = total.astype(BF16)
    hidden_out[...] = hidden
    normed[...] = layer_norm(hidden.astype(F32)).astype(BF16)

    owners = counts.shape[1]
    position = lax.broadcasted_iota(jnp.int32, (1, rows), 1)
    end = counts[0, 0]
    owner = (position >= end).astype(jnp.int32)
    for d in range(1, owners - 1):
        end = end + counts[0, d]
        owner = owner + (position >= end).astype(jnp.int32)
    seg_row = (owner + owners * users[...]).astype(F32)
    seg = jnp.broadcast_to(seg_row, (SEG_ROWS, rows))
    seg_out[...] = seg

    width = 2 * group
    for kind, base in ((1, 3), (2, 1), (0, 2)):
        for g in range(2):
            at = base * width + g * group
            block = jnp.dot(normed[...], w_joined[:, at : at + group], preferred_element_type=F32)
            qkv_out[g, :, kind * group : (kind + 1) * group] = silu_of(block).astype(BF16)
    near = batch_at % 2
    far = 1 - near
    send_b[:rows, :] = qkv_out[far, :, group:]
    send_c[:rows, :] = qkv_out[far, :, :group]
    send_b[rows:, :rows] = seg.astype(BF16)
    send_b[rows:, rows:] = seg.astype(BF16)
    send_c[rows:, :] = seg.astype(BF16)
    send_a[rows:, :rows] = seg.astype(BF16)
    send_a[rows:, rows:] = seg.astype(BF16)

    @pl.when(batch_at == 0)
    def _():
        send_a[:rows, :] = qkv_out[near, :, group:]

    @pl.when(batch_at != 0)
    def _():
        which = jnp.where(batch_at == 1, far, near)
        send_a[:rows, :group] = qkv_out[which, :, :group]
        send_a[:rows, group:] = jnp.zeros((rows, group), BF16)

    for g in range(2):
        at = g * group
        block = jnp.dot(normed[...], w_joined[:, at : at + group], preferred_element_type=F32)
        gate_out[:, at : at + group] = silu_of(block).astype(BF16)


def diagonal_kernel(qkv, seg, mixed_out):
    rows = qkv.shape[1]
    group = qkv.shape[2] // 3
    seg_row = seg[0:1, :]
    allowed = (seg_column(seg_row) == seg_row) & (
        lax.broadcasted_iota(jnp.int32, (rows, rows), 1)
        <= lax.broadcasted_iota(jnp.int32, (rows, rows), 0)
    )
    for g in range(2):
        for h in range(group // HEAD_DIM):
            lo = h * HEAD_DIM
            weights = head_weights(
                qkv[g, :, lo : lo + HEAD_DIM], qkv[g, :, group + lo : group + lo + HEAD_DIM], allowed
            )
            value = qkv[g, :, 2 * group + lo : 2 * group + lo + HEAD_DIM]
            mixed_out[g, :, lo : lo + HEAD_DIM] = jnp.dot(weights, value, preferred_element_type=F32)


def seg_row_of(ref, rows):
    return ref[rows : rows + SEG_ROWS, :rows].astype(F32)[0:1, :]


def far_kernel(place, qkv, seg, got_a, got_b, got_c, send_d, send_e):
    batch_at = place[0]
    rows = qkv.shape[1]
    group = qkv.shape[2] // 3
    near = batch_at % 2

    def block(query, query_at, key_value, key_at, allowed, h):
        lo = h * HEAD_DIM
        weights = head_weights(
            query(query_at + lo), key_value(key_at + lo), allowed
        )
        return jnp.dot(weights, key_value(key_at + group + lo), preferred_element_type=F32)

    def own(at):
        return qkv[near, :, at : at + HEAD_DIM]

    def of(ref):
        return lambda at: ref[:rows, at : at + HEAD_DIM]

    seg_own = seg[0:1, :]
    seg_a, seg_b, seg_c = (seg_row_of(ref, rows) for ref in (got_a, got_b, got_c))

    def run(query_ref, query_seg, others, out):
        column = seg_column(query_seg)
        masks = [column == row for _, _, row in others]
        for h in range(group // HEAD_DIM):
            total = None
            for (key_value, key_at, _), allowed in zip(others, masks):
                term = block(of(query_ref), 0, key_value, key_at, allowed, h)
                total = term if total is None else total + term
            out[:, h * HEAD_DIM : (h + 1) * HEAD_DIM] = total.astype(BF16)

    from_own = (own, group, seg_own)
    from_a = (of(got_a), 0, seg_a)
    from_b = (of(got_b), 0, seg_b)

    @pl.when(batch_at == 0)
    def _():
        run(got_a, seg_a, [from_own], send_d)
        send_e[...] = jnp.zeros_like(send_e)

    @pl.when(batch_at == 1)
    def _():
        run(got_c, seg_c, [from_own, from_b], send_d)
        run(got_a, seg_a, [from_own, from_b], send_e)

    @pl.when(batch_at == 2)
    def _():
        run(got_c, seg_c, [from_own, from_b, from_a], send_d)
        send_e[...] = jnp.zeros_like(send_e)

    @pl.when(batch_at == 3)
    def _():
        send_d[...] = jnp.zeros_like(send_d)
        send_e[...] = jnp.zeros_like(send_e)


def near_kernel(place, qkv, seg, got_a, got_b, mixed, near_out):
    batch_at = place[0]
    rows = qkv.shape[1]
    group = qkv.shape[2] // 3
    near = batch_at % 2
    column = seg_column(seg[0:1, :])
    near_out[...] = mixed[near]

    def add(ref):
        allowed = column == seg_row_of(ref, rows)
        for h in range(group // HEAD_DIM):
            lo = h * HEAD_DIM
            weights = head_weights(
                qkv[near, :, lo : lo + HEAD_DIM], ref[:rows, lo : lo + HEAD_DIM], allowed
            )
            near_out[:, lo : lo + HEAD_DIM] += jnp.dot(
                weights, ref[:rows, group + lo : group + lo + HEAD_DIM], preferred_element_type=F32
            )

    @pl.when(batch_at > 0)
    def _():
        add(got_b)

    @pl.when(batch_at == 2)
    def _():
        add(got_a)


def finish_kernel(place, mixed, near_mixed, got_d, got_e, gate, hidden, w_out, out, whole):
    near = place[0] % 2
    group = near_mixed.shape[1]
    whole[near] = near_mixed[...] + got_e[...].astype(F32)
    whole[1 - near] = mixed[1 - near] + got_d[...].astype(F32)
    both = jnp.concatenate([whole[0], whole[1]], axis=1)
    gated = (layer_norm(both) * gate[...].astype(F32)).astype(BF16)
    branch = jnp.dot(gated, w_out[...], preferred_element_type=F32).astype(BF16)
    out[...] = (hidden[...].astype(F32) + branch.astype(F32)).astype(BF16)


VMEM = pl.BlockSpec(memory_space=pltpu.VMEM)
SMEM = pl.BlockSpec(memory_space=pltpu.SMEM)


def call(kernel, in_specs, outs, operands, flops, scratch=(), limit=32 << 20):
    return pl.pallas_call(
        kernel,
        out_shape=[jax.ShapeDtypeStruct(shape, dtype) for shape, dtype in outs],
        in_specs=in_specs,
        out_specs=[VMEM] * len(outs),
        scratch_shapes=list(scratch),
        compiler_params=pltpu.CompilerParams(vmem_limit_bytes=limit),
        cost_estimate=pl.CostEstimate(flops=flops, bytes_accessed=flops // 256, transcendentals=0),
    )(*operands)


def chain_plan(lookups, input_weight, joined_weight, output_weight, owner_counts, user_index):
    cols = lax.axis_size("col")
    batch_at = lax.axis_index("batch").astype(jnp.int32)
    col_at = lax.axis_index("col").astype(jnp.int32)
    place = jnp.stack([batch_at, col_at])
    pieces = lookups.reshape(cols, lookups.shape[0] // cols, lookups.shape[1])
    rows = pieces.shape[1]

    def piece(shift):
        return lax.dynamic_index_in_dim(pieces, col_at ^ shift, 0, keepdims=False)

    got = [piece(0)] + [
        lax.ppermute(piece(shift), "col", [(i, i ^ shift) for i in range(cols)])
        for shift in range(1, cols)
    ]
    width = HEADS * HEAD_DIM
    group = width // 2
    features = input_weight.shape[1]
    hidden, gate, qkv, seg, send_a, send_b, send_c = call(
        project_kernel,
        [SMEM, SMEM] + [VMEM] * 7,
        [
            ((rows, features), BF16),
            ((rows, width), BF16),
            ((2, rows, 3 * group), BF16),
            ((SEG_ROWS, rows), F32),
            ((rows + SEG_ROWS, 2 * group), BF16),
            ((rows + SEG_ROWS, 2 * group), BF16),
            ((rows + SEG_ROWS, group), BF16),
        ],
        (place, owner_counts, *got, input_weight, joined_weight, user_index.reshape(1, rows)),
        2 * rows * features * (features + 4 * width),
        [pltpu.VMEM((rows, features), BF16)],
    )
    got_a = lax.ppermute(send_a, "batch", [(0, 2), (3, 1), (1, 0)])
    got_b = lax.ppermute(send_b, "batch", [(0, 1), (1, 2), (2, 3)])
    got_c = lax.ppermute(send_c, "batch", [(2, 1), (3, 2)])
    pair_flops = 4 * rows * rows * group
    (mixed,) = call(
        diagonal_kernel, [VMEM] * 2, [((2, rows, group), F32)], (qkv, seg), 2 * pair_flops
    )
    send_d, send_e = call(
        far_kernel,
        [SMEM] + [VMEM] * 5,
        [((rows, group), BF16)] * 2,
        (place, qkv, seg, got_a, got_b, got_c),
        4 * pair_flops,
    )
    got_d = lax.ppermute(send_d, "batch", [(0, 1), (1, 2), (2, 3)])
    got_e = lax.ppermute(send_e, "batch", [(1, 3)])
    (near_mixed,) = call(
        near_kernel,
        [SMEM] + [VMEM] * 5,
        [((rows, group), F32)],
        (place, qkv, seg, got_a, got_b, mixed),
        2 * pair_flops,
    )
    (out,) = call(
        finish_kernel,
        [SMEM] + [VMEM] * 7,
        [((rows, features), BF16)],
        (place, mixed, near_mixed, got_d, got_e, gate, hidden, output_weight),
        2 * rows * width * features,
        [pltpu.VMEM((2, rows, group), F32)],
    )
    return out


def solution(mesh):
    chain = mesh.shape["batch"] == HEADS and mesh.shape["col"] & (mesh.shape["col"] - 1) == 0
    return jax.shard_map(
        chain_plan if chain else owners_plan,
        mesh=mesh,
        in_specs=(
            P(("rep", "batch"), "col"),
            P(),
            P(),
            P(),
            P(("rep", "batch", "col"), None),
            P(("rep", "batch", "col")),
        ),
        out_specs=P(("rep", "batch", "col"), None),
        check_vma=False,
    )
```

```python
import functools

import jax
import jax.numpy as jnp
from jax import lax
from jax.experimental import pallas as pl
from jax.experimental.pallas import tpu as pltpu
from jax.sharding import PartitionSpec as P

HEADS = 4
HEAD_DIM = 128
SEG_ROWS = 8

eps_norm = 1e-06

F32 = jnp.float32
BF16 = jnp.bfloat16


def layer_norm(values):
    row_mean = jnp.mean(values, axis=-1, keepdims=True)
    centered = values - row_mean
    row_var = jnp.mean(centered * centered, axis=-1, keepdims=True)
    return centered * lax.rsqrt(row_var + eps_norm)


def project(hidden_rows, joined_weight):
    normed = layer_norm(hidden_rows.astype(F32)).astype(BF16)
    return jax.nn.silu(jnp.dot(normed, joined_weight, preferred_element_type=F32)).astype(BF16)


def attend(joined_rows, seg_ids):
    width = HEADS * HEAD_DIM
    total = joined_rows.shape[0]
    gate_part = joined_rows[:, :width]
    value_part = joined_rows[:, width : 2 * width].reshape(total, HEADS, HEAD_DIM)
    query_part = joined_rows[:, 2 * width : 3 * width].reshape(total, HEADS, HEAD_DIM)
    key_part = joined_rows[:, 3 * width :].reshape(total, HEADS, HEAD_DIM)
    scores = jnp.einsum(
        "ihd,jhd->hij", query_part, key_part, preferred_element_type=F32
    ) * HEAD_DIM ** (-0.5)
    positions = jnp.arange(total, dtype=jnp.int32)
    allowed = (positions[None, :] <= positions[:, None]) & (seg_ids[None, :] == seg_ids[:, None])
    weights = jnp.where(allowed[None], jax.nn.silu(scores), 0.0).astype(BF16)
    mixed = jnp.einsum(
        "hij,jhd->ihd", weights, value_part, preferred_element_type=F32
    ).reshape(total, width)
    return (layer_norm(mixed) * gate_part.astype(F32)).astype(BF16)


def owners_plan(lookups, input_weight, joined_weight, output_weight, owner_counts, user_index):
    token_block = lax.all_to_all(lookups, "col", split_axis=0, concat_axis=1, tiled=True)
    hidden = jnp.dot(token_block, input_weight, preferred_element_type=F32).astype(BF16)
    local_rows = hidden.shape[0]
    owners = lax.axis_size("batch")
    capacity = local_rows // owners + local_rows // (2 * owners)
    counts = owner_counts[0]
    bin_ends = jnp.cumsum(counts)
    bin_starts = bin_ends - counts
    slot_ids = jnp.arange(capacity, dtype=jnp.int32)
    filled = slot_ids[None, :] < counts[:, None]
    gather_rows = jnp.where(filled, bin_starts[:, None] + slot_ids[None, :], 0).reshape(-1)
    seg_send = jnp.where(filled.reshape(-1), user_index[gather_rows], -1).reshape(owners, capacity)
    payload = hidden[gather_rows].reshape(owners, capacity, -1)
    received, seg_ids = (
        lax.all_to_all(payload, "batch", split_axis=0, concat_axis=0, tiled=True),
        lax.all_to_all(seg_send, "batch", split_axis=0, concat_axis=0, tiled=True),
    )
    joined_rows = project(received.reshape(owners * capacity, -1), joined_weight)
    gated_rows = attend(joined_rows, seg_ids.reshape(-1))
    token_pos = jnp.arange(local_rows, dtype=jnp.int32)
    owner_ids = jnp.arange(owners, dtype=jnp.int32)
    dest_owner = jnp.sum((token_pos[:, None] >= bin_ends[None, :]).astype(jnp.int32), axis=1)
    onehot = dest_owner[:, None] == owner_ids[None, :]
    first_slot = jnp.sum(jnp.where(onehot, bin_starts[None, :], 0), axis=1)
    back_rows = dest_owner * capacity + token_pos - first_slot
    returned = lax.all_to_all(
        gated_rows.reshape(owners, capacity, -1), "batch", split_axis=0, concat_axis=0, tiled=True
    )
    own_gated = returned.reshape(owners * capacity, -1)[back_rows]
    branch_rows = jnp.dot(own_gated, output_weight, preferred_element_type=F32).astype(BF16)
    return (hidden.astype(F32) + branch_rows.astype(F32)).astype(BF16)


def silu_of(values):
    half = 0.5 * values
    return half + half * jnp.tanh(half)


def head_weights(query, key, allowed):
    scores = lax.dot_general(query, key, (((1,), (1,)), ((), ())), preferred_element_type=F32)
    half = scores * (0.5 * HEAD_DIM ** (-0.5))
    return jnp.where(allowed, half + half * jnp.tanh(half), 0.0).astype(BF16)


def seg_column(seg_row):
    wide = jnp.broadcast_to(seg_row, (128, seg_row.shape[1]))
    return wide.T[:, :1]


def segments_kernel(counts, users, seg_out):
    rows = users.shape[1]
    owners = counts.shape[1]
    position = lax.broadcasted_iota(jnp.int32, (1, rows), 1)
    end = counts[0, 0]
    owner = (position >= end).astype(jnp.int32)
    for d in range(1, owners - 1):
        end = end + counts[0, d]
        owner = owner + (position >= end).astype(jnp.int32)
    seg_out[...] = jnp.broadcast_to((owner + owners * users[...]).astype(F32), seg_out.shape)


def columns_of(w_joined, block, index, group):
    start = pl.multiple_of(block * 2 * group + index * group, group)
    return w_joined[:, pl.ds(start, group)]


def put_seg(ref, seg):
    rows = seg.shape[1]
    for at in range(0, ref.shape[1], rows):
        ref[rows:, at : at + rows] = seg.astype(BF16)


def project_first_kernel(
    place, own, part1, part2, part3, w_in, w_joined, seg, hidden_out, normed, send_b
):
    batch_at, col_at = place[0], place[1]
    rows, piece = own.shape
    group = send_b.shape[1] // 2
    total = None
    for shift, part in enumerate((own, part1, part2, part3)):
        start = pl.multiple_of((col_at ^ shift) * piece, piece)
        term = jnp.dot(part[...], w_in[pl.ds(start, piece), :], preferred_element_type=F32)
        total = term if total is None else total + term
    hidden = total.astype(BF16)
    hidden_out[...] = hidden
    normed[...] = layer_norm(hidden.astype(F32)).astype(BF16)
    far = 1 - batch_at % 2
    for at, block in ((0, 3), (group, 1)):
        joined = jnp.dot(
            normed[...], columns_of(w_joined, block, far, group), preferred_element_type=F32
        )
        send_b[:rows, at : at + group] = silu_of(joined).astype(BF16)
    put_seg(send_b, seg[...])


def project_rest_kernel(place, normed, w_joined, seg, send_a, send_c, send_f, query_near):
    batch_at = place[0]
    rows = normed.shape[0]
    group = send_c.shape[1]
    near = batch_at % 2

    def joined(block, index):
        return silu_of(
            jnp.dot(
                normed[...], columns_of(w_joined, block, index, group), preferred_element_type=F32
            )
        ).astype(BF16)

    query_near[...] = joined(2, near)
    send_c[:rows, :] = joined(2, 1 - near)
    put_seg(send_c, seg[...])
    put_seg(send_f, seg[...])

    @pl.when(batch_at == 1)
    def _():
        send_f[:rows, :] = send_c[:rows, :]

    @pl.when(batch_at != 1)
    def _():
        send_f[:rows, :] = query_near[...]

    send_a[:rows, :group] = joined(3, near)
    send_a[:rows, group:] = joined(1, near)
    put_seg(send_a, seg[...])


def seg_row_of(ref, rows):
    return ref[rows : rows + SEG_ROWS, :rows].astype(F32)[0:1, :]


def add_blocks(query, key_values, out):
    group = query.shape[1]
    rows = query.shape[0] - SEG_ROWS
    column = seg_column(seg_row_of(query, rows))
    masks = [column == seg_row_of(ref, rows) for ref in key_values]
    for lo in range(0, group, HEAD_DIM):
        hi = lo + HEAD_DIM
        total = None
        for ref, allowed in zip(key_values, masks):
            weights = head_weights(query[:rows, lo:hi], ref[:rows, lo:hi], allowed)
            term = jnp.dot(
                weights, ref[:rows, group + lo : group + hi], preferred_element_type=F32
            )
            total = term if total is None else total + term
        out[:, lo:hi] = total.astype(BF16)


def add_near(query_near, column, key_value, mixed):
    rows, group = query_near.shape
    allowed = column == seg_row_of(key_value, rows)
    for lo in range(0, group, HEAD_DIM):
        hi = lo + HEAD_DIM
        weights = head_weights(query_near[:, lo:hi], key_value[:rows, lo:hi], allowed)
        mixed[:, lo:hi] += jnp.dot(
            weights, key_value[:rows, group + lo : group + hi], preferred_element_type=F32
        )


def own_kernel(
    place, got_b, query_near, send_a, send_b, send_c, seg, normed, w_joined, mixed_out, gate_out
):
    rows, group = query_near.shape
    seg_row = seg[0:1, :]
    column = seg_column(seg_row)
    allowed = (column == seg_row) & (
        lax.broadcasted_iota(jnp.int32, (rows, rows), 1)
        <= lax.broadcasted_iota(jnp.int32, (rows, rows), 0)
    )
    for side, (query, key_value) in enumerate(((query_near, send_a), (send_c, send_b))):
        for lo in range(0, group, HEAD_DIM):
            hi = lo + HEAD_DIM
            weights = head_weights(query[:rows, lo:hi], key_value[:rows, lo:hi], allowed)
            mixed_out[side, :, lo:hi] = jnp.dot(
                weights, key_value[:rows, group + lo : group + hi], preferred_element_type=F32
            )

    @pl.when(place[0] > 0)
    def _():
        add_near(query_near, column, got_b, mixed_out.at[0])

    for at in range(0, 2 * group, group):
        block = jnp.dot(normed[...], w_joined[:, at : at + group], preferred_element_type=F32)
        gate_out[:, at : at + group] = silu_of(block).astype(BF16)


def far_kernel(place, got_b, mixed, send_a, got_f, got_c, got_a, send_e, send_d):
    @pl.when(place[0] == 0)
    def _():
        add_blocks(got_f, [send_a], send_d)

    @pl.when(place[0] == 1)
    def _():
        add_blocks(got_f, [send_a, got_b], send_e)
        add_blocks(got_c, [send_a, got_b], send_d)

    @pl.when(place[0] == 2)
    def _():
        add_blocks(got_c, [send_a, got_b, got_a], send_d)

    @pl.when(place[0] != 1)
    def _():
        send_e[...] = jnp.zeros_like(send_e)

    @pl.when(place[0] > 2)
    def _():
        send_d[...] = jnp.zeros_like(send_d)


def near_kernel(place, query_near, seg, got_a, mixed, near_out):
    near_out[...] = mixed[0]

    @pl.when(place[0] == 2)
    def _():
        add_near(query_near, seg_column(seg[0:1, :]), got_a, near_out)


def finish_kernel(place, mixed, near_mixed, got_e, got_d, gate, hidden, w_out, out, whole):
    near = place[0] % 2
    whole[near] = near_mixed[...] + got_e[...].astype(F32)
    whole[1 - near] = mixed[1] + got_d[...].astype(F32)
    both = jnp.concatenate([whole[0], whole[1]], axis=1)
    gated = (layer_norm(both) * gate[...].astype(F32)).astype(BF16)
    branch = jnp.dot(gated, w_out[...], preferred_element_type=F32).astype(BF16)
    out[...] = (hidden[...].astype(F32) + branch.astype(F32)).astype(BF16)


VMEM = pl.BlockSpec(memory_space=pltpu.VMEM)
SMEM = pl.BlockSpec(memory_space=pltpu.SMEM)


def call(kernel, in_specs, outs, operands, flops, scratch=(), limit=32 << 20):
    return pl.pallas_call(
        kernel,
        out_shape=[jax.ShapeDtypeStruct(shape, dtype) for shape, dtype in outs],
        in_specs=in_specs,
        out_specs=[VMEM] * len(outs),
        scratch_shapes=list(scratch),
        compiler_params=pltpu.CompilerParams(vmem_limit_bytes=limit),
        cost_estimate=pl.CostEstimate(flops=flops, bytes_accessed=0, transcendentals=0),
    )(*operands)


def chain_plan(lookups, input_weight, joined_weight, output_weight, owner_counts, user_index):
    cols = lax.axis_size("col")
    batch_at = lax.axis_index("batch").astype(jnp.int32)
    col_at = lax.axis_index("col").astype(jnp.int32)
    place = jnp.stack([batch_at, col_at])
    pieces = lookups.reshape(cols, lookups.shape[0] // cols, lookups.shape[1])
    rows = pieces.shape[1]

    def piece(shift):
        return lax.dynamic_index_in_dim(pieces, col_at ^ shift, 0, keepdims=False)

    parts = [piece(0)] + [
        lax.ppermute(piece(shift), "col", [(i, i ^ shift) for i in range(cols)])
        for shift in range(1, cols)
    ]
    width = HEADS * HEAD_DIM
    group = width // 2
    features = input_weight.shape[1]
    tall = rows + SEG_ROWS
    (seg,) = call(
        segments_kernel,
        [SMEM, VMEM],
        [((SEG_ROWS, rows), F32)],
        (owner_counts, user_index.reshape(1, rows)),
        2 * rows * features * (features + 4 * width),
    )
    hidden, normed, send_b = call(
        project_first_kernel,
        [SMEM] + [VMEM] * 7,
        [((rows, features), BF16), ((rows, features), BF16), ((tall, 2 * group), BF16)],
        (place, *parts, input_weight, joined_weight, seg),
        2 * rows * features * (features + 2 * group),
    )
    got_b = lax.ppermute(send_b, "batch", [(0, 1), (1, 2), (2, 3)])
    send_a, send_c, send_f, query_near = call(
        project_rest_kernel,
        [SMEM] + [VMEM] * 3,
        [
            ((tall, 2 * group), BF16),
            ((tall, group), BF16),
            ((tall, group), BF16),
            ((rows, group), BF16),
        ],
        (place, normed, joined_weight, seg),
        2 * rows * features * 4 * group,
    )
    got_a = lax.ppermute(send_a, "batch", [(0, 2)])
    got_f = lax.ppermute(send_f, "batch", [(3, 1), (1, 0)])
    got_c = lax.ppermute(send_c, "batch", [(2, 1), (3, 2)])
    pair_flops = 4 * rows * rows * group
    mixed, gate = call(
        own_kernel,
        [SMEM] + [VMEM] * 8,
        [((2, rows, group), F32), ((rows, width), BF16)],
        (place, got_b, query_near, send_a, send_b, send_c, seg, normed, joined_weight),
        3 * pair_flops + 2 * rows * features * width,
    )
    send_e, send_d = call(
        far_kernel,
        [SMEM] + [VMEM] * 6,
        [((rows, group), BF16)] * 2,
        (place, got_b, mixed, send_a, got_f, got_c, got_a),
        rows,
    )
    got_e = lax.ppermute(send_e, "batch", [(1, 3)])
    got_d = lax.ppermute(send_d, "batch", [(0, 1), (1, 2), (2, 3)])
    (near_mixed,) = call(
        near_kernel,
        [SMEM] + [VMEM] * 4,
        [((rows, group), F32)],
        (place, query_near, seg, got_a, mixed),
        rows,
    )
    (out,) = call(
        finish_kernel,
        [SMEM] + [VMEM] * 7,
        [((rows, features), BF16)],
        (place, mixed, near_mixed, got_e, got_d, gate, hidden, output_weight),
        2 * rows * width * features,
        [pltpu.VMEM((2, rows, group), F32)],
    )
    return out


def solution(mesh):
    chain = mesh.shape["batch"] == HEADS and mesh.shape["col"] & (mesh.shape["col"] - 1) == 0
    return jax.shard_map(
        chain_plan if chain else owners_plan,
        mesh=mesh,
        in_specs=(
            P(("rep", "batch"), "col"),
            P(),
            P(),
            P(),
            P(("rep", "batch", "col"), None),
            P(("rep", "batch", "col")),
        ),
        out_specs=P(("rep", "batch", "col"), None),
        check_vma=False,
    )
```

```python
import functools

import jax
import jax.numpy as jnp
from jax import lax
from jax.experimental import pallas as pl
from jax.experimental.pallas import tpu as pltpu
from jax.sharding import PartitionSpec as P

HEADS = 4
HEAD_DIM = 128
SEG_ROWS = 8

eps_norm = 1e-06

F32 = jnp.float32
BF16 = jnp.bfloat16


def layer_norm(values):
    row_mean = jnp.mean(values, axis=-1, keepdims=True)
    centered = values - row_mean
    row_var = jnp.mean(centered * centered, axis=-1, keepdims=True)
    return centered * lax.rsqrt(row_var + eps_norm)


def project(hidden_rows, joined_weight):
    normed = layer_norm(hidden_rows.astype(F32)).astype(BF16)
    return jax.nn.silu(jnp.dot(normed, joined_weight, preferred_element_type=F32)).astype(BF16)


def attend(joined_rows, seg_ids):
    width = HEADS * HEAD_DIM
    total = joined_rows.shape[0]
    gate_part = joined_rows[:, :width]
    value_part = joined_rows[:, width : 2 * width].reshape(total, HEADS, HEAD_DIM)
    query_part = joined_rows[:, 2 * width : 3 * width].reshape(total, HEADS, HEAD_DIM)
    key_part = joined_rows[:, 3 * width :].reshape(total, HEADS, HEAD_DIM)
    scores = jnp.einsum(
        "ihd,jhd->hij", query_part, key_part, preferred_element_type=F32
    ) * HEAD_DIM ** (-0.5)
    positions = jnp.arange(total, dtype=jnp.int32)
    allowed = (positions[None, :] <= positions[:, None]) & (seg_ids[None, :] == seg_ids[:, None])
    weights = jnp.where(allowed[None], jax.nn.silu(scores), 0.0).astype(BF16)
    mixed = jnp.einsum(
        "hij,jhd->ihd", weights, value_part, preferred_element_type=F32
    ).reshape(total, width)
    return (layer_norm(mixed) * gate_part.astype(F32)).astype(BF16)


def owners_plan(lookups, input_weight, joined_weight, output_weight, owner_counts, user_index):
    token_block = lax.all_to_all(lookups, "col", split_axis=0, concat_axis=1, tiled=True)
    hidden = jnp.dot(token_block, input_weight, preferred_element_type=F32).astype(BF16)
    local_rows = hidden.shape[0]
    owners = lax.axis_size("batch")
    capacity = local_rows // owners + local_rows // (2 * owners)
    counts = owner_counts[0]
    bin_ends = jnp.cumsum(counts)
    bin_starts = bin_ends - counts
    slot_ids = jnp.arange(capacity, dtype=jnp.int32)
    filled = slot_ids[None, :] < counts[:, None]
    gather_rows = jnp.where(filled, bin_starts[:, None] + slot_ids[None, :], 0).reshape(-1)
    seg_send = jnp.where(filled.reshape(-1), user_index[gather_rows], -1).reshape(owners, capacity)
    payload = hidden[gather_rows].reshape(owners, capacity, -1)
    received, seg_ids = (
        lax.all_to_all(payload, "batch", split_axis=0, concat_axis=0, tiled=True),
        lax.all_to_all(seg_send, "batch", split_axis=0, concat_axis=0, tiled=True),
    )
    joined_rows = project(received.reshape(owners * capacity, -1), joined_weight)
    gated_rows = attend(joined_rows, seg_ids.reshape(-1))
    token_pos = jnp.arange(local_rows, dtype=jnp.int32)
    owner_ids = jnp.arange(owners, dtype=jnp.int32)
    dest_owner = jnp.sum((token_pos[:, None] >= bin_ends[None, :]).astype(jnp.int32), axis=1)
    onehot = dest_owner[:, None] == owner_ids[None, :]
    first_slot = jnp.sum(jnp.where(onehot, bin_starts[None, :], 0), axis=1)
    back_rows = dest_owner * capacity + token_pos - first_slot
    returned = lax.all_to_all(
        gated_rows.reshape(owners, capacity, -1), "batch", split_axis=0, concat_axis=0, tiled=True
    )
    own_gated = returned.reshape(owners * capacity, -1)[back_rows]
    branch_rows = jnp.dot(own_gated, output_weight, preferred_element_type=F32).astype(BF16)
    return (hidden.astype(F32) + branch_rows.astype(F32)).astype(BF16)


def silu_of(values):
    half = 0.5 * values
    return half + half * jnp.tanh(half)


def head_weights(query, key, allowed):
    scores = lax.dot_general(query, key, (((1,), (1,)), ((), ())), preferred_element_type=F32)
    half = scores * (0.5 * HEAD_DIM ** (-0.5))
    return jnp.where(allowed, half + half * jnp.tanh(half), 0.0).astype(BF16)


def seg_column(seg_row):
    wide = jnp.broadcast_to(seg_row, (128, seg_row.shape[1]))
    return wide.T[:, :1]


def segments_kernel(counts, users, seg_out):
    rows = users.shape[1]
    owners = counts.shape[1]
    position = lax.broadcasted_iota(jnp.int32, (1, rows), 1)
    end = counts[0, 0]
    owner = (position >= end).astype(jnp.int32)
    for d in range(1, owners - 1):
        end = end + counts[0, d]
        owner = owner + (position >= end).astype(jnp.int32)
    seg_out[...] = jnp.broadcast_to((owner + owners * users[...]).astype(F32), seg_out.shape)


def put_seg(ref, seg):
    rows = seg.shape[1]
    for at in range(0, ref.shape[1], rows):
        ref[rows:, at : at + rows] = seg.astype(BF16)


def silu_dot(normed, weight):
    return silu_of(jnp.dot(normed[...], weight[...], preferred_element_type=F32)).astype(BF16)


def project_first_kernel(
    place, part3, part2, part1, own, w_in, w_key, w_value, seg, hidden_out, normed, send_b
):
    col_at = place[1]
    rows, piece = own.shape
    group = w_key.shape[1]
    total = None
    for shift, part in enumerate((own, part1, part2, part3)):
        start = pl.multiple_of((col_at ^ shift) * piece, piece)
        term = jnp.dot(part[...], w_in[pl.ds(start, piece), :], preferred_element_type=F32)
        total = term if total is None else total + term
    hidden = total.astype(BF16)
    hidden_out[...] = hidden
    normed[...] = layer_norm(hidden.astype(F32)).astype(BF16)
    send_b[:rows, :group] = silu_dot(normed, w_key)
    send_b[:rows, group:] = silu_dot(normed, w_value)
    put_seg(send_b, seg[...])


def project_query_kernel(normed, w_far, w_near, seg, send_c, send_f):
    rows = normed.shape[0]
    send_c[:rows, :] = silu_dot(normed, w_far)
    put_seg(send_c, seg[...])
    send_f[:rows, :] = silu_dot(normed, w_near)
    put_seg(send_f, seg[...])


def project_near_kernel(normed, w_key, w_value, seg, send_c, send_a):
    rows = normed.shape[0]
    group = w_key.shape[1]
    send_a[:rows, :group] = silu_dot(normed, w_key)
    send_a[:rows, group:] = silu_dot(normed, w_value)
    put_seg(send_a, seg[...])


def seg_row_of(ref, rows):
    return ref[rows : rows + SEG_ROWS, :rows].astype(F32)[0:1, :]


def add_blocks(query, key_values, out):
    group = query.shape[1]
    rows = query.shape[0] - SEG_ROWS
    column = seg_column(seg_row_of(query, rows))
    masks = [column == seg_row_of(ref, rows) for ref in key_values]
    for lo in range(0, group, HEAD_DIM):
        hi = lo + HEAD_DIM
        total = None
        for ref, allowed in zip(key_values, masks):
            weights = head_weights(query[:rows, lo:hi], ref[:rows, lo:hi], allowed)
            term = jnp.dot(
                weights, ref[:rows, group + lo : group + hi], preferred_element_type=F32
            )
            total = term if total is None else total + term
        out[:, lo:hi] = total.astype(out.dtype)


def add_near(send_f, column, key_value, mixed):
    rows, group = mixed.shape
    allowed = column == seg_row_of(key_value, rows)
    for lo in range(0, group, HEAD_DIM):
        hi = lo + HEAD_DIM
        weights = head_weights(send_f[:rows, lo:hi], key_value[:rows, lo:hi], allowed)
        mixed[:, lo:hi] += jnp.dot(
            weights, key_value[:rows, group + lo : group + hi], preferred_element_type=F32
        )


def own_kernel(send_f, send_a, send_b, send_c, seg, normed, w_gate, mixed_out, gate_out):
    rows, group = mixed_out.shape[1:]
    seg_row = seg[0:1, :]
    allowed = (seg_column(seg_row) == seg_row) & (
        lax.broadcasted_iota(jnp.int32, (rows, rows), 1)
        <= lax.broadcasted_iota(jnp.int32, (rows, rows), 0)
    )
    for side, (query, key_value) in enumerate(((send_f, send_a), (send_c, send_b))):
        for lo in range(0, group, HEAD_DIM):
            hi = lo + HEAD_DIM
            weights = head_weights(query[:rows, lo:hi], key_value[:rows, lo:hi], allowed)
            mixed_out[side, :, lo:hi] = jnp.dot(
                weights, key_value[:rows, group + lo : group + hi], preferred_element_type=F32
            )
    gate_out[...] = silu_dot(normed, w_gate)


def far_g_kernel(place, got_b, mixed, send_a, got_c, send_g, part_d):
    @pl.when(place[0] == 0)
    def _():
        add_blocks(got_c, [send_a], send_g)

    @pl.when(place[0] == 1)
    def _():
        add_blocks(got_c, [send_a, got_b], send_g)

    @pl.when(place[0] == 2)
    def _():
        add_blocks(got_c, [send_a, got_b], part_d)

    @pl.when(place[0] > 1)
    def _():
        send_g[...] = jnp.zeros_like(send_g)

    @pl.when(place[0] != 2)
    def _():
        part_d[...] = jnp.zeros_like(part_d)


def far_e_kernel(place, got_b, send_a, send_g, got_f, send_e):
    @pl.when(place[0] == 1)
    def _():
        add_blocks(got_f, [send_a, got_b], send_e)

    @pl.when(place[0] != 1)
    def _():
        send_e[...] = jnp.zeros_like(send_e)


def far_last_kernel(place, part_d, got_c, send_e, got_a, send_d, total):
    total[...] = part_d[...]

    @pl.when(place[0] == 2)
    def _():
        rows = total.shape[0]
        add_near(got_c, seg_column(seg_row_of(got_c, rows)), got_a, total)

    send_d[...] = total[...].astype(BF16)


def near_kernel(place, send_f, seg, got_a, got_b, got_e, got_g, mixed, near_out, far_out):
    near_out[...] = mixed[0] + got_e[...].astype(F32)
    far_out[...] = mixed[1] + got_g[...].astype(F32)
    column = seg_column(seg[0:1, :])

    @pl.when(place[0] > 0)
    def _():
        add_near(send_f, column, got_b, near_out)

    @pl.when(place[0] == 2)
    def _():
        add_near(send_f, column, got_a, near_out)


def finish_kernel(place, far_mixed, near_mixed, got_d, gate, hidden, w_out, out, whole):
    near = place[0] % 2
    whole[near] = near_mixed[...]
    whole[1 - near] = far_mixed[...] + got_d[...].astype(F32)
    both = jnp.concatenate([whole[0], whole[1]], axis=1)
    gated = (layer_norm(both) * gate[...].astype(F32)).astype(BF16)
    branch = jnp.dot(gated, w_out[...], preferred_element_type=F32).astype(BF16)
    out[...] = (hidden[...].astype(F32) + branch.astype(F32)).astype(BF16)


VMEM = pl.BlockSpec(memory_space=pltpu.VMEM)
SMEM = pl.BlockSpec(memory_space=pltpu.SMEM)


def call(kernel, in_specs, outs, operands, flops, scratch=(), limit=32 << 20):
    return pl.pallas_call(
        kernel,
        out_shape=[jax.ShapeDtypeStruct(shape, dtype) for shape, dtype in outs],
        in_specs=in_specs,
        out_specs=[VMEM] * len(outs),
        scratch_shapes=list(scratch),
        compiler_params=pltpu.CompilerParams(vmem_limit_bytes=limit),
        cost_estimate=pl.CostEstimate(flops=flops, bytes_accessed=0, transcendentals=0),
    )(*operands)


def chain_plan(lookups, input_weight, joined_weight, output_weight, owner_counts, user_index):
    cols = lax.axis_size("col")
    batch_at = lax.axis_index("batch").astype(jnp.int32)
    col_at = lax.axis_index("col").astype(jnp.int32)
    place = jnp.stack([batch_at, col_at])
    pieces = lookups.reshape(cols, lookups.shape[0] // cols, lookups.shape[1])
    rows = pieces.shape[1]

    def piece(shift):
        return lax.dynamic_index_in_dim(pieces, col_at ^ shift, 0, keepdims=False)

    parts = [piece(0)] + [
        lax.ppermute(piece(shift), "col", [(i, i ^ shift) for i in range(cols)])
        for shift in range(1, cols)
    ]
    width = HEADS * HEAD_DIM
    group = width // 2
    features = input_weight.shape[1]
    tall = rows + SEG_ROWS
    (seg,) = call(
        segments_kernel,
        [SMEM, VMEM],
        [((SEG_ROWS, rows), F32)],
        (owner_counts, user_index.reshape(1, rows)),
        2 * rows * features * (features + 4 * width),
    )
    near = batch_at % 2
    far = 1 - near

    def weight_of(block, index):
        return lax.dynamic_slice_in_dim(joined_weight, block * width + index * group, group, 1)

    hidden, normed, send_b = call(
        project_first_kernel,
        [SMEM] + [VMEM] * 8,
        [((rows, features), BF16), ((rows, features), BF16), ((tall, 2 * group), BF16)],
        (place, *parts[::-1], input_weight, weight_of(3, far), weight_of(1, far), seg),
        2 * rows * features * (features + 2 * group),
    )
    got_b = lax.ppermute(send_b, "batch", [(0, 1), (1, 2), (2, 3), (3, 0)])
    send_c, send_f = call(
        project_query_kernel,
        [VMEM] * 4,
        [((tall, group), BF16)] * 2,
        (normed, weight_of(2, far), weight_of(2, near), seg),
        2 * rows * features * 2 * group,
    )
    got_f = lax.ppermute(send_f, "batch", [(3, 1)])
    got_c = lax.ppermute(send_c, "batch", [(1, 0), (2, 1), (3, 2)])
    (send_a,) = call(
        project_near_kernel,
        [VMEM] * 5,
        [((tall, 2 * group), BF16)],
        (normed, weight_of(3, near), weight_of(1, near), seg, send_c),
        2 * rows * features * 2 * group,
    )
    got_a = lax.ppermute(send_a, "batch", [(0, 2)])
    pair_flops = 4 * rows * rows * group
    mixed, gate = call(
        own_kernel,
        [VMEM] * 7,
        [((2, rows, group), F32), ((rows, width), BF16)],
        (send_f, send_a, send_b, send_c, seg, normed, joined_weight[:, :width]),
        2 * pair_flops + 2 * rows * features * width,
    )
    send_g, part_d = call(
        far_g_kernel,
        [SMEM] + [VMEM] * 4,
        [((rows, group), BF16), ((rows, group), F32)],
        (place, got_b, mixed, send_a, got_c),
        4 * rows * features * features,
    )
    got_g = lax.ppermute(send_g, "batch", [(0, 1), (1, 2)])
    (send_e,) = call(
        far_e_kernel,
        [SMEM] + [VMEM] * 4,
        [((rows, group), BF16)],
        (place, got_b, send_a, send_g, got_f),
        4 * rows * features * features,
    )
    got_e = lax.ppermute(send_e, "batch", [(1, 3)])
    (send_d,) = call(
        far_last_kernel,
        [SMEM] + [VMEM] * 4,
        [((rows, group), BF16)],
        (place, part_d, got_c, send_e, got_a),
        rows,
        [pltpu.VMEM((rows, group), F32)],
    )
    got_d = lax.ppermute(send_d, "batch", [(2, 3)])
    near_mixed, far_mixed = call(
        near_kernel,
        [SMEM] + [VMEM] * 7,
        [((rows, group), F32)] * 2,
        (place, send_f, seg, got_a, got_b, got_e, got_g, mixed),
        rows,
    )
    (out,) = call(
        finish_kernel,
        [SMEM] + [VMEM] * 6,
        [((rows, features), BF16)],
        (place, far_mixed, near_mixed, got_d, gate, hidden, output_weight),
        2 * rows * width * features,
        [pltpu.VMEM((2, rows, group), F32)],
    )
    return out


def solution(mesh):
    chain = mesh.shape["batch"] == HEADS and mesh.shape["col"] & (mesh.shape["col"] - 1) == 0
    return jax.shard_map(
        chain_plan if chain else owners_plan,
        mesh=mesh,
        in_specs=(
            P(("rep", "batch"), "col"),
            P(),
            P(),
            P(),
            P(("rep", "batch", "col"), None),
            P(("rep", "batch", "col")),
        ),
        out_specs=P(("rep", "batch", "col"), None),
        check_vma=False,
    )
```

```python
import functools

import jax
import jax.numpy as jnp
from jax import lax
from jax.experimental import pallas as pl
from jax.experimental.pallas import tpu as pltpu
from jax.sharding import PartitionSpec as P

HEADS = 4
HEAD_DIM = 128
SEG_ROWS = 8

eps_norm = 1e-06

F32 = jnp.float32
BF16 = jnp.bfloat16


def layer_norm(values):
    row_mean = jnp.mean(values, axis=-1, keepdims=True)
    centered = values - row_mean
    row_var = jnp.mean(centered * centered, axis=-1, keepdims=True)
    return centered * lax.rsqrt(row_var + eps_norm)


def project(hidden_rows, joined_weight):
    normed = layer_norm(hidden_rows.astype(F32)).astype(BF16)
    return jax.nn.silu(jnp.dot(normed, joined_weight, preferred_element_type=F32)).astype(BF16)


def attend(joined_rows, seg_ids):
    width = HEADS * HEAD_DIM
    total = joined_rows.shape[0]
    gate_part = joined_rows[:, :width]
    value_part = joined_rows[:, width : 2 * width].reshape(total, HEADS, HEAD_DIM)
    query_part = joined_rows[:, 2 * width : 3 * width].reshape(total, HEADS, HEAD_DIM)
    key_part = joined_rows[:, 3 * width :].reshape(total, HEADS, HEAD_DIM)
    scores = jnp.einsum(
        "ihd,jhd->hij", query_part, key_part, preferred_element_type=F32
    ) * HEAD_DIM ** (-0.5)
    positions = jnp.arange(total, dtype=jnp.int32)
    allowed = (positions[None, :] <= positions[:, None]) & (seg_ids[None, :] == seg_ids[:, None])
    weights = jnp.where(allowed[None], jax.nn.silu(scores), 0.0).astype(BF16)
    mixed = jnp.einsum(
        "hij,jhd->ihd", weights, value_part, preferred_element_type=F32
    ).reshape(total, width)
    return (layer_norm(mixed) * gate_part.astype(F32)).astype(BF16)


def owners_plan(lookups, input_weight, joined_weight, output_weight, owner_counts, user_index):
    token_block = lax.all_to_all(lookups, "col", split_axis=0, concat_axis=1, tiled=True)
    hidden = jnp.dot(token_block, input_weight, preferred_element_type=F32).astype(BF16)
    local_rows = hidden.shape[0]
    owners = lax.axis_size("batch")
    capacity = local_rows // owners + local_rows // (2 * owners)
    counts = owner_counts[0]
    bin_ends = jnp.cumsum(counts)
    bin_starts = bin_ends - counts
    slot_ids = jnp.arange(capacity, dtype=jnp.int32)
    filled = slot_ids[None, :] < counts[:, None]
    gather_rows = jnp.where(filled, bin_starts[:, None] + slot_ids[None, :], 0).reshape(-1)
    seg_send = jnp.where(filled.reshape(-1), user_index[gather_rows], -1).reshape(owners, capacity)
    payload = hidden[gather_rows].reshape(owners, capacity, -1)
    received, seg_ids = (
        lax.all_to_all(payload, "batch", split_axis=0, concat_axis=0, tiled=True),
        lax.all_to_all(seg_send, "batch", split_axis=0, concat_axis=0, tiled=True),
    )
    joined_rows = project(received.reshape(owners * capacity, -1), joined_weight)
    gated_rows = attend(joined_rows, seg_ids.reshape(-1))
    token_pos = jnp.arange(local_rows, dtype=jnp.int32)
    owner_ids = jnp.arange(owners, dtype=jnp.int32)
    dest_owner = jnp.sum((token_pos[:, None] >= bin_ends[None, :]).astype(jnp.int32), axis=1)
    onehot = dest_owner[:, None] == owner_ids[None, :]
    first_slot = jnp.sum(jnp.where(onehot, bin_starts[None, :], 0), axis=1)
    back_rows = dest_owner * capacity + token_pos - first_slot
    returned = lax.all_to_all(
        gated_rows.reshape(owners, capacity, -1), "batch", split_axis=0, concat_axis=0, tiled=True
    )
    own_gated = returned.reshape(owners * capacity, -1)[back_rows]
    branch_rows = jnp.dot(own_gated, output_weight, preferred_element_type=F32).astype(BF16)
    return (hidden.astype(F32) + branch_rows.astype(F32)).astype(BF16)


def silu_of(values):
    half = 0.5 * values
    return half + half * jnp.tanh(half)


def head_weights(query, key, allowed):
    scores = lax.dot_general(query, key, (((1,), (1,)), ((), ())), preferred_element_type=F32)
    half = scores * (0.5 * HEAD_DIM ** (-0.5))
    return jnp.where(allowed, half + half * jnp.tanh(half), 0.0).astype(BF16)


def seg_column(seg_row):
    wide = jnp.broadcast_to(seg_row, (128, seg_row.shape[1]))
    return wide.T[:, :1]


def segments_kernel(counts, users, seg_out):
    rows = users.shape[1]
    owners = counts.shape[1]
    position = lax.broadcasted_iota(jnp.int32, (1, rows), 1)
    end = counts[0, 0]
    owner = (position >= end).astype(jnp.int32)
    for d in range(1, owners - 1):
        end = end + counts[0, d]
        owner = owner + (position >= end).astype(jnp.int32)
    seg_out[...] = jnp.broadcast_to((owner + owners * users[...]).astype(F32), seg_out.shape)


def put_seg(ref, seg):
    rows = seg.shape[1]
    for at in range(0, ref.shape[1], rows):
        ref[rows:, at : at + rows] = seg.astype(BF16)


def silu_dot(normed, weight):
    return silu_of(jnp.dot(normed[...], weight[...], preferred_element_type=F32)).astype(BF16)


def project_first_kernel(
    place, part3, part2, part1, own, w_in, w_key, w_value, seg, hidden_out, normed, send_b
):
    col_at = place[1]
    rows, piece = own.shape
    group = w_key.shape[1]
    total = None
    for shift, part in enumerate((own, part1, part2, part3)):
        start = pl.multiple_of((col_at ^ shift) * piece, piece)
        term = jnp.dot(part[...], w_in[pl.ds(start, piece), :], preferred_element_type=F32)
        total = term if total is None else total + term
    hidden = total.astype(BF16)
    hidden_out[...] = hidden
    normed[...] = layer_norm(hidden.astype(F32)).astype(BF16)
    send_b[:rows, :group] = silu_dot(normed, w_key)
    send_b[:rows, group:] = silu_dot(normed, w_value)
    put_seg(send_b, seg[...])


def project_query_kernel(normed, w_far, w_sent, seg, send_a, send_c, send_f):
    rows = normed.shape[0]
    for weight, ref in ((w_far, send_c), (w_sent, send_f)):
        ref[:rows, :] = silu_dot(normed, weight)
        put_seg(ref, seg[...])


def project_near_kernel(normed, w_key, w_value, seg, send_a):
    rows = normed.shape[0]
    group = w_key.shape[1]
    send_a[:rows, :group] = silu_dot(normed, w_key)
    send_a[:rows, group:] = silu_dot(normed, w_value)
    put_seg(send_a, seg[...])


def seg_row_of(ref, rows):
    return ref[rows : rows + SEG_ROWS, :rows].astype(F32)[0:1, :]


def add_blocks(query, key_values, out):
    group = query.shape[1]
    rows = query.shape[0] - SEG_ROWS
    column = seg_column(seg_row_of(query, rows))
    masks = [column == seg_row_of(ref, rows) for ref in key_values]
    for lo in range(0, group, HEAD_DIM):
        hi = lo + HEAD_DIM
        total = None
        for ref, allowed in zip(key_values, masks):
            weights = head_weights(query[:rows, lo:hi], ref[:rows, lo:hi], allowed)
            term = jnp.dot(
                weights, ref[:rows, group + lo : group + hi], preferred_element_type=F32
            )
            total = term if total is None else total + term
        out[:, lo:hi] = total.astype(out.dtype)


def add_near(query, column, key_value, mixed):
    rows, group = mixed.shape
    allowed = column == seg_row_of(key_value, rows)
    for lo in range(0, group, HEAD_DIM):
        hi = lo + HEAD_DIM
        weights = head_weights(query[:rows, lo:hi], key_value[:rows, lo:hi], allowed)
        mixed[:, lo:hi] += jnp.dot(
            weights, key_value[:rows, group + lo : group + hi], preferred_element_type=F32
        )


def own_kernel(
    send_a, send_b, send_c, seg, normed, w_query, w_near, w_far, mixed_out, query_near, gate_out
):
    rows, group = mixed_out.shape[1:]
    seg_row = seg[0:1, :]
    allowed = (seg_column(seg_row) == seg_row) & (
        lax.broadcasted_iota(jnp.int32, (rows, rows), 1)
        <= lax.broadcasted_iota(jnp.int32, (rows, rows), 0)
    )
    query_near[...] = silu_dot(normed, w_query)
    for side, (query, key_value) in enumerate(((query_near, send_a), (send_c, send_b))):
        for lo in range(0, group, HEAD_DIM):
            hi = lo + HEAD_DIM
            weights = head_weights(query[:rows, lo:hi], key_value[:rows, lo:hi], allowed)
            mixed_out[side, :, lo:hi] = jnp.dot(
                weights, key_value[:rows, group + lo : group + hi], preferred_element_type=F32
            )
    gate_out[0] = silu_dot(normed, w_near)
    gate_out[1] = silu_dot(normed, w_far)


def far_g_kernel(place, got_b, send_e, send_a, got_c, send_g):
    @pl.when(place[0] == 1)
    def _():
        add_blocks(got_c, [send_a, got_b], send_g)

    @pl.when(place[0] != 1)
    def _():
        send_g[...] = jnp.zeros_like(send_g)


def far_e_kernel(place, got_b, send_a, mixed, got_f, send_e):
    @pl.when(place[0] == 0)
    def _():
        add_blocks(got_f, [send_a], send_e)

    @pl.when(place[0] == 1)
    def _():
        add_blocks(got_f, [send_a, got_b], send_e)

    @pl.when(place[0] > 1)
    def _():
        send_e[...] = jnp.zeros_like(send_e)


def far_d_kernel(place, got_b, send_a, got_h, got_a, send_d):
    @pl.when(place[0] == 2)
    def _():
        add_blocks(got_h, [send_a, got_b, got_a], send_d)

    @pl.when(place[0] != 2)
    def _():
        send_d[...] = jnp.zeros_like(send_d)


def near_kernel(place, query_near, seg, got_a, got_b, mixed, near_out):
    near_out[...] = mixed[0]
    column = seg_column(seg[0:1, :])

    @pl.when(place[0] > 0)
    def _():
        add_near(query_near, column, got_b, near_out)

    @pl.when(place[0] == 2)
    def _():
        add_near(query_near, column, got_a, near_out)


def finish_kernel(place, near_mixed, mixed, got_d, got_eg, gate, hidden, w_out, out):
    near = place[0] % 2
    last = place[0] == place[2]
    got = got_eg[...].astype(F32)
    group = near_mixed.shape[1]
    sides = (
        near_mixed[...] + jnp.where(last, got, 0.0),
        mixed[1] + got_d[...].astype(F32) + jnp.where(last, 0.0, got),
    )
    total = sum(jnp.sum(side, axis=-1, keepdims=True) for side in sides)
    sides = [side - total / (2 * group) for side in sides]
    total = sum(jnp.sum(side * side, axis=-1, keepdims=True) for side in sides)
    scale = lax.rsqrt(total / (2 * group) + eps_norm)
    branch = None
    for index, (which, side) in enumerate(zip((near, 1 - near), sides)):
        gated = (side * scale * gate[index].astype(F32)).astype(BF16)
        start = pl.multiple_of(which * group, group)
        term = jnp.dot(gated, w_out[pl.ds(start, group), :], preferred_element_type=F32)
        branch = term if branch is None else branch + term
    out[...] = (hidden[...].astype(F32) + branch.astype(BF16).astype(F32)).astype(BF16)


VMEM = pl.BlockSpec(memory_space=pltpu.VMEM)
SMEM = pl.BlockSpec(memory_space=pltpu.SMEM)


def call(kernel, in_specs, outs, operands, flops, scratch=(), limit=32 << 20):
    return pl.pallas_call(
        kernel,
        out_shape=[jax.ShapeDtypeStruct(shape, dtype) for shape, dtype in outs],
        in_specs=in_specs,
        out_specs=[VMEM] * len(outs),
        scratch_shapes=list(scratch),
        compiler_params=pltpu.CompilerParams(vmem_limit_bytes=limit),
        cost_estimate=pl.CostEstimate(flops=flops, bytes_accessed=0, transcendentals=0),
    )(*operands)


def chain_plan(lookups, input_weight, joined_weight, output_weight, owner_counts, user_index):
    cols = lax.axis_size("col")
    batch_at = lax.axis_index("batch").astype(jnp.int32)
    col_at = lax.axis_index("col").astype(jnp.int32)
    place = jnp.stack([batch_at, col_at, jnp.int32(lax.axis_size("batch") - 1)])
    pieces = lookups.reshape(cols, lookups.shape[0] // cols, lookups.shape[1])
    rows = pieces.shape[1]

    def piece(shift):
        return lax.dynamic_index_in_dim(pieces, col_at ^ shift, 0, keepdims=False)

    parts = [piece(0)] + [
        lax.ppermute(piece(shift), "col", [(i, i ^ shift) for i in range(cols)])
        for shift in range(1, cols)
    ]
    width = HEADS * HEAD_DIM
    group = width // 2
    features = input_weight.shape[1]
    tall = rows + SEG_ROWS
    (seg,) = call(
        segments_kernel,
        [SMEM, VMEM],
        [((SEG_ROWS, rows), F32)],
        (owner_counts, user_index.reshape(1, rows)),
        2 * rows * features * (features + 4 * width),
    )
    near = batch_at % 2
    far = 1 - near

    def weight_of(block, index):
        return lax.dynamic_slice_in_dim(joined_weight, block * width + index * group, group, 1)

    hidden, normed, send_b = call(
        project_first_kernel,
        [SMEM] + [VMEM] * 8,
        [((rows, features), BF16), ((rows, features), BF16), ((tall, 2 * group), BF16)],
        (place, *parts[::-1], input_weight, weight_of(3, far), weight_of(1, far), seg),
        2 * rows * features * (features + 2 * group),
    )
    got_b = lax.ppermute(send_b, "batch", [(0, 1), (1, 2), (2, 3), (3, 0)])
    (send_a,) = call(
        project_near_kernel,
        [VMEM] * 4,
        [((tall, 2 * group), BF16)],
        (normed, weight_of(3, near), weight_of(1, near), seg),
        2 * rows * features * 2 * group,
    )
    got_a = lax.ppermute(send_a, "batch", [(0, 2)])
    send_c, send_f = call(
        project_query_kernel,
        [VMEM] * 5,
        [((tall, group), BF16)] * 2,
        (normed, weight_of(2, far), weight_of(2, jnp.where(batch_at == 1, far, near)), seg, send_a),
        2 * rows * features * 2 * group,
    )
    got_f = lax.ppermute(send_f, "batch", [(3, 1), (1, 0)])
    got_c = lax.ppermute(send_c, "batch", [(2, 1)])
    got_h = lax.ppermute(send_c, "batch", [(3, 2)])
    pair_flops = 4 * rows * rows * group
    mixed, query_near, gate = call(
        own_kernel,
        [VMEM] * 8,
        [((2, rows, group), F32), ((rows, group), BF16), ((2, rows, group), BF16)],
        (
            send_a, send_b, send_c, seg, normed, weight_of(2, near), weight_of(0, near),
            weight_of(0, far),
        ),
        2 * pair_flops + 2 * rows * features * width,
    )
    (send_e,) = call(
        far_e_kernel,
        [SMEM] + [VMEM] * 4,
        [((rows, group), BF16)],
        (place, got_b, send_a, mixed, got_f),
        1 << 30,
    )
    got_e = lax.ppermute(send_e, "batch", [(1, 3), (0, 1)])
    (send_g,) = call(
        far_g_kernel,
        [SMEM] + [VMEM] * 4,
        [((rows, group), BF16)],
        (place, got_b, send_e, send_a, got_c),
        1 << 30,
    )
    got_g = lax.ppermute(send_g, "batch", [(1, 2)])
    (send_d,) = call(
        far_d_kernel,
        [SMEM] + [VMEM] * 4,
        [((rows, group), BF16)],
        (place, got_b, send_a, got_h, got_a),
        rows,
    )
    got_d = lax.ppermute(send_d, "batch", [(2, 3)])
    (near_mixed,) = call(
        near_kernel,
        [SMEM] + [VMEM] * 5,
        [((rows, group), F32)],
        (place, query_near, seg, got_a, got_b, mixed),
        rows,
    )
    (out,) = call(
        finish_kernel,
        [SMEM] + [VMEM] * 7,
        [((rows, features), BF16)],
        (place, near_mixed, mixed, got_d, got_e + got_g, gate, hidden, output_weight),
        rows,
    )
    return out


def solution(mesh):
    chain = mesh.shape["batch"] == HEADS and mesh.shape["col"] & (mesh.shape["col"] - 1) == 0
    return jax.shard_map(
        chain_plan if chain else owners_plan,
        mesh=mesh,
        in_specs=(
            P(("rep", "batch"), "col"),
            P(),
            P(),
            P(),
            P(("rep", "batch", "col"), None),
            P(("rep", "batch", "col")),
        ),
        out_specs=P(("rep", "batch", "col"), None),
        check_vma=False,
    )
```

```python
import functools

import jax
import jax.numpy as jnp
from jax import lax
from jax.experimental import pallas as pl
from jax.experimental.pallas import tpu as pltpu
from jax.sharding import PartitionSpec as P

HEADS = 4
HEAD_DIM = 128
SEG_ROWS = 8

eps_norm = 1e-06

F32 = jnp.float32
BF16 = jnp.bfloat16


def layer_norm(values):
    row_mean = jnp.mean(values, axis=-1, keepdims=True)
    centered = values - row_mean
    row_var = jnp.mean(centered * centered, axis=-1, keepdims=True)
    return centered * lax.rsqrt(row_var + eps_norm)


def project(hidden_rows, joined_weight):
    normed = layer_norm(hidden_rows.astype(F32)).astype(BF16)
    return jax.nn.silu(jnp.dot(normed, joined_weight, preferred_element_type=F32)).astype(BF16)


def attend(joined_rows, seg_ids):
    width = HEADS * HEAD_DIM
    total = joined_rows.shape[0]
    gate_part = joined_rows[:, :width]
    value_part = joined_rows[:, width : 2 * width].reshape(total, HEADS, HEAD_DIM)
    query_part = joined_rows[:, 2 * width : 3 * width].reshape(total, HEADS, HEAD_DIM)
    key_part = joined_rows[:, 3 * width :].reshape(total, HEADS, HEAD_DIM)
    scores = jnp.einsum(
        "ihd,jhd->hij", query_part, key_part, preferred_element_type=F32
    ) * HEAD_DIM ** (-0.5)
    positions = jnp.arange(total, dtype=jnp.int32)
    allowed = (positions[None, :] <= positions[:, None]) & (seg_ids[None, :] == seg_ids[:, None])
    weights = jnp.where(allowed[None], jax.nn.silu(scores), 0.0).astype(BF16)
    mixed = jnp.einsum(
        "hij,jhd->ihd", weights, value_part, preferred_element_type=F32
    ).reshape(total, width)
    return (layer_norm(mixed) * gate_part.astype(F32)).astype(BF16)


def owners_plan(lookups, input_weight, joined_weight, output_weight, owner_counts, user_index):
    token_block = lax.all_to_all(lookups, "col", split_axis=0, concat_axis=1, tiled=True)
    hidden = jnp.dot(token_block, input_weight, preferred_element_type=F32).astype(BF16)
    local_rows = hidden.shape[0]
    owners = lax.axis_size("batch")
    capacity = local_rows // owners + local_rows // (2 * owners)
    counts = owner_counts[0]
    bin_ends = jnp.cumsum(counts)
    bin_starts = bin_ends - counts
    slot_ids = jnp.arange(capacity, dtype=jnp.int32)
    filled = slot_ids[None, :] < counts[:, None]
    gather_rows = jnp.where(filled, bin_starts[:, None] + slot_ids[None, :], 0).reshape(-1)
    seg_send = jnp.where(filled.reshape(-1), user_index[gather_rows], -1).reshape(owners, capacity)
    payload = hidden[gather_rows].reshape(owners, capacity, -1)
    received, seg_ids = (
        lax.all_to_all(payload, "batch", split_axis=0, concat_axis=0, tiled=True),
        lax.all_to_all(seg_send, "batch", split_axis=0, concat_axis=0, tiled=True),
    )
    joined_rows = project(received.reshape(owners * capacity, -1), joined_weight)
    gated_rows = attend(joined_rows, seg_ids.reshape(-1))
    token_pos = jnp.arange(local_rows, dtype=jnp.int32)
    owner_ids = jnp.arange(owners, dtype=jnp.int32)
    dest_owner = jnp.sum((token_pos[:, None] >= bin_ends[None, :]).astype(jnp.int32), axis=1)
    onehot = dest_owner[:, None] == owner_ids[None, :]
    first_slot = jnp.sum(jnp.where(onehot, bin_starts[None, :], 0), axis=1)
    back_rows = dest_owner * capacity + token_pos - first_slot
    returned = lax.all_to_all(
        gated_rows.reshape(owners, capacity, -1), "batch", split_axis=0, concat_axis=0, tiled=True
    )
    own_gated = returned.reshape(owners * capacity, -1)[back_rows]
    branch_rows = jnp.dot(own_gated, output_weight, preferred_element_type=F32).astype(BF16)
    return (hidden.astype(F32) + branch_rows.astype(F32)).astype(BF16)


def silu_of(values):
    half = 0.5 * values
    return half + half * jnp.tanh(half)


def head_weights(query, key, allowed):
    scores = lax.dot_general(query, key, (((1,), (1,)), ((), ())), preferred_element_type=F32)
    half = scores * (0.5 * HEAD_DIM ** (-0.5))
    return jnp.where(allowed, half + half * jnp.tanh(half), 0.0).astype(BF16)


def seg_column(seg_row):
    wide = jnp.broadcast_to(seg_row, (128, seg_row.shape[1]))
    return wide.T[:, :1]


def segments_kernel(counts, users, seg_out):
    rows = users.shape[1]
    owners = counts.shape[1]
    position = lax.broadcasted_iota(jnp.int32, (1, rows), 1)
    end = counts[0, 0]
    owner = (position >= end).astype(jnp.int32)
    for d in range(1, owners - 1):
        end = end + counts[0, d]
        owner = owner + (position >= end).astype(jnp.int32)
    seg_out[...] = jnp.broadcast_to((owner + owners * users[...]).astype(F32), seg_out.shape)


def put_seg(ref, seg):
    rows = seg.shape[1]
    for at in range(0, ref.shape[1], rows):
        ref[rows:, at : at + rows] = seg.astype(BF16)


def silu_dot(normed, weight):
    return silu_of(jnp.dot(normed[...], weight[...], preferred_element_type=F32)).astype(BF16)


def project_first_kernel(
    place, part3, part2, part1, own, w_in, w_key, w_value, seg, hidden_out, normed, send_b
):
    col_at = place[1]
    rows, piece = own.shape
    group = w_key.shape[1]
    total = None
    for shift, part in enumerate((own, part1, part2, part3)):
        start = pl.multiple_of((col_at ^ shift) * piece, piece)
        term = jnp.dot(part[...], w_in[pl.ds(start, piece), :], preferred_element_type=F32)
        total = term if total is None else total + term
    hidden = total.astype(BF16)
    hidden_out[...] = hidden
    normed[...] = layer_norm(hidden.astype(F32)).astype(BF16)
    send_b[:rows, :group] = silu_dot(normed, w_key)
    send_b[:rows, group:] = silu_dot(normed, w_value)
    put_seg(send_b, seg[...])


def project_query_kernel(normed, w_far, w_sent, seg, send_c, send_f):
    rows = normed.shape[0]
    for weight, ref in ((w_far, send_c), (w_sent, send_f)):
        ref[:rows, :] = silu_dot(normed, weight)
        put_seg(ref, seg[...])


def project_near_kernel(
    place, send_b, send_c, seg, normed, w_query, w_near, w_far, w_key, w_value,
    send_a, mixed_out, query_near, gate_out,
):
    rows = normed.shape[0]
    group = w_key.shape[1]
    send_a[:rows, :group] = silu_dot(normed, w_key)
    send_a[:rows, group:] = silu_dot(normed, w_value)
    put_seg(send_a, seg[...])

    @pl.when(place[0] == 0)
    def _():
        attend_own(
            send_a, send_b, send_c, seg, normed, (w_query, w_near, w_far),
            mixed_out, query_near, gate_out,
        )


def seg_row_of(ref, rows):
    return ref[rows : rows + SEG_ROWS, :rows].astype(F32)[0:1, :]


def add_blocks(query, key_values, out):
    group = query.shape[1]
    rows = query.shape[0] - SEG_ROWS
    column = seg_column(seg_row_of(query, rows))
    masks = [column == seg_row_of(ref, rows) for ref in key_values]
    for lo in range(0, group, HEAD_DIM):
        hi = lo + HEAD_DIM
        total = None
        for ref, allowed in zip(key_values, masks):
            weights = head_weights(query[:rows, lo:hi], ref[:rows, lo:hi], allowed)
            term = jnp.dot(
                weights, ref[:rows, group + lo : group + hi], preferred_element_type=F32
            )
            total = term if total is None else total + term
        out[:, lo:hi] = total.astype(out.dtype)


def add_near(query, column, key_value, mixed):
    rows, group = mixed.shape
    allowed = column == seg_row_of(key_value, rows)
    for lo in range(0, group, HEAD_DIM):
        hi = lo + HEAD_DIM
        weights = head_weights(query[:rows, lo:hi], key_value[:rows, lo:hi], allowed)
        mixed[:, lo:hi] += jnp.dot(
            weights, key_value[:rows, group + lo : group + hi], preferred_element_type=F32
        )


def attend_own(send_a, send_b, send_c, seg, normed, weights, mixed_out, query_near, gate_out):
    rows, group = mixed_out.shape[1:]
    w_query, w_near, w_far = weights
    seg_row = seg[0:1, :]
    allowed = (seg_column(seg_row) == seg_row) & (
        lax.broadcasted_iota(jnp.int32, (rows, rows), 1)
        <= lax.broadcasted_iota(jnp.int32, (rows, rows), 0)
    )
    query_near[...] = silu_dot(normed, w_query)
    for side, (query, key_value) in enumerate(((query_near, send_a), (send_c, send_b))):
        for lo in range(0, group, HEAD_DIM):
            hi = lo + HEAD_DIM
            weights = head_weights(query[:rows, lo:hi], key_value[:rows, lo:hi], allowed)
            mixed_out[side, :, lo:hi] = jnp.dot(
                weights, key_value[:rows, group + lo : group + hi], preferred_element_type=F32
            )
    gate_out[0] = silu_dot(normed, w_near)
    gate_out[1] = silu_dot(normed, w_far)


def own_kernel(
    place, send_a, send_b, send_c, seg, normed, w_query, w_near, w_far,
    mixed_in, query_in, gate_in, mixed, query_near, gate,
):
    @pl.when((place[0] != 0) & (place[0] != place[2]))
    def _():
        attend_own(
            send_a, send_b, send_c, seg, normed, (w_query, w_near, w_far), mixed, query_near, gate
        )


def far_g_kernel(place, got_b, send_e, send_a, got_c, send_g):
    @pl.when(place[0] == 1)
    def _():
        add_blocks(got_c, [send_a, got_b], send_g)

    @pl.when(place[0] != 1)
    def _():
        send_g[...] = jnp.zeros_like(send_g)


def far_e_kernel(place, got_b, send_a, mixed, got_f, send_e):
    @pl.when(place[0] == 0)
    def _():
        add_blocks(got_f, [send_a], send_e)

    @pl.when(place[0] == 1)
    def _():
        add_blocks(got_f, [send_a, got_b], send_e)

    @pl.when(place[0] > 1)
    def _():
        send_e[...] = jnp.zeros_like(send_e)


def far_d_kernel(place, got_b, send_a, got_h, got_a, send_d):
    @pl.when(place[0] == 2)
    def _():
        add_blocks(got_h, [send_a, got_b, got_a], send_d)

    @pl.when(place[0] != 2)
    def _():
        send_d[...] = jnp.zeros_like(send_d)


def near_kernel(
    place, got_a, got_b, send_a, send_b, send_c, seg, normed, w_query, w_near, w_far,
    mixed_in, query_in, gate_in, mixed, query_near, gate,
):
    column = seg_column(seg[0:1, :])

    @pl.when(place[0] == place[2])
    def _():
        attend_own(
            send_a, send_b, send_c, seg, normed, (w_query, w_near, w_far), mixed, query_near, gate
        )

    @pl.when(place[0] > 0)
    def _():
        add_near(query_near, column, got_b, mixed.at[0])

    @pl.when(place[0] == 2)
    def _():
        add_near(query_near, column, got_a, mixed.at[0])


def finish_kernel(place, mixed, got_d, got_eg, gate, hidden, w_out, out):
    near = place[0] % 2
    last = place[0] == place[2]
    got = got_eg[...].astype(F32)
    group = mixed.shape[2]
    sides = (
        mixed[0] + jnp.where(last, got, 0.0),
        mixed[1] + got_d[...].astype(F32) + jnp.where(last, 0.0, got),
    )
    total = sum(jnp.sum(side, axis=-1, keepdims=True) for side in sides)
    sides = [side - total / (2 * group) for side in sides]
    total = sum(jnp.sum(side * side, axis=-1, keepdims=True) for side in sides)
    scale = lax.rsqrt(total / (2 * group) + eps_norm)
    branch = None
    for index, (which, side) in enumerate(zip((near, 1 - near), sides)):
        gated = (side * scale * gate[index].astype(F32)).astype(BF16)
        start = pl.multiple_of(which * group, group)
        term = jnp.dot(gated, w_out[pl.ds(start, group), :], preferred_element_type=F32)
        branch = term if branch is None else branch + term
    out[...] = (hidden[...].astype(F32) + branch.astype(BF16).astype(F32)).astype(BF16)


VMEM = pl.BlockSpec(memory_space=pltpu.VMEM)
SMEM = pl.BlockSpec(memory_space=pltpu.SMEM)


def call(kernel, in_specs, outs, operands, flops, scratch=(), limit=32 << 20, aliases=()):
    return pl.pallas_call(
        kernel,
        out_shape=[jax.ShapeDtypeStruct(shape, dtype) for shape, dtype in outs],
        in_specs=in_specs,
        out_specs=[VMEM] * len(outs),
        scratch_shapes=list(scratch),
        input_output_aliases=dict(aliases),
        compiler_params=pltpu.CompilerParams(vmem_limit_bytes=limit),
        cost_estimate=pl.CostEstimate(flops=flops, bytes_accessed=0, transcendentals=0),
    )(*operands)


def chain_plan(lookups, input_weight, joined_weight, output_weight, owner_counts, user_index):
    cols = lax.axis_size("col")
    batch_at = lax.axis_index("batch").astype(jnp.int32)
    col_at = lax.axis_index("col").astype(jnp.int32)
    place = jnp.stack([batch_at, col_at, jnp.int32(lax.axis_size("batch") - 1)])
    pieces = lookups.reshape(cols, lookups.shape[0] // cols, lookups.shape[1])
    rows = pieces.shape[1]

    def piece(source, shift):
        return lax.dynamic_index_in_dim(source, col_at ^ shift, 0, keepdims=False)

    def exchange(block, shift):
        return lax.ppermute(block, "col", [(i, i ^ shift) for i in range(cols)])

    across = piece(pieces, 2)
    pieces, across = lax.optimization_barrier((pieces, across))
    parts = [piece(pieces, 0)] + [
        exchange(across if shift == 2 else piece(pieces, shift), shift)
        for shift in range(1, cols)
    ]
    width = HEADS * HEAD_DIM
    group = width // 2
    features = input_weight.shape[1]
    tall = rows + SEG_ROWS
    (seg,) = call(
        segments_kernel,
        [SMEM, VMEM],
        [((SEG_ROWS, rows), F32)],
        (owner_counts, user_index.reshape(1, rows)),
        2 * rows * features * (features + 4 * width),
    )
    near = batch_at % 2
    far = 1 - near

    def weight_of(block, index):
        return lax.dynamic_slice_in_dim(joined_weight, block * width + index * group, group, 1)

    hidden, normed, send_b = call(
        project_first_kernel,
        [SMEM] + [VMEM] * 8,
        [((rows, features), BF16), ((rows, features), BF16), ((tall, 2 * group), BF16)],
        (place, *parts[::-1], input_weight, weight_of(3, far), weight_of(1, far), seg),
        2 * rows * features * (features + 2 * group),
    )
    got_b = lax.ppermute(send_b, "batch", [(0, 1), (1, 2), (2, 3), (3, 0)])
    send_c, send_f = call(
        project_query_kernel,
        [VMEM] * 4,
        [((tall, group), BF16)] * 2,
        (normed, weight_of(2, far), weight_of(2, jnp.where(batch_at == 1, far, near)), seg),
        2 * rows * features * 2 * group,
    )
    got_f = lax.ppermute(send_f, "batch", [(3, 1), (1, 0)])
    own_inputs = (
        send_b, send_c, seg, normed, weight_of(2, near), weight_of(0, near), weight_of(0, far),
    )
    own_outs = [((2, rows, group), F32), ((rows, group), BF16), ((2, rows, group), BF16)]
    send_a, *own = call(
        project_near_kernel,
        [SMEM] + [VMEM] * 9,
        [((tall, 2 * group), BF16)] + own_outs,
        (place, *own_inputs, weight_of(3, near), weight_of(1, near)),
        2 * rows * features * 2 * group,
    )
    got_a = lax.ppermute(send_a, "batch", [(0, 2)])
    got_c = lax.ppermute(send_c, "batch", [(2, 1)])
    got_h = lax.ppermute(send_c, "batch", [(3, 2)])
    pair_flops = 4 * rows * rows * group
    own = call(
        own_kernel,
        [SMEM] + [VMEM] * 11,
        own_outs,
        (place, send_a, *own_inputs, *own),
        2 * pair_flops + 2 * rows * features * width,
        aliases={9: 0, 10: 1, 11: 2},
    )
    mixed = own[0]
    (send_e,) = call(
        far_e_kernel,
        [SMEM] + [VMEM] * 4,
        [((rows, group), BF16)],
        (place, got_b, send_a, mixed, got_f),
        1 << 30,
    )
    got_e = lax.ppermute(send_e, "batch", [(1, 3), (0, 1)])
    (send_g,) = call(
        far_g_kernel,
        [SMEM] + [VMEM] * 4,
        [((rows, group), BF16)],
        (place, got_b, send_e, send_a, got_c),
        1 << 30,
    )
    got_g = lax.ppermute(send_g, "batch", [(1, 2)])
    (send_d,) = call(
        far_d_kernel,
        [SMEM] + [VMEM] * 4,
        [((rows, group), BF16)],
        (place, got_b, send_a, got_h, got_a),
        rows,
    )
    got_d = lax.ppermute(send_d, "batch", [(2, 3)])
    mixed, _, gate = call(
        near_kernel,
        [SMEM] + [VMEM] * 13,
        own_outs,
        (place, got_a, got_b, send_a, *own_inputs, *own),
        rows,
        aliases={11: 0, 12: 1, 13: 2},
    )
    (out,) = call(
        finish_kernel,
        [SMEM] + [VMEM] * 6,
        [((rows, features), BF16)],
        (place, mixed, got_d, got_e + got_g, gate, hidden, output_weight),
        rows,
    )
    return out


def solution(mesh):
    chain = mesh.shape["batch"] == HEADS and mesh.shape["col"] & (mesh.shape["col"] - 1) == 0
    return jax.shard_map(
        chain_plan if chain else owners_plan,
        mesh=mesh,
        in_specs=(
            P(("rep", "batch"), "col"),
            P(),
            P(),
            P(),
            P(("rep", "batch", "col"), None),
            P(("rep", "batch", "col")),
        ),
        out_specs=P(("rep", "batch", "col"), None),
        check_vma=False,
    )
```

```python
import functools

import jax
import jax.numpy as jnp
from jax import lax
from jax.experimental import pallas as pl
from jax.experimental.pallas import tpu as pltpu
from jax.sharding import PartitionSpec as P

HEADS = 4
HEAD_DIM = 128
SEG_ROWS = 8

eps_norm = 1e-06

F32 = jnp.float32
BF16 = jnp.bfloat16


def layer_norm(values):
    row_mean = jnp.mean(values, axis=-1, keepdims=True)
    centered = values - row_mean
    row_var = jnp.mean(centered * centered, axis=-1, keepdims=True)
    return centered * lax.rsqrt(row_var + eps_norm)


def project(hidden_rows, joined_weight):
    normed = layer_norm(hidden_rows.astype(F32)).astype(BF16)
    return jax.nn.silu(jnp.dot(normed, joined_weight, preferred_element_type=F32)).astype(BF16)


def attend(joined_rows, seg_ids):
    width = HEADS * HEAD_DIM
    total = joined_rows.shape[0]
    gate_part = joined_rows[:, :width]
    value_part = joined_rows[:, width : 2 * width].reshape(total, HEADS, HEAD_DIM)
    query_part = joined_rows[:, 2 * width : 3 * width].reshape(total, HEADS, HEAD_DIM)
    key_part = joined_rows[:, 3 * width :].reshape(total, HEADS, HEAD_DIM)
    scores = jnp.einsum(
        "ihd,jhd->hij", query_part, key_part, preferred_element_type=F32
    ) * HEAD_DIM ** (-0.5)
    positions = jnp.arange(total, dtype=jnp.int32)
    allowed = (positions[None, :] <= positions[:, None]) & (seg_ids[None, :] == seg_ids[:, None])
    weights = jnp.where(allowed[None], jax.nn.silu(scores), 0.0).astype(BF16)
    mixed = jnp.einsum(
        "hij,jhd->ihd", weights, value_part, preferred_element_type=F32
    ).reshape(total, width)
    return (layer_norm(mixed) * gate_part.astype(F32)).astype(BF16)


def owners_plan(lookups, input_weight, joined_weight, output_weight, owner_counts, user_index):
    token_block = lax.all_to_all(lookups, "col", split_axis=0, concat_axis=1, tiled=True)
    hidden = jnp.dot(token_block, input_weight, preferred_element_type=F32).astype(BF16)
    local_rows = hidden.shape[0]
    owners = lax.axis_size("batch")
    capacity = local_rows // owners + local_rows // (2 * owners)
    counts = owner_counts[0]
    bin_ends = jnp.cumsum(counts)
    bin_starts = bin_ends - counts
    slot_ids = jnp.arange(capacity, dtype=jnp.int32)
    filled = slot_ids[None, :] < counts[:, None]
    gather_rows = jnp.where(filled, bin_starts[:, None] + slot_ids[None, :], 0).reshape(-1)
    seg_send = jnp.where(filled.reshape(-1), user_index[gather_rows], -1).reshape(owners, capacity)
    payload = hidden[gather_rows].reshape(owners, capacity, -1)
    received, seg_ids = (
        lax.all_to_all(payload, "batch", split_axis=0, concat_axis=0, tiled=True),
        lax.all_to_all(seg_send, "batch", split_axis=0, concat_axis=0, tiled=True),
    )
    joined_rows = project(received.reshape(owners * capacity, -1), joined_weight)
    gated_rows = attend(joined_rows, seg_ids.reshape(-1))
    token_pos = jnp.arange(local_rows, dtype=jnp.int32)
    owner_ids = jnp.arange(owners, dtype=jnp.int32)
    dest_owner = jnp.sum((token_pos[:, None] >= bin_ends[None, :]).astype(jnp.int32), axis=1)
    onehot = dest_owner[:, None] == owner_ids[None, :]
    first_slot = jnp.sum(jnp.where(onehot, bin_starts[None, :], 0), axis=1)
    back_rows = dest_owner * capacity + token_pos - first_slot
    returned = lax.all_to_all(
        gated_rows.reshape(owners, capacity, -1), "batch", split_axis=0, concat_axis=0, tiled=True
    )
    own_gated = returned.reshape(owners * capacity, -1)[back_rows]
    branch_rows = jnp.dot(own_gated, output_weight, preferred_element_type=F32).astype(BF16)
    return (hidden.astype(F32) + branch_rows.astype(F32)).astype(BF16)


def batch_index():
    return lax.axis_index("batch")


def is_last():
    return lax.axis_index("batch") == lax.axis_size("batch") - 1


def silu_of(values):
    half = 0.5 * values
    return half + half * jnp.tanh(half)


def head_weights(query, key, allowed):
    scores = lax.dot_general(query, key, (((1,), (1,)), ((), ())), preferred_element_type=F32)
    half = scores * (0.5 * HEAD_DIM ** (-0.5))
    return jnp.where(allowed, half + half * jnp.tanh(half), 0.0).astype(BF16)


def seg_column(seg_row):
    wide = jnp.broadcast_to(seg_row, (128, seg_row.shape[1]))
    return wide.T[:, :1]


def segments_kernel(counts, users, seg_out):
    rows = users.shape[1]
    owners = counts.shape[1]
    position = lax.broadcasted_iota(jnp.int32, (1, rows), 1)
    end = counts[0, 0]
    owner = (position >= end).astype(jnp.int32)
    for d in range(1, owners - 1):
        end = end + counts[0, d]
        owner = owner + (position >= end).astype(jnp.int32)
    seg_out[...] = jnp.broadcast_to((owner + owners * users[...]).astype(F32), seg_out.shape)


def put_seg(ref, seg):
    rows = seg.shape[1]
    for at in range(0, ref.shape[1], rows):
        ref[rows:, at : at + rows] = seg.astype(BF16)


def silu_dot(normed, weight):
    return silu_of(jnp.dot(normed[...], weight[...], preferred_element_type=F32)).astype(BF16)


def project_first_kernel(
    part3, part2, part1, own, w_in, w_key, w_value, seg, hidden_out, normed, send_b
):
    col_at = lax.axis_index("col")
    rows, piece = own.shape
    group = w_key.shape[1]
    total = None
    for shift, part in enumerate((own, part1, part2, part3)):
        start = pl.multiple_of((col_at ^ shift) * piece, piece)
        term = jnp.dot(part[...], w_in[pl.ds(start, piece), :], preferred_element_type=F32)
        total = term if total is None else total + term
    hidden = total.astype(BF16)
    hidden_out[...] = hidden
    normed[...] = layer_norm(hidden.astype(F32)).astype(BF16)
    send_b[:rows, :group] = silu_dot(normed, w_key)
    send_b[:rows, group:] = silu_dot(normed, w_value)
    put_seg(send_b, seg[...])


def project_query_kernel(normed, w_far, w_sent, seg, send_c, send_f):
    rows = normed.shape[0]
    for weight, ref in ((w_far, send_c), (w_sent, send_f)):
        ref[:rows, :] = silu_dot(normed, weight)
        put_seg(ref, seg[...])


def project_near_kernel(
    send_b, send_c, seg, normed, w_query, w_near, w_far, w_key, w_value,
    send_a, mixed_out, query_near, gate_out,
):
    rows = normed.shape[0]
    group = w_key.shape[1]
    send_a[:rows, :group] = silu_dot(normed, w_key)
    send_a[:rows, group:] = silu_dot(normed, w_value)
    put_seg(send_a, seg[...])

    @pl.when(batch_index() == 0)
    def _():
        attend_own(
            send_a, send_b, send_c, seg, normed, (w_query, w_near, w_far),
            mixed_out, query_near, gate_out,
        )


def seg_row_of(ref, rows):
    return ref[rows : rows + SEG_ROWS, :rows].astype(F32)[0:1, :]


def add_blocks(query, key_values, out):
    group = query.shape[1]
    rows = query.shape[0] - SEG_ROWS
    column = seg_column(seg_row_of(query, rows))
    masks = [column == seg_row_of(ref, rows) for ref in key_values]
    for lo in range(0, group, HEAD_DIM):
        hi = lo + HEAD_DIM
        total = None
        for ref, allowed in zip(key_values, masks):
            weights = head_weights(query[:rows, lo:hi], ref[:rows, lo:hi], allowed)
            term = jnp.dot(
                weights, ref[:rows, group + lo : group + hi], preferred_element_type=F32
            )
            total = term if total is None else total + term
        out[:, lo:hi] = total.astype(out.dtype)


def add_near(query, column, key_value, mixed):
    rows, group = mixed.shape
    allowed = column == seg_row_of(key_value, rows)
    for lo in range(0, group, HEAD_DIM):
        hi = lo + HEAD_DIM
        weights = head_weights(query[:rows, lo:hi], key_value[:rows, lo:hi], allowed)
        mixed[:, lo:hi] += jnp.dot(
            weights, key_value[:rows, group + lo : group + hi], preferred_element_type=F32
        )


def attend_own(send_a, send_b, send_c, seg, normed, weights, mixed_out, query_near, gate_out):
    rows, group = mixed_out.shape[1:]
    w_query, w_near, w_far = weights
    seg_row = seg[0:1, :]
    allowed = (seg_column(seg_row) == seg_row) & (
        lax.broadcasted_iota(jnp.int32, (rows, rows), 1)
        <= lax.broadcasted_iota(jnp.int32, (rows, rows), 0)
    )
    query_near[...] = silu_dot(normed, w_query)
    for side, (query, key_value) in enumerate(((query_near, send_a), (send_c, send_b))):
        for lo in range(0, group, HEAD_DIM):
            hi = lo + HEAD_DIM
            weights = head_weights(query[:rows, lo:hi], key_value[:rows, lo:hi], allowed)
            mixed_out[side, :, lo:hi] = jnp.dot(
                weights, key_value[:rows, group + lo : group + hi], preferred_element_type=F32
            )
    gate_out[0] = silu_dot(normed, w_near)
    gate_out[1] = silu_dot(normed, w_far)


def own_kernel(
    send_a, send_b, send_c, seg, normed, w_query, w_near, w_far,
    mixed_in, query_in, gate_in, mixed, query_near, gate,
):
    @pl.when((batch_index() != 0) & ~is_last())
    def _():
        attend_own(
            send_a, send_b, send_c, seg, normed, (w_query, w_near, w_far), mixed, query_near, gate
        )


def far_g_kernel(got_b, send_e, send_a, got_c, send_g):
    @pl.when(batch_index() == 1)
    def _():
        add_blocks(got_c, [send_a, got_b], send_g)

    @pl.when(batch_index() != 1)
    def _():
        send_g[...] = jnp.zeros_like(send_g)


def far_e_kernel(got_b, send_a, mixed, got_f, send_e):
    @pl.when(batch_index() == 0)
    def _():
        add_blocks(got_f, [send_a], send_e)

    @pl.when(batch_index() == 1)
    def _():
        add_blocks(got_f, [send_a, got_b], send_e)

    @pl.when(batch_index() > 1)
    def _():
        send_e[...] = jnp.zeros_like(send_e)


def far_d_kernel(got_b, send_a, got_h, got_a, send_d):
    @pl.when(batch_index() == 2)
    def _():
        add_blocks(got_h, [send_a, got_b, got_a], send_d)

    @pl.when(batch_index() != 2)
    def _():
        send_d[...] = jnp.zeros_like(send_d)


def near_kernel(
    got_a, got_b, send_a, send_b, send_c, seg, normed, w_query, w_near, w_far,
    mixed_in, query_in, gate_in, mixed, query_near, gate,
):
    column = seg_column(seg[0:1, :])

    @pl.when(is_last())
    def _():
        attend_own(
            send_a, send_b, send_c, seg, normed, (w_query, w_near, w_far), mixed, query_near, gate
        )

    @pl.when(batch_index() > 0)
    def _():
        add_near(query_near, column, got_b, mixed.at[0])

    @pl.when(batch_index() == 2)
    def _():
        add_near(query_near, column, got_a, mixed.at[0])


def finish_kernel(mixed, got_d, got_eg, gate, hidden, w_out, out):
    near = batch_index() % 2
    last = is_last()
    got = got_eg[...].astype(F32)
    group = mixed.shape[2]
    sides = (
        mixed[0] + jnp.where(last, got, 0.0),
        mixed[1] + got_d[...].astype(F32) + jnp.where(last, 0.0, got),
    )
    total = sum(jnp.sum(side, axis=-1, keepdims=True) for side in sides)
    sides = [side - total / (2 * group) for side in sides]
    total = sum(jnp.sum(side * side, axis=-1, keepdims=True) for side in sides)
    scale = lax.rsqrt(total / (2 * group) + eps_norm)
    branch = None
    for index, (which, side) in enumerate(zip((near, 1 - near), sides)):
        gated = (side * scale * gate[index].astype(F32)).astype(BF16)
        start = pl.multiple_of(which * group, group)
        term = jnp.dot(gated, w_out[pl.ds(start, group), :], preferred_element_type=F32)
        branch = term if branch is None else branch + term
    out[...] = (hidden[...].astype(F32) + branch.astype(BF16).astype(F32)).astype(BF16)


VMEM = pl.BlockSpec(memory_space=pltpu.VMEM)
SMEM = pl.BlockSpec(memory_space=pltpu.SMEM)


def call(kernel, in_specs, outs, operands, flops, scratch=(), limit=32 << 20, aliases=()):
    return pl.pallas_call(
        kernel,
        out_shape=[jax.ShapeDtypeStruct(shape, dtype) for shape, dtype in outs],
        in_specs=in_specs,
        out_specs=[VMEM] * len(outs),
        scratch_shapes=list(scratch),
        input_output_aliases=dict(aliases),
        compiler_params=pltpu.CompilerParams(vmem_limit_bytes=limit),
        cost_estimate=pl.CostEstimate(flops=flops, bytes_accessed=0, transcendentals=0),
    )(*operands)


def chain_plan(lookups, input_weight, joined_weight, output_weight, owner_counts, user_index):
    cols = lax.axis_size("col")
    batch_at = lax.axis_index("batch").astype(jnp.int32)
    col_at = lax.axis_index("col").astype(jnp.int32)
    pieces = lookups.reshape(cols, lookups.shape[0] // cols, lookups.shape[1])
    rows = pieces.shape[1]

    def piece(source, shift):
        return lax.dynamic_index_in_dim(source, col_at ^ shift, 0, keepdims=False)

    def exchange(block, shift):
        return lax.ppermute(block, "col", [(i, i ^ shift) for i in range(cols)])

    across = piece(pieces, 2)
    pieces, across = lax.optimization_barrier((pieces, across))
    parts = [piece(pieces, 0)] + [
        exchange(across if shift == 2 else piece(pieces, shift), shift)
        for shift in range(1, cols)
    ]
    width = HEADS * HEAD_DIM
    group = width // 2
    features = input_weight.shape[1]
    tall = rows + SEG_ROWS
    (seg,) = call(
        segments_kernel,
        [SMEM, VMEM],
        [((SEG_ROWS, rows), F32)],
        (owner_counts, user_index.reshape(1, rows)),
        2 * rows * features * (features + 4 * width),
    )
    near = batch_at % 2
    far = 1 - near

    def weight_of(block, index):
        return lax.dynamic_slice_in_dim(joined_weight, block * width + index * group, group, 1)

    hidden, normed, send_b = call(
        project_first_kernel,
        [VMEM] * 8,
        [((rows, features), BF16), ((rows, features), BF16), ((tall, 2 * group), BF16)],
        (*parts[::-1], input_weight, weight_of(3, far), weight_of(1, far), seg),
        2 * rows * features * (features + 2 * group),
    )
    got_b = lax.ppermute(send_b, "batch", [(0, 1), (1, 2), (2, 3), (3, 0)])
    send_c, send_f = call(
        project_query_kernel,
        [VMEM] * 4,
        [((tall, group), BF16)] * 2,
        (normed, weight_of(2, far), weight_of(2, jnp.where(batch_at == 1, far, near)), seg),
        2 * rows * features * 2 * group,
    )
    got_f = lax.ppermute(send_f, "batch", [(3, 1), (1, 0)])
    own_inputs = (
        send_b, send_c, seg, normed, weight_of(2, near), weight_of(0, near), weight_of(0, far),
    )
    own_outs = [((2, rows, group), F32), ((rows, group), BF16), ((2, rows, group), BF16)]
    send_a, *own = call(
        project_near_kernel,
        [VMEM] * 9,
        [((tall, 2 * group), BF16)] + own_outs,
        (*own_inputs, weight_of(3, near), weight_of(1, near)),
        2 * rows * features * 2 * group,
    )
    got_a = lax.ppermute(send_a, "batch", [(0, 2)])
    got_c = lax.ppermute(send_c, "batch", [(2, 1)])
    got_h = lax.ppermute(send_c, "batch", [(3, 2)])
    pair_flops = 4 * rows * rows * group
    own = call(
        own_kernel,
        [VMEM] * 11,
        own_outs,
        (send_a, *own_inputs, *own),
        2 * pair_flops + 2 * rows * features * width,
        aliases={8: 0, 9: 1, 10: 2},
    )
    mixed = own[0]
    (send_e,) = call(
        far_e_kernel,
        [VMEM] * 4,
        [((rows, group), BF16)],
        (got_b, send_a, mixed, got_f),
        1 << 30,
    )
    got_e = lax.ppermute(send_e, "batch", [(1, 3), (0, 1)])
    (send_g,) = call(
        far_g_kernel,
        [VMEM] * 4,
        [((rows, group), BF16)],
        (got_b, send_e, send_a, got_c),
        1 << 30,
    )
    got_g = lax.ppermute(send_g, "batch", [(1, 2)])
    (send_d,) = call(
        far_d_kernel,
        [VMEM] * 4,
        [((rows, group), BF16)],
        (got_b, send_a, got_h, got_a),
        rows,
    )
    got_d = lax.ppermute(send_d, "batch", [(2, 3)])
    mixed, _, gate = call(
        near_kernel,
        [VMEM] * 13,
        own_outs,
        (got_a, got_b, send_a, *own_inputs, *own),
        rows,
        aliases={10: 0, 11: 1, 12: 2},
    )
    (out,) = call(
        finish_kernel,
        [VMEM] * 6,
        [((rows, features), BF16)],
        (mixed, got_d, got_e + got_g, gate, hidden, output_weight),
        rows,
    )
    return out


def solution(mesh):
    chain = mesh.shape["batch"] == HEADS and mesh.shape["col"] & (mesh.shape["col"] - 1) == 0
    return jax.shard_map(
        chain_plan if chain else owners_plan,
        mesh=mesh,
        in_specs=(
            P(("rep", "batch"), "col"),
            P(),
            P(),
            P(),
            P(("rep", "batch", "col"), None),
            P(("rep", "batch", "col")),
        ),
        out_specs=P(("rep", "batch", "col"), None),
        check_vma=False,
    )
```

```python
import functools

import jax
import jax.numpy as jnp
from jax import lax
from jax.experimental import pallas as pl
from jax.experimental.pallas import tpu as pltpu
from jax.sharding import PartitionSpec as P

HEADS = 4
HEAD_DIM = 128
SEG_ROWS = 8

eps_norm = 1e-06

F32 = jnp.float32
BF16 = jnp.bfloat16


def layer_norm(values):
    row_mean = jnp.mean(values, axis=-1, keepdims=True)
    centered = values - row_mean
    row_var = jnp.mean(centered * centered, axis=-1, keepdims=True)
    return centered * lax.rsqrt(row_var + eps_norm)


def project(hidden_rows, joined_weight):
    normed = layer_norm(hidden_rows.astype(F32)).astype(BF16)
    return jax.nn.silu(jnp.dot(normed, joined_weight, preferred_element_type=F32)).astype(BF16)


def attend(joined_rows, seg_ids):
    width = HEADS * HEAD_DIM
    total = joined_rows.shape[0]
    gate_part = joined_rows[:, :width]
    value_part = joined_rows[:, width : 2 * width].reshape(total, HEADS, HEAD_DIM)
    query_part = joined_rows[:, 2 * width : 3 * width].reshape(total, HEADS, HEAD_DIM)
    key_part = joined_rows[:, 3 * width :].reshape(total, HEADS, HEAD_DIM)
    scores = jnp.einsum(
        "ihd,jhd->hij", query_part, key_part, preferred_element_type=F32
    ) * HEAD_DIM ** (-0.5)
    positions = jnp.arange(total, dtype=jnp.int32)
    allowed = (positions[None, :] <= positions[:, None]) & (seg_ids[None, :] == seg_ids[:, None])
    weights = jnp.where(allowed[None], jax.nn.silu(scores), 0.0).astype(BF16)
    mixed = jnp.einsum(
        "hij,jhd->ihd", weights, value_part, preferred_element_type=F32
    ).reshape(total, width)
    return (layer_norm(mixed) * gate_part.astype(F32)).astype(BF16)


def owners_plan(lookups, input_weight, joined_weight, output_weight, owner_counts, user_index):
    token_block = lax.all_to_all(lookups, "col", split_axis=0, concat_axis=1, tiled=True)
    hidden = jnp.dot(token_block, input_weight, preferred_element_type=F32).astype(BF16)
    local_rows = hidden.shape[0]
    owners = lax.axis_size("batch")
    capacity = local_rows // owners + local_rows // (2 * owners)
    counts = owner_counts[0]
    bin_ends = jnp.cumsum(counts)
    bin_starts = bin_ends - counts
    slot_ids = jnp.arange(capacity, dtype=jnp.int32)
    filled = slot_ids[None, :] < counts[:, None]
    gather_rows = jnp.where(filled, bin_starts[:, None] + slot_ids[None, :], 0).reshape(-1)
    seg_send = jnp.where(filled.reshape(-1), user_index[gather_rows], -1).reshape(owners, capacity)
    payload = hidden[gather_rows].reshape(owners, capacity, -1)
    received, seg_ids = (
        lax.all_to_all(payload, "batch", split_axis=0, concat_axis=0, tiled=True),
        lax.all_to_all(seg_send, "batch", split_axis=0, concat_axis=0, tiled=True),
    )
    joined_rows = project(received.reshape(owners * capacity, -1), joined_weight)
    gated_rows = attend(joined_rows, seg_ids.reshape(-1))
    token_pos = jnp.arange(local_rows, dtype=jnp.int32)
    owner_ids = jnp.arange(owners, dtype=jnp.int32)
    dest_owner = jnp.sum((token_pos[:, None] >= bin_ends[None, :]).astype(jnp.int32), axis=1)
    onehot = dest_owner[:, None] == owner_ids[None, :]
    first_slot = jnp.sum(jnp.where(onehot, bin_starts[None, :], 0), axis=1)
    back_rows = dest_owner * capacity + token_pos - first_slot
    returned = lax.all_to_all(
        gated_rows.reshape(owners, capacity, -1), "batch", split_axis=0, concat_axis=0, tiled=True
    )
    own_gated = returned.reshape(owners * capacity, -1)[back_rows]
    branch_rows = jnp.dot(own_gated, output_weight, preferred_element_type=F32).astype(BF16)
    return (hidden.astype(F32) + branch_rows.astype(F32)).astype(BF16)


def batch_index():
    return lax.axis_index("batch")


def is_last():
    return lax.axis_index("batch") == lax.axis_size("batch") - 1


def silu_of(values):
    half = 0.5 * values
    return half + half * jnp.tanh(half)


def head_weights(query, key, allowed):
    scores = lax.dot_general(query, key, (((1,), (1,)), ((), ())), preferred_element_type=F32)
    half = scores * (0.5 * HEAD_DIM ** (-0.5))
    return jnp.where(allowed, half + half * jnp.tanh(half), 0.0).astype(BF16)


def seg_column(seg_row):
    wide = jnp.broadcast_to(seg_row, (128, seg_row.shape[1]))
    return wide.T[:, :1]


def segments_kernel(counts, users, seg_out):
    rows = users.shape[1]
    owners = counts.shape[1]
    position = lax.broadcasted_iota(jnp.int32, (1, rows), 1)
    end = counts[:, :1]
    owner = (position >= end).astype(jnp.int32)
    for d in range(1, owners - 1):
        end = end + counts[:, d : d + 1]
        owner = owner + (position >= end).astype(jnp.int32)
    seg_out[...] = jnp.broadcast_to((owner + owners * users[...]).astype(F32), seg_out.shape)


def put_seg(ref, seg):
    rows = seg.shape[1]
    for at in range(0, ref.shape[1], rows):
        ref[rows:, at : at + rows] = seg.astype(BF16)


def silu_dot(normed, weight):
    return silu_of(jnp.dot(normed[...], weight[...], preferred_element_type=F32)).astype(BF16)


def is_upward():
    return lax.axis_index("col") % 2 == 0


def put_keys(normed, w_key, w_value, out):
    rows = normed.shape[0]
    group = w_key.shape[1]
    out[:rows, :group] = silu_dot(normed, w_key)
    out[:rows, group : 2 * group] = silu_dot(normed, w_value)


def put_query(normed, w_query, out):
    rows = normed.shape[0]
    group = w_query.shape[1]
    out[:rows, :group] = silu_dot(normed, w_query)
    out[:rows, group:] = jnp.zeros((rows, group), BF16)


def add_pieces(pieces, w_in, total):
    for shift, piece in pieces.items():
        width = piece.shape[1]
        start = pl.multiple_of((lax.axis_index("col") ^ shift) * width, width)
        term = jnp.dot(piece[...], w_in[pl.ds(start, width), :], preferred_element_type=F32)
        total = term if total is None else total + term
    return total


def partial_kernel(part2, part1, own, w_in, partial):
    partial[...] = add_pieces({0: own, 1: part1, 2: part2}, w_in, None)


def project_first_kernel(
    part3, partial, w_in, w_key, w_value, w_query, seg, hidden_out, normed, send_1
):
    total = add_pieces({3: part3}, w_in, partial[...])
    hidden = total.astype(BF16)
    hidden_out[...] = hidden
    normed[...] = layer_norm(hidden.astype(F32)).astype(BF16)
    put_seg(send_1, seg[...])

    @pl.when(is_upward())
    def _():
        put_keys(normed, w_key, w_value, send_1)

    @pl.when(~is_upward())
    def _():
        put_query(normed, w_query, send_1)


def project_second_kernel(
    normed, send_1, w_key, w_value, w_query, seg, send_2, far_keys, far_query
):
    rows = normed.shape[0]
    group = w_query.shape[1]
    put_seg(send_2, seg[...])

    @pl.when(is_upward())
    def _():
        put_query(normed, w_query, send_2)
        far_query[...] = send_2[:rows, :group]
        far_keys[...] = send_1[:rows, :]

    @pl.when(~is_upward())
    def _():
        put_keys(normed, w_key, w_value, send_2)
        far_query[...] = send_1[:rows, :group]
        far_keys[...] = send_2[:rows, :]


def sort_first_kernel(got_1, got_b, got_c):
    @pl.when(is_upward())
    def _():
        got_b[...] = got_1[...]

    @pl.when(~is_upward())
    def _():
        got_c[...] = got_1[:, : got_c.shape[1]]


def sort_second_kernel(got_2, up_in, down_in, got_b, got_c):
    @pl.when(is_upward())
    def _():
        got_c[...] = got_2[:, : got_c.shape[1]]

    @pl.when(~is_upward())
    def _():
        got_b[...] = got_2[...]


def project_query_kernel(normed, w_near, seg, send_2, send_f):
    rows = normed.shape[0]
    send_f[:rows, :] = silu_dot(normed, w_near)
    put_seg(send_f, seg[...])


def attend_own(send_a, send_f, far_keys, far_query, seg, normed, w_near, w_far, mixed, gate):
    rows, group = mixed.shape[1:]
    seg_row = seg[0:1, :]
    allowed = (seg_column(seg_row) == seg_row) & (
        lax.broadcasted_iota(jnp.int32, (rows, rows), 1)
        <= lax.broadcasted_iota(jnp.int32, (rows, rows), 0)
    )
    for side, (query, key_value) in enumerate(((send_f, send_a), (far_query, far_keys))):
        for lo in range(0, group, HEAD_DIM):
            hi = lo + HEAD_DIM
            weights = head_weights(query[:rows, lo:hi], key_value[:rows, lo:hi], allowed)
            mixed[side, :, lo:hi] = jnp.dot(
                weights, key_value[:rows, group + lo : group + hi], preferred_element_type=F32
            )
    gate[0] = silu_dot(normed, w_near)
    gate[1] = silu_dot(normed, w_far)


def project_near_kernel(
    send_f, far_keys, far_query, seg, normed, w_near, w_far, w_key, w_value, send_a, mixed, gate
):
    put_keys(normed, w_key, w_value, send_a)
    put_seg(send_a, seg[...])

    @pl.when(~is_last())
    def _():
        attend_own(send_a, send_f, far_keys, far_query, seg, normed, w_near, w_far, mixed, gate)


def seg_row_of(ref, rows):
    return ref[rows : rows + SEG_ROWS, :rows].astype(F32)[0:1, :]


def add_blocks(query, key_values, out):
    group = query.shape[1]
    rows = query.shape[0] - SEG_ROWS
    column = seg_column(seg_row_of(query, rows))
    masks = [column == seg_row_of(ref, rows) for ref in key_values]
    for lo in range(0, group, HEAD_DIM):
        hi = lo + HEAD_DIM
        total = None
        for ref, allowed in zip(key_values, masks):
            weights = head_weights(query[:rows, lo:hi], ref[:rows, lo:hi], allowed)
            term = jnp.dot(
                weights, ref[:rows, group + lo : group + hi], preferred_element_type=F32
            )
            total = term if total is None else total + term
        out[:, lo:hi] = total.astype(out.dtype)


def add_near(query, column, key_value, mixed):
    rows, group = mixed.shape
    allowed = column == seg_row_of(key_value, rows)
    for lo in range(0, group, HEAD_DIM):
        hi = lo + HEAD_DIM
        weights = head_weights(query[:rows, lo:hi], key_value[:rows, lo:hi], allowed)
        mixed[:, lo:hi] += jnp.dot(
            weights, key_value[:rows, group + lo : group + hi], preferred_element_type=F32
        )


def early_kernel(got_b, got_c, send_a, early_1, early_2):
    @pl.when(batch_index() == 1)
    def _():
        add_blocks(got_c, [send_a, got_b], early_1)

    @pl.when(batch_index() == 2)
    def _():
        add_blocks(got_c, [send_a, got_b], early_2)


def far_kernel(got_b, got_c, got_f, send_a, early_1, send_e, send_g):
    @pl.when(batch_index() == 0)
    def _():
        add_blocks(got_c, [send_a], send_e)

    @pl.when(batch_index() == 1)
    def _():
        add_blocks(got_f, [send_a, got_b], send_e)
        send_g[...] = early_1[...]

    @pl.when(batch_index() > 1)
    def _():
        send_e[...] = jnp.zeros_like(send_e)

    @pl.when(batch_index() != 1)
    def _():
        send_g[...] = jnp.zeros_like(send_g)


def far_d_kernel(early_2, got_c, got_a, send_d, total):
    @pl.when(batch_index() == 2)
    def _():
        rows = total.shape[0]
        total[...] = early_2[...]
        add_near(got_c, seg_column(seg_row_of(got_c, rows)), got_a, total)
        send_d[...] = total[...].astype(BF16)

    @pl.when(batch_index() != 2)
    def _():
        send_d[...] = jnp.zeros_like(send_d)


def near_kernel(
    got_a, got_b, send_a, send_f, far_keys, far_query, seg, normed, w_near, w_far,
    mixed_in, gate_in, mixed, gate,
):
    column = seg_column(seg[0:1, :])

    @pl.when(is_last())
    def _():
        attend_own(send_a, send_f, far_keys, far_query, seg, normed, w_near, w_far, mixed, gate)

    @pl.when(batch_index() > 0)
    def _():
        add_near(send_f, column, got_b, mixed.at[0])

    @pl.when(batch_index() == 2)
    def _():
        add_near(send_f, column, got_a, mixed.at[0])


def finish_kernel(mixed, got_d, got_eg, gate, hidden, w_out, out):
    near = batch_index() % 2
    last = is_last()
    got = got_eg[...].astype(F32)
    group = mixed.shape[2]
    sides = (
        mixed[0] + jnp.where(last, got, 0.0),
        mixed[1] + got_d[...].astype(F32) + jnp.where(last, 0.0, got),
    )
    total = sum(jnp.sum(side, axis=-1, keepdims=True) for side in sides)
    sides = [side - total / (2 * group) for side in sides]
    total = sum(jnp.sum(side * side, axis=-1, keepdims=True) for side in sides)
    scale = lax.rsqrt(total / (2 * group) + eps_norm)
    branch = None
    for index, (which, side) in enumerate(zip((near, 1 - near), sides)):
        gated = (side * scale * gate[index].astype(F32)).astype(BF16)
        start = pl.multiple_of(which * group, group)
        term = jnp.dot(gated, w_out[pl.ds(start, group), :], preferred_element_type=F32)
        branch = term if branch is None else branch + term
    out[...] = (hidden[...].astype(F32) + branch.astype(BF16).astype(F32)).astype(BF16)


VMEM = pl.BlockSpec(memory_space=pltpu.VMEM)


def call(kernel, in_specs, outs, operands, flops, scratch=(), limit=32 << 20, aliases=()):
    return pl.pallas_call(
        kernel,
        out_shape=[jax.ShapeDtypeStruct(shape, dtype) for shape, dtype in outs],
        in_specs=in_specs,
        out_specs=[VMEM] * len(outs),
        scratch_shapes=list(scratch),
        input_output_aliases=dict(aliases),
        compiler_params=pltpu.CompilerParams(vmem_limit_bytes=limit),
        cost_estimate=pl.CostEstimate(flops=flops, bytes_accessed=0, transcendentals=0),
    )(*operands)


def chain_plan(lookups, input_weight, joined_weight, output_weight, owner_counts, user_index):
    cols = lax.axis_size("col")
    batch_at = lax.axis_index("batch").astype(jnp.int32)
    col_at = lax.axis_index("col").astype(jnp.int32)
    pieces = lookups.reshape(cols, lookups.shape[0] // cols, lookups.shape[1])
    rows = pieces.shape[1]

    def piece(source, shift):
        return lax.dynamic_index_in_dim(source, col_at ^ shift, 0, keepdims=False)

    def exchange(block, shift):
        return lax.ppermute(block, "col", [(i, i ^ shift) for i in range(cols)])

    across = piece(pieces, 2)
    pieces, across = lax.optimization_barrier((pieces, across))
    parts = [piece(pieces, 0)] + [
        exchange(across if shift == 2 else piece(pieces, shift), shift)
        for shift in range(1, cols)
    ]
    width = HEADS * HEAD_DIM
    group = width // 2
    features = input_weight.shape[1]
    tall = rows + SEG_ROWS
    (seg,) = call(
        segments_kernel,
        [VMEM] * 2,
        [((SEG_ROWS, rows), F32)],
        (owner_counts, user_index.reshape(1, rows)),
        1 << 30,
    )
    near = batch_at % 2
    far = 1 - near

    def weight_of(block, index):
        return lax.dynamic_slice_in_dim(joined_weight, block * width + index * group, group, 1)

    last = lax.axis_size("batch") - 1

    def up_and_down(block, parity):
        perm = []
        for at in range(cols):
            step = 1 if at % 2 == parity else -1
            for source in range(last + 1):
                inside = 0 <= source + step <= last
                target = (source + step, at) if inside else (source, at ^ 1)
                perm.append((source * cols + at, target[0] * cols + target[1]))
        return lax.ppermute(block, ("batch", "col"), perm)

    far_weights = (weight_of(3, far), weight_of(1, far), weight_of(2, far))
    (partial,) = call(
        partial_kernel,
        [VMEM] * 4,
        [((rows, features), F32)],
        (parts[2], parts[1], parts[0], input_weight),
        rows,
    )
    hidden, normed, send_1 = call(
        project_first_kernel,
        [VMEM] * 7,
        [((rows, features), BF16), ((rows, features), BF16), ((tall, 2 * group), BF16)],
        (parts[3], partial, input_weight, *far_weights, seg),
        2 * rows * features * (features + 2 * group),
    )
    got_1 = up_and_down(send_1, 0)
    send_2, far_keys, far_query = call(
        project_second_kernel,
        [VMEM] * 6,
        [((tall, 2 * group), BF16), ((rows, 2 * group), BF16), ((rows, group), BF16)],
        (normed, send_1, *far_weights, seg),
        2 * rows * features * 2 * group,
    )
    got_2 = up_and_down(send_2, 1)
    (send_f,) = call(
        project_query_kernel,
        [VMEM] * 4,
        [((tall, group), BF16)],
        (normed, weight_of(2, near), seg, send_2),
        2 * rows * features * group,
    )
    got_f = lax.ppermute(send_f, "batch", [(3, 1)])
    own_inputs = (send_f, far_keys, far_query, seg, normed, weight_of(0, near), weight_of(0, far))
    own_outs = [((2, rows, group), F32), ((2, rows, group), BF16)]
    send_a, *own = call(
        project_near_kernel,
        [VMEM] * 9,
        [((tall, 2 * group), BF16)] + own_outs,
        (*own_inputs, weight_of(3, near), weight_of(1, near)),
        2 * rows * features * 2 * group,
    )
    got_a = lax.ppermute(send_a, "batch", [(0, 2)])
    sorted_outs = [((tall, 2 * group), BF16), ((tall, group), BF16)]
    got_b, got_c = call(sort_first_kernel, [VMEM], sorted_outs, (got_1,), 1 << 30)
    got_b, got_c = call(
        sort_second_kernel, [VMEM] * 3, sorted_outs, (got_2, got_b, got_c), rows,
        aliases={1: 0, 2: 1},
    )
    early_1, early_2 = call(
        early_kernel,
        [VMEM] * 3,
        [((rows, group), BF16), ((rows, group), F32)],
        (got_b, got_c, send_a),
        1 << 30,
    )
    send_e, send_g = call(
        far_kernel,
        [VMEM] * 5,
        [((rows, group), BF16)] * 2,
        (got_b, got_c, got_f, send_a, early_1),
        1 << 30,
    )
    got_e = lax.ppermute(send_e, "batch", [(1, 3), (0, 1)])
    got_g = lax.ppermute(send_g, "batch", [(1, 2)])
    (send_d,) = call(
        far_d_kernel,
        [VMEM] * 3,
        [((rows, group), BF16)],
        (early_2, got_c, got_a),
        rows,
        [pltpu.VMEM((rows, group), F32)],
    )
    got_d = lax.ppermute(send_d, "batch", [(2, 3)])
    mixed, gate = call(
        near_kernel,
        [VMEM] * 12,
        own_outs,
        (got_a, got_b, send_a, *own_inputs, *own),
        rows,
        aliases={10: 0, 11: 1},
    )
    (out,) = call(
        finish_kernel,
        [VMEM] * 6,
        [((rows, features), BF16)],
        (mixed, got_d, got_e + got_g, gate, hidden, output_weight),
        rows,
    )
    return out


def solution(mesh):
    chain = mesh.shape["batch"] == HEADS and mesh.shape["col"] & (mesh.shape["col"] - 1) == 0
    return jax.shard_map(
        chain_plan if chain else owners_plan,
        mesh=mesh,
        in_specs=(
            P(("rep", "batch"), "col"),
            P(),
            P(),
            P(),
            P(("rep", "batch", "col"), None),
            P(("rep", "batch", "col")),
        ),
        out_specs=P(("rep", "batch", "col"), None),
        check_vma=False,
    )
```

```python
import functools

import jax
import jax.numpy as jnp
from jax import lax
from jax.experimental import pallas as pl
from jax.experimental.pallas import tpu as pltpu
from jax.sharding import PartitionSpec as P

HEADS = 4
HEAD_DIM = 128
SEG_ROWS = 8

eps_norm = 1e-06

F32 = jnp.float32
BF16 = jnp.bfloat16


def layer_norm(values):
    row_mean = jnp.mean(values, axis=-1, keepdims=True)
    centered = values - row_mean
    row_var = jnp.mean(centered * centered, axis=-1, keepdims=True)
    return centered * lax.rsqrt(row_var + eps_norm)


def project(hidden_rows, joined_weight):
    normed = layer_norm(hidden_rows.astype(F32)).astype(BF16)
    return jax.nn.silu(jnp.dot(normed, joined_weight, preferred_element_type=F32)).astype(BF16)


def attend(joined_rows, seg_ids):
    width = HEADS * HEAD_DIM
    total = joined_rows.shape[0]
    gate_part = joined_rows[:, :width]
    value_part = joined_rows[:, width : 2 * width].reshape(total, HEADS, HEAD_DIM)
    query_part = joined_rows[:, 2 * width : 3 * width].reshape(total, HEADS, HEAD_DIM)
    key_part = joined_rows[:, 3 * width :].reshape(total, HEADS, HEAD_DIM)
    scores = jnp.einsum(
        "ihd,jhd->hij", query_part, key_part, preferred_element_type=F32
    ) * HEAD_DIM ** (-0.5)
    positions = jnp.arange(total, dtype=jnp.int32)
    allowed = (positions[None, :] <= positions[:, None]) & (seg_ids[None, :] == seg_ids[:, None])
    weights = jnp.where(allowed[None], jax.nn.silu(scores), 0.0).astype(BF16)
    mixed = jnp.einsum(
        "hij,jhd->ihd", weights, value_part, preferred_element_type=F32
    ).reshape(total, width)
    return (layer_norm(mixed) * gate_part.astype(F32)).astype(BF16)


def owners_plan(lookups, input_weight, joined_weight, output_weight, owner_counts, user_index):
    token_block = lax.all_to_all(lookups, "col", split_axis=0, concat_axis=1, tiled=True)
    hidden = jnp.dot(token_block, input_weight, preferred_element_type=F32).astype(BF16)
    local_rows = hidden.shape[0]
    owners = lax.axis_size("batch")
    capacity = local_rows // owners + local_rows // (2 * owners)
    counts = owner_counts[0]
    bin_ends = jnp.cumsum(counts)
    bin_starts = bin_ends - counts
    slot_ids = jnp.arange(capacity, dtype=jnp.int32)
    filled = slot_ids[None, :] < counts[:, None]
    gather_rows = jnp.where(filled, bin_starts[:, None] + slot_ids[None, :], 0).reshape(-1)
    seg_send = jnp.where(filled.reshape(-1), user_index[gather_rows], -1).reshape(owners, capacity)
    payload = hidden[gather_rows].reshape(owners, capacity, -1)
    received, seg_ids = (
        lax.all_to_all(payload, "batch", split_axis=0, concat_axis=0, tiled=True),
        lax.all_to_all(seg_send, "batch", split_axis=0, concat_axis=0, tiled=True),
    )
    joined_rows = project(received.reshape(owners * capacity, -1), joined_weight)
    gated_rows = attend(joined_rows, seg_ids.reshape(-1))
    token_pos = jnp.arange(local_rows, dtype=jnp.int32)
    owner_ids = jnp.arange(owners, dtype=jnp.int32)
    dest_owner = jnp.sum((token_pos[:, None] >= bin_ends[None, :]).astype(jnp.int32), axis=1)
    onehot = dest_owner[:, None] == owner_ids[None, :]
    first_slot = jnp.sum(jnp.where(onehot, bin_starts[None, :], 0), axis=1)
    back_rows = dest_owner * capacity + token_pos - first_slot
    returned = lax.all_to_all(
        gated_rows.reshape(owners, capacity, -1), "batch", split_axis=0, concat_axis=0, tiled=True
    )
    own_gated = returned.reshape(owners * capacity, -1)[back_rows]
    branch_rows = jnp.dot(own_gated, output_weight, preferred_element_type=F32).astype(BF16)
    return (hidden.astype(F32) + branch_rows.astype(F32)).astype(BF16)


def batch_index():
    return lax.axis_index("batch")


def is_last():
    return lax.axis_index("batch") == lax.axis_size("batch") - 1


def silu_of(values):
    half = 0.5 * values
    return half + half * jnp.tanh(half)


def head_weights(query, key, allowed):
    scores = lax.dot_general(query, key, (((1,), (1,)), ((), ())), preferred_element_type=F32)
    half = scores * (0.5 * HEAD_DIM ** (-0.5))
    return jnp.where(allowed, half + half * jnp.tanh(half), 0.0).astype(BF16)


def seg_column(seg_row):
    wide = jnp.broadcast_to(seg_row, (128, seg_row.shape[1]))
    return wide.T[:, :1]


def segments_kernel(counts, users, seg_out):
    rows = users.shape[1]
    owners = counts.shape[1]
    position = lax.broadcasted_iota(jnp.int32, (1, rows), 1)
    end = counts[:, :1]
    owner = (position >= end).astype(jnp.int32)
    for d in range(1, owners - 1):
        end = end + counts[:, d : d + 1]
        owner = owner + (position >= end).astype(jnp.int32)
    seg_out[...] = jnp.broadcast_to((owner + owners * users[...]).astype(F32), seg_out.shape)


def put_seg(ref, seg):
    rows = seg.shape[1]
    for at in range(0, ref.shape[1], rows):
        ref[rows:, at : at + rows] = seg.astype(BF16)


def silu_dot(normed, weight):
    return silu_of(jnp.dot(normed[...], weight[...], preferred_element_type=F32)).astype(BF16)


def is_upward():
    return lax.axis_index("col") % 2 == 0


def put_keys(normed, w_key, w_value, out):
    rows = normed.shape[0]
    group = w_key.shape[1]
    out[:rows, :group] = silu_dot(normed, w_key)
    out[:rows, group : 2 * group] = silu_dot(normed, w_value)


def put_query(normed, w_query, out):
    rows = normed.shape[0]
    group = w_query.shape[1]
    out[:rows, :group] = silu_dot(normed, w_query)
    out[:rows, group:] = jnp.zeros((rows, group), BF16)


def add_pieces(pieces, w_in, total):
    for shift, piece in pieces.items():
        width = piece.shape[1]
        start = pl.multiple_of((lax.axis_index("col") ^ shift) * width, width)
        term = jnp.dot(piece[...], w_in[pl.ds(start, width), :], preferred_element_type=F32)
        total = term if total is None else total + term
    return total


def partial_kernel(part2, part1, own, w_in, partial):
    partial[...] = add_pieces({0: own, 1: part1, 2: part2}, w_in, None)


def project_first_kernel(
    part3, partial, w_in, w_key, w_value, w_query, seg, hidden_out, normed, send_1
):
    total = add_pieces({3: part3}, w_in, partial[...])
    hidden = total.astype(BF16)
    hidden_out[...] = hidden
    normed[...] = layer_norm(hidden.astype(F32)).astype(BF16)
    put_seg(send_1, seg[...])

    @pl.when(is_upward())
    def _():
        put_keys(normed, w_key, w_value, send_1)

    @pl.when(~is_upward())
    def _():
        put_query(normed, w_query, send_1)


def project_second_kernel(
    normed, send_1, w_key, w_value, w_query, seg, send_2, far_keys, far_query
):
    rows = normed.shape[0]
    group = w_query.shape[1]
    put_seg(send_2, seg[...])

    @pl.when(is_upward())
    def _():
        put_query(normed, w_query, send_2)
        far_query[...] = send_2[:rows, :group]
        far_keys[...] = send_1[:rows, :]

    @pl.when(~is_upward())
    def _():
        put_keys(normed, w_key, w_value, send_2)
        far_query[...] = send_1[:rows, :group]
        far_keys[...] = send_2[:rows, :]


def sort_first_kernel(got_1, got_b, got_c):
    @pl.when(is_upward())
    def _():
        got_b[...] = got_1[...]

    @pl.when(~is_upward())
    def _():
        got_c[...] = got_1[:, : got_c.shape[1]]


def sort_second_kernel(got_2, up_in, down_in, got_b, got_c):
    @pl.when(is_upward())
    def _():
        got_c[...] = got_2[:, : got_c.shape[1]]

    @pl.when(~is_upward())
    def _():
        got_b[...] = got_2[...]


def project_query_kernel(normed, w_near, seg, send_2, send_f):
    rows = normed.shape[0]
    send_f[:rows, :] = silu_dot(normed, w_near)
    put_seg(send_f, seg[...])


def attend_own(send_a, send_f, far_keys, far_query, seg, normed, w_near, w_far, mixed, gate):
    rows, group = mixed.shape[1:]
    seg_row = seg[0:1, :]
    allowed = (seg_column(seg_row) == seg_row) & (
        lax.broadcasted_iota(jnp.int32, (rows, rows), 1)
        <= lax.broadcasted_iota(jnp.int32, (rows, rows), 0)
    )
    for side, (query, key_value) in enumerate(((send_f, send_a), (far_query, far_keys))):
        for lo in range(0, group, HEAD_DIM):
            hi = lo + HEAD_DIM
            weights = head_weights(query[:rows, lo:hi], key_value[:rows, lo:hi], allowed)
            mixed[side, :, lo:hi] = jnp.dot(
                weights, key_value[:rows, group + lo : group + hi], preferred_element_type=F32
            )
    gate[0] = silu_dot(normed, w_near)
    gate[1] = silu_dot(normed, w_far)


def project_near_kernel(
    send_f, far_keys, far_query, seg, normed, w_near, w_far, w_key, w_value, send_a, mixed, gate
):
    put_keys(normed, w_key, w_value, send_a)
    put_seg(send_a, seg[...])

    @pl.when(~is_last())
    def _():
        attend_own(send_a, send_f, far_keys, far_query, seg, normed, w_near, w_far, mixed, gate)


def seg_row_of(ref, rows):
    return ref[rows : rows + SEG_ROWS, :rows].astype(F32)[0:1, :]


def add_blocks(query, key_values, out):
    group = query.shape[1]
    rows = query.shape[0] - SEG_ROWS
    column = seg_column(seg_row_of(query, rows))
    masks = [column == seg_row_of(ref, rows) for ref in key_values]
    for lo in range(0, group, HEAD_DIM):
        hi = lo + HEAD_DIM
        total = None
        for ref, allowed in zip(key_values, masks):
            weights = head_weights(query[:rows, lo:hi], ref[:rows, lo:hi], allowed)
            term = jnp.dot(
                weights, ref[:rows, group + lo : group + hi], preferred_element_type=F32
            )
            total = term if total is None else total + term
        out[:, lo:hi] = total.astype(out.dtype)


def add_near(query, column, key_value, mixed):
    rows, group = mixed.shape
    allowed = column == seg_row_of(key_value, rows)
    for lo in range(0, group, HEAD_DIM):
        hi = lo + HEAD_DIM
        weights = head_weights(query[:rows, lo:hi], key_value[:rows, lo:hi], allowed)
        mixed[:, lo:hi] += jnp.dot(
            weights, key_value[:rows, group + lo : group + hi], preferred_element_type=F32
        )


def early_kernel(got_b, got_c, send_a, early_1, early_2):
    @pl.when(batch_index() == 1)
    def _():
        add_blocks(got_c, [send_a, got_b], early_1)

    @pl.when(batch_index() == 2)
    def _():
        add_blocks(got_c, [send_a, got_b], early_2)


def far_kernel(got_b, got_c, got_f, send_a, early_1, send_e, send_g):
    @pl.when(batch_index() == 0)
    def _():
        add_blocks(got_c, [send_a], send_e)

    @pl.when(batch_index() == 1)
    def _():
        add_blocks(got_f, [send_a, got_b], send_e)
        send_g[...] = early_1[...]

    @pl.when(batch_index() > 1)
    def _():
        send_e[...] = jnp.zeros_like(send_e)

    @pl.when(batch_index() != 1)
    def _():
        send_g[...] = jnp.zeros_like(send_g)


def far_d_kernel(early_2, got_c, got_a, send_d, total):
    @pl.when(batch_index() == 2)
    def _():
        rows = total.shape[0]
        total[...] = early_2[...]
        add_near(got_c, seg_column(seg_row_of(got_c, rows)), got_a, total)
        send_d[...] = total[...].astype(BF16)

    @pl.when(batch_index() != 2)
    def _():
        send_d[...] = jnp.zeros_like(send_d)


def near_kernel(
    got_a, got_b, send_a, send_f, far_keys, far_query, seg, normed, w_near, w_far,
    mixed_in, gate_in, mixed, gate,
):
    column = seg_column(seg[0:1, :])

    @pl.when(is_last())
    def _():
        attend_own(send_a, send_f, far_keys, far_query, seg, normed, w_near, w_far, mixed, gate)

    @pl.when(batch_index() > 0)
    def _():
        add_near(send_f, column, got_b, mixed.at[0])

    @pl.when(batch_index() == 2)
    def _():
        add_near(send_f, column, got_a, mixed.at[0])


def finish_kernel(mixed, got_d, got_eg, gate, hidden, w_out, out):
    near = batch_index() % 2
    last = is_last()
    got = got_eg[...].astype(F32)
    group = mixed.shape[2]
    sides = (
        mixed[0] + jnp.where(last, got, 0.0),
        mixed[1] + got_d[...].astype(F32) + jnp.where(last, 0.0, got),
    )
    total = sum(jnp.sum(side, axis=-1, keepdims=True) for side in sides)
    sides = [side - total / (2 * group) for side in sides]
    total = sum(jnp.sum(side * side, axis=-1, keepdims=True) for side in sides)
    scale = lax.rsqrt(total / (2 * group) + eps_norm)
    branch = None
    for index, (which, side) in enumerate(zip((near, 1 - near), sides)):
        gated = (side * scale * gate[index].astype(F32)).astype(BF16)
        start = pl.multiple_of(which * group, group)
        term = jnp.dot(gated, w_out[pl.ds(start, group), :], preferred_element_type=F32)
        branch = term if branch is None else branch + term
    out[...] = (hidden[...].astype(F32) + branch.astype(BF16).astype(F32)).astype(BF16)


VMEM = pl.BlockSpec(memory_space=pltpu.VMEM)


def call(kernel, in_specs, outs, operands, flops, scratch=(), limit=32 << 20, aliases=()):
    return pl.pallas_call(
        kernel,
        out_shape=[jax.ShapeDtypeStruct(shape, dtype) for shape, dtype in outs],
        in_specs=in_specs,
        out_specs=[VMEM] * len(outs),
        scratch_shapes=list(scratch),
        input_output_aliases=dict(aliases),
        compiler_params=pltpu.CompilerParams(vmem_limit_bytes=limit),
        cost_estimate=pl.CostEstimate(flops=flops, bytes_accessed=0, transcendentals=0),
    )(*operands)


def chain_plan(lookups, input_weight, joined_weight, output_weight, owner_counts, user_index):
    cols = lax.axis_size("col")
    batch_at = lax.axis_index("batch").astype(jnp.int32)
    col_at = lax.axis_index("col").astype(jnp.int32)
    pieces = lookups.reshape(cols, lookups.shape[0] // cols, lookups.shape[1])
    rows = pieces.shape[1]

    def piece(source, shift):
        return lax.dynamic_index_in_dim(source, col_at ^ shift, 0, keepdims=False)

    def exchange(block, shift):
        return lax.ppermute(block, "col", [(i, i ^ shift) for i in range(cols)])

    across = piece(pieces, 2)
    pieces, across = lax.optimization_barrier((pieces, across))
    parts = [piece(pieces, 0)] + [
        exchange(across if shift == 2 else piece(pieces, shift), shift)
        for shift in range(1, cols)
    ]
    width = HEADS * HEAD_DIM
    group = width // 2
    features = input_weight.shape[1]
    tall = rows + SEG_ROWS
    (seg,) = call(
        segments_kernel,
        [VMEM] * 2,
        [((SEG_ROWS, rows), F32)],
        (owner_counts, user_index.reshape(1, rows)),
        1 << 30,
    )
    near = batch_at % 2
    far = 1 - near

    def weight_of(block, index):
        return lax.dynamic_slice_in_dim(joined_weight, block * width + index * group, group, 1)

    last = lax.axis_size("batch") - 1

    def up_and_down(block, parity):
        perm = []
        for at in range(cols):
            step = 1 if at % 2 == parity else -1
            for source in range(last + 1):
                inside = 0 <= source + step <= last
                target = (source + step, at) if inside else (source, at ^ 1)
                perm.append((source * cols + at, target[0] * cols + target[1]))
        return lax.ppermute(block, ("batch", "col"), perm)

    def closed(block, legs):
        perm = []
        for at in range(cols):
            for source in range(last + 1):
                target = (legs[source], at) if source in legs else (source, at ^ 1)
                perm.append((source * cols + at, target[0] * cols + target[1]))
        return lax.ppermute(block, ("batch", "col"), perm)

    far_weights = (weight_of(3, far), weight_of(1, far), weight_of(2, far))
    (partial,) = call(
        partial_kernel,
        [VMEM] * 4,
        [((rows, features), F32)],
        (parts[2], parts[1], parts[0], input_weight),
        rows,
    )
    hidden, normed, send_1 = call(
        project_first_kernel,
        [VMEM] * 7,
        [((rows, features), BF16), ((rows, features), BF16), ((tall, 2 * group), BF16)],
        (parts[3], partial, input_weight, *far_weights, seg),
        2 * rows * features * (features + 2 * group),
    )
    got_1 = up_and_down(send_1, 0)
    send_2, far_keys, far_query = call(
        project_second_kernel,
        [VMEM] * 6,
        [((tall, 2 * group), BF16), ((rows, 2 * group), BF16), ((rows, group), BF16)],
        (normed, send_1, *far_weights, seg),
        2 * rows * features * 2 * group,
    )
    got_2 = up_and_down(send_2, 1)
    (send_f,) = call(
        project_query_kernel,
        [VMEM] * 4,
        [((tall, group), BF16)],
        (normed, weight_of(2, near), seg, send_2),
        2 * rows * features * group,
    )
    got_f = lax.ppermute(send_f, "batch", [(3, 1)])
    own_inputs = (send_f, far_keys, far_query, seg, normed, weight_of(0, near), weight_of(0, far))
    own_outs = [((2, rows, group), F32), ((2, rows, group), BF16)]
    send_a, *own = call(
        project_near_kernel,
        [VMEM] * 9,
        [((tall, 2 * group), BF16)] + own_outs,
        (*own_inputs, weight_of(3, near), weight_of(1, near)),
        2 * rows * features * 2 * group,
    )
    got_a = lax.ppermute(send_a, "batch", [(0, 2)])
    sorted_outs = [((tall, 2 * group), BF16), ((tall, group), BF16)]
    got_b, got_c = call(sort_first_kernel, [VMEM], sorted_outs, (got_1,), 1 << 30)
    got_b, got_c = call(
        sort_second_kernel, [VMEM] * 3, sorted_outs, (got_2, got_b, got_c), rows,
        aliases={1: 0, 2: 1},
    )
    early_1, early_2 = call(
        early_kernel,
        [VMEM] * 3,
        [((rows, group), BF16), ((rows, group), F32)],
        (got_b, got_c, send_a),
        1 << 30,
    )
    send_e, send_g = call(
        far_kernel,
        [VMEM] * 5,
        [((rows, group), BF16)] * 2,
        (got_b, got_c, got_f, send_a, early_1),
        1 << 30,
    )
    got_e = lax.ppermute(send_e, "batch", [(1, 3), (0, 1)])
    got_g = closed(send_g, {1: 2, 2: 1})
    (send_d,) = call(
        far_d_kernel,
        [VMEM] * 3,
        [((rows, group), BF16)],
        (early_2, got_c, got_a),
        rows,
        [pltpu.VMEM((rows, group), F32)],
    )
    got_d = closed(send_d, {2: 3, 3: 2})
    mixed, gate = call(
        near_kernel,
        [VMEM] * 12,
        own_outs,
        (got_a, got_b, send_a, *own_inputs, *own),
        rows,
        aliases={10: 0, 11: 1},
    )
    (out,) = call(
        finish_kernel,
        [VMEM] * 6,
        [((rows, features), BF16)],
        (mixed, got_d, got_e + got_g, gate, hidden, output_weight),
        rows,
    )
    return out


def solution(mesh):
    chain = mesh.shape["batch"] == HEADS and mesh.shape["col"] & (mesh.shape["col"] - 1) == 0
    return jax.shard_map(
        chain_plan if chain else owners_plan,
        mesh=mesh,
        in_specs=(
            P(("rep", "batch"), "col"),
            P(),
            P(),
            P(),
            P(("rep", "batch", "col"), None),
            P(("rep", "batch", "col")),
        ),
        out_specs=P(("rep", "batch", "col"), None),
        check_vma=False,
    )
```

```python
import jax
import jax.numpy as jnp
from jax import lax
from jax.experimental import pallas as pl
from jax.experimental.pallas import tpu as pltpu
from jax.sharding import PartitionSpec as P

HEADS = 4
HEAD_DIM = 128
SEG_ROWS = 8

eps_norm = 1e-06

F32 = jnp.float32
BF16 = jnp.bfloat16


def layer_norm(values):
    row_mean = jnp.mean(values, axis=-1, keepdims=True)
    centered = values - row_mean
    row_var = jnp.mean(centered * centered, axis=-1, keepdims=True)
    return centered * lax.rsqrt(row_var + eps_norm)


def project(hidden_rows, joined_weight):
    normed = layer_norm(hidden_rows.astype(F32)).astype(BF16)
    return jax.nn.silu(jnp.dot(normed, joined_weight, preferred_element_type=F32)).astype(BF16)


def attend(joined_rows, seg_ids):
    width = HEADS * HEAD_DIM
    total = joined_rows.shape[0]
    gate_part = joined_rows[:, :width]
    value_part = joined_rows[:, width : 2 * width].reshape(total, HEADS, HEAD_DIM)
    query_part = joined_rows[:, 2 * width : 3 * width].reshape(total, HEADS, HEAD_DIM)
    key_part = joined_rows[:, 3 * width :].reshape(total, HEADS, HEAD_DIM)
    scores = jnp.einsum(
        "ihd,jhd->hij", query_part, key_part, preferred_element_type=F32
    ) * HEAD_DIM ** (-0.5)
    positions = jnp.arange(total, dtype=jnp.int32)
    allowed = (positions[None, :] <= positions[:, None]) & (seg_ids[None, :] == seg_ids[:, None])
    weights = jnp.where(allowed[None], jax.nn.silu(scores), 0.0).astype(BF16)
    mixed = jnp.einsum(
        "hij,jhd->ihd", weights, value_part, preferred_element_type=F32
    ).reshape(total, width)
    return (layer_norm(mixed) * gate_part.astype(F32)).astype(BF16)


def owners_plan(lookups, input_weight, joined_weight, output_weight, owner_counts, user_index):
    token_block = lax.all_to_all(lookups, "col", split_axis=0, concat_axis=1, tiled=True)
    hidden = jnp.dot(token_block, input_weight, preferred_element_type=F32).astype(BF16)
    local_rows = hidden.shape[0]
    owners = lax.axis_size("batch")
    capacity = local_rows // owners + local_rows // (2 * owners)
    counts = owner_counts[0]
    bin_ends = jnp.cumsum(counts)
    bin_starts = bin_ends - counts
    slot_ids = jnp.arange(capacity, dtype=jnp.int32)
    filled = slot_ids[None, :] < counts[:, None]
    gather_rows = jnp.where(filled, bin_starts[:, None] + slot_ids[None, :], 0).reshape(-1)
    seg_send = jnp.where(filled.reshape(-1), user_index[gather_rows], -1).reshape(owners, capacity)
    payload = hidden[gather_rows].reshape(owners, capacity, -1)
    received, seg_ids = (
        lax.all_to_all(payload, "batch", split_axis=0, concat_axis=0, tiled=True),
        lax.all_to_all(seg_send, "batch", split_axis=0, concat_axis=0, tiled=True),
    )
    joined_rows = project(received.reshape(owners * capacity, -1), joined_weight)
    gated_rows = attend(joined_rows, seg_ids.reshape(-1))
    token_pos = jnp.arange(local_rows, dtype=jnp.int32)
    owner_ids = jnp.arange(owners, dtype=jnp.int32)
    dest_owner = jnp.sum((token_pos[:, None] >= bin_ends[None, :]).astype(jnp.int32), axis=1)
    onehot = dest_owner[:, None] == owner_ids[None, :]
    first_slot = jnp.sum(jnp.where(onehot, bin_starts[None, :], 0), axis=1)
    back_rows = dest_owner * capacity + token_pos - first_slot
    returned = lax.all_to_all(
        gated_rows.reshape(owners, capacity, -1), "batch", split_axis=0, concat_axis=0, tiled=True
    )
    own_gated = returned.reshape(owners * capacity, -1)[back_rows]
    branch_rows = jnp.dot(own_gated, output_weight, preferred_element_type=F32).astype(BF16)
    return (hidden.astype(F32) + branch_rows.astype(F32)).astype(BF16)


def batch_index():
    return lax.axis_index("batch")


def is_last():
    return lax.axis_index("batch") == lax.axis_size("batch") - 1


def silu_of(values):
    half = 0.5 * values
    return half + half * jnp.tanh(half)


def head_weights(query, key, allowed):
    scores = lax.dot_general(query, key, (((1,), (1,)), ((), ())), preferred_element_type=F32)
    half = scores * (0.5 * HEAD_DIM ** (-0.5))
    return jnp.where(allowed, half + half * jnp.tanh(half), 0.0).astype(BF16)


def seg_column(seg_row):
    wide = jnp.broadcast_to(seg_row, (128, seg_row.shape[1]))
    return wide.T[:, :1]


def segments_kernel(counts, users, seg_out):
    rows = users.shape[1]
    owners = counts.shape[1]
    position = lax.broadcasted_iota(jnp.int32, (1, rows), 1)
    end = counts[:, :1]
    owner = (position >= end).astype(jnp.int32)
    for d in range(1, owners - 1):
        end = end + counts[:, d : d + 1]
        owner = owner + (position >= end).astype(jnp.int32)
    seg_out[...] = jnp.broadcast_to((owner + owners * users[...]).astype(F32), seg_out.shape)


def put_seg(ref, seg):
    rows = seg.shape[1]
    for at in range(0, ref.shape[1], rows):
        ref[rows:, at : at + rows] = seg.astype(BF16)


def silu_dot(normed, weight):
    return silu_of(jnp.dot(normed[...], weight[...], preferred_element_type=F32)).astype(BF16)


def is_upward():
    return lax.axis_index("col") % 2 == 0


def put_keys(normed, w_key, w_value, out):
    rows = normed.shape[0]
    group = w_key.shape[1]
    out[:rows, :group] = silu_dot(normed, w_key)
    out[:rows, group : 2 * group] = silu_dot(normed, w_value)


def put_query(normed, w_query, out):
    rows = normed.shape[0]
    group = w_query.shape[1]
    out[:rows, :group] = silu_dot(normed, w_query)
    out[:rows, group:] = jnp.zeros((rows, group), BF16)


def add_pieces(pieces, w_in, total):
    for shift, piece in pieces.items():
        width = piece.shape[1]
        start = pl.multiple_of((lax.axis_index("col") ^ shift) * width, width)
        term = jnp.dot(piece[...], w_in[pl.ds(start, width), :], preferred_element_type=F32)
        total = term if total is None else total + term
    return total


def partial_kernel(part2, part1, own, w_in, partial):
    partial[...] = add_pieces({0: own, 1: part1, 2: part2}, w_in, None)


def project_first_kernel(
    part3, partial, w_in, w_key, w_value, w_query, seg, hidden_out, normed, send_1
):
    total = add_pieces({3: part3}, w_in, partial[...])
    hidden = total.astype(BF16)
    hidden_out[...] = hidden
    normed[...] = layer_norm(hidden.astype(F32)).astype(BF16)
    put_seg(send_1, seg[...])

    @pl.when(is_upward())
    def _():
        put_keys(normed, w_key, w_value, send_1)

    @pl.when(~is_upward())
    def _():
        put_query(normed, w_query, send_1)


def project_second_kernel(
    normed, send_1, w_key, w_value, w_query, seg, send_2, far_keys, far_query
):
    rows = normed.shape[0]
    group = w_query.shape[1]
    put_seg(send_2, seg[...])

    @pl.when(is_upward())
    def _():
        put_query(normed, w_query, send_2)
        far_query[...] = send_2[:rows, :group]
        far_keys[...] = send_1[:rows, :]

    @pl.when(~is_upward())
    def _():
        put_keys(normed, w_key, w_value, send_2)
        far_query[...] = send_1[:rows, :group]
        far_keys[...] = send_2[:rows, :]


def sort_first_kernel(got_1, got_b, got_c):
    @pl.when(is_upward())
    def _():
        got_b[...] = got_1[...]

    @pl.when(~is_upward())
    def _():
        got_c[...] = got_1[:, : got_c.shape[1]]


def sort_second_kernel(got_2, up_in, down_in, got_b, got_c):
    @pl.when(is_upward())
    def _():
        got_c[...] = got_2[:, : got_c.shape[1]]

    @pl.when(~is_upward())
    def _():
        got_b[...] = got_2[...]


def project_query_kernel(normed, w_near, seg, send_2, send_f):
    rows = normed.shape[0]
    send_f[:rows, :] = silu_dot(normed, w_near)
    put_seg(send_f, seg[...])


def attend_own(send_a, send_f, far_keys, far_query, seg, normed, w_near, w_far, mixed, gate):
    rows, group = mixed.shape[1:]
    seg_row = seg[0:1, :]
    allowed = (seg_column(seg_row) == seg_row) & (
        lax.broadcasted_iota(jnp.int32, (rows, rows), 1)
        <= lax.broadcasted_iota(jnp.int32, (rows, rows), 0)
    )
    for side, (query, key_value) in enumerate(((send_f, send_a), (far_query, far_keys))):
        for lo in range(0, group, HEAD_DIM):
            hi = lo + HEAD_DIM
            weights = head_weights(query[:rows, lo:hi], key_value[:rows, lo:hi], allowed)
            mixed[side, :, lo:hi] = jnp.dot(
                weights, key_value[:rows, group + lo : group + hi], preferred_element_type=F32
            )
    gate[0] = silu_dot(normed, w_near)
    gate[1] = silu_dot(normed, w_far)


def project_near_kernel(
    send_f, far_keys, far_query, seg, normed, w_near, w_far, w_key, w_value, send_a, mixed, gate
):
    put_keys(normed, w_key, w_value, send_a)
    put_seg(send_a, seg[...])

    @pl.when(~is_last())
    def _():
        attend_own(send_a, send_f, far_keys, far_query, seg, normed, w_near, w_far, mixed, gate)


def seg_row_of(ref, rows):
    return ref[rows : rows + SEG_ROWS, :rows].astype(F32)[0:1, :]


def add_blocks(query, key_values, out):
    group = query.shape[1]
    rows = query.shape[0] - SEG_ROWS
    column = seg_column(seg_row_of(query, rows))
    masks = [column == seg_row_of(ref, rows) for ref in key_values]
    for lo in range(0, group, HEAD_DIM):
        hi = lo + HEAD_DIM
        total = None
        for ref, allowed in zip(key_values, masks):
            weights = head_weights(query[:rows, lo:hi], ref[:rows, lo:hi], allowed)
            term = jnp.dot(
                weights, ref[:rows, group + lo : group + hi], preferred_element_type=F32
            )
            total = term if total is None else total + term
        out[:, lo:hi] = total.astype(out.dtype)


def add_near(query, column, key_value, mixed):
    rows, group = mixed.shape
    allowed = column == seg_row_of(key_value, rows)
    for lo in range(0, group, HEAD_DIM):
        hi = lo + HEAD_DIM
        weights = head_weights(query[:rows, lo:hi], key_value[:rows, lo:hi], allowed)
        mixed[:, lo:hi] += jnp.dot(
            weights, key_value[:rows, group + lo : group + hi], preferred_element_type=F32
        )


def early_kernel(got_b, got_c, send_a, early_1, early_2):
    @pl.when(batch_index() == 1)
    def _():
        add_blocks(got_c, [send_a, got_b], early_1)

    @pl.when(batch_index() == 2)
    def _():
        add_blocks(got_c, [send_a, got_b], early_2)


def far_kernel(got_b, got_c, got_f, send_a, early_1, send_e, send_g):
    @pl.when(batch_index() == 0)
    def _():
        add_blocks(got_c, [send_a], send_e)

    @pl.when(batch_index() == 1)
    def _():
        add_blocks(got_f, [send_a, got_b], send_e)
        send_g[...] = early_1[...]

    @pl.when(batch_index() > 1)
    def _():
        send_e[...] = jnp.zeros_like(send_e)

    @pl.when(batch_index() != 1)
    def _():
        send_g[...] = jnp.zeros_like(send_g)


def far_d_kernel(early_2, got_c, got_a, send_d, total):
    @pl.when(batch_index() == 2)
    def _():
        rows = total.shape[0]
        total[...] = early_2[...]
        add_near(got_c, seg_column(seg_row_of(got_c, rows)), got_a, total)
        send_d[...] = total[...].astype(BF16)

    @pl.when(batch_index() != 2)
    def _():
        send_d[...] = jnp.zeros_like(send_d)


def near_kernel(
    got_a, got_b, send_a, send_f, far_keys, far_query, seg, normed, w_near, w_far,
    mixed_in, gate_in, mixed, gate,
):
    column = seg_column(seg[0:1, :])

    @pl.when(is_last())
    def _():
        attend_own(send_a, send_f, far_keys, far_query, seg, normed, w_near, w_far, mixed, gate)

    @pl.when(batch_index() > 0)
    def _():
        add_near(send_f, column, got_b, mixed.at[0])

    @pl.when(batch_index() == 2)
    def _():
        add_near(send_f, column, got_a, mixed.at[0])


def finish_kernel(mixed, got_d, got_eg, gate, hidden, w_out, out):
    near = batch_index() % 2
    last = is_last()
    got = got_eg[...].astype(F32)
    group = mixed.shape[2]
    sides = (
        mixed[0] + jnp.where(last, got, 0.0),
        mixed[1] + got_d[...].astype(F32) + jnp.where(last, 0.0, got),
    )
    total = sum(jnp.sum(side, axis=-1, keepdims=True) for side in sides)
    sides = [side - total / (2 * group) for side in sides]
    total = sum(jnp.sum(side * side, axis=-1, keepdims=True) for side in sides)
    scale = lax.rsqrt(total / (2 * group) + eps_norm)
    branch = None
    for index, (which, side) in enumerate(zip((near, 1 - near), sides)):
        gated = (side * scale * gate[index].astype(F32)).astype(BF16)
        start = pl.multiple_of(which * group, group)
        term = jnp.dot(gated, w_out[pl.ds(start, group), :], preferred_element_type=F32)
        branch = term if branch is None else branch + term
    out[...] = (hidden[...].astype(F32) + branch.astype(BF16).astype(F32)).astype(BF16)


VMEM = pl.BlockSpec(memory_space=pltpu.VMEM)


def call(kernel, in_specs, outs, operands, flops, scratch=(), limit=32 << 20, aliases=()):
    return pl.pallas_call(
        kernel,
        out_shape=[jax.ShapeDtypeStruct(shape, dtype) for shape, dtype in outs],
        in_specs=in_specs,
        out_specs=[VMEM] * len(outs),
        scratch_shapes=list(scratch),
        input_output_aliases=dict(aliases),
        compiler_params=pltpu.CompilerParams(vmem_limit_bytes=limit),
        cost_estimate=pl.CostEstimate(flops=flops, bytes_accessed=0, transcendentals=0),
    )(*operands)


def chain_plan(lookups, input_weight, joined_weight, output_weight, owner_counts, user_index):
    cols = lax.axis_size("col")
    batch_at = lax.axis_index("batch").astype(jnp.int32)
    col_at = lax.axis_index("col").astype(jnp.int32)
    pieces = lookups.reshape(cols, lookups.shape[0] // cols, lookups.shape[1])
    rows = pieces.shape[1]

    def piece(source, shift):
        return lax.dynamic_index_in_dim(source, col_at ^ shift, 0, keepdims=False)

    def exchange(block, shift):
        return lax.ppermute(block, "col", [(i, i ^ shift) for i in range(cols)])

    across = piece(pieces, 2)
    pieces, across = lax.optimization_barrier((pieces, across))
    parts = [piece(pieces, 0)] + [
        exchange(across if shift == 2 else piece(pieces, shift), shift)
        for shift in range(1, cols)
    ]
    width = HEADS * HEAD_DIM
    group = width // 2
    features = input_weight.shape[1]
    tall = rows + SEG_ROWS
    (seg,) = call(
        segments_kernel,
        [VMEM] * 2,
        [((SEG_ROWS, rows), F32)],
        (owner_counts, user_index.reshape(1, rows)),
        1 << 30,
    )
    near = batch_at % 2
    far = 1 - near

    def weight_of(block, index):
        return lax.dynamic_slice_in_dim(joined_weight, block * width + index * group, group, 1)

    last = lax.axis_size("batch") - 1

    def up_and_down(block, parity):
        perm = []
        for at in range(cols):
            step = 1 if at % 2 == parity else -1
            for source in range(last + 1):
                inside = 0 <= source + step <= last
                target = (source + step, at) if inside else (source, at ^ 1)
                perm.append((source * cols + at, target[0] * cols + target[1]))
        return lax.ppermute(block, ("batch", "col"), perm)

    def closed(block, legs):
        perm = []
        for at in range(cols):
            for source in range(last + 1):
                target = (legs[source], at) if source in legs else (source, at ^ 1)
                perm.append((source * cols + at, target[0] * cols + target[1]))
        return lax.ppermute(block, ("batch", "col"), perm)

    far_weights = (weight_of(3, far), weight_of(1, far), weight_of(2, far))
    (partial,) = call(
        partial_kernel,
        [VMEM] * 4,
        [((rows, features), F32)],
        (parts[2], parts[1], parts[0], input_weight),
        rows,
    )
    hidden, normed, send_1 = call(
        project_first_kernel,
        [VMEM] * 7,
        [((rows, features), BF16), ((rows, features), BF16), ((tall, 2 * group), BF16)],
        (parts[3], partial, input_weight, *far_weights, seg),
        2 * rows * features * (features + 2 * group),
    )
    got_1 = up_and_down(send_1, 0)
    send_2, far_keys, far_query = call(
        project_second_kernel,
        [VMEM] * 6,
        [((tall, 2 * group), BF16), ((rows, 2 * group), BF16), ((rows, group), BF16)],
        (normed, send_1, *far_weights, seg),
        2 * rows * features * 2 * group,
    )
    got_2 = up_and_down(send_2, 1)
    (send_f,) = call(
        project_query_kernel,
        [VMEM] * 4,
        [((tall, group), BF16)],
        (normed, weight_of(2, near), seg, send_2),
        2 * rows * features * group,
    )
    got_f = lax.ppermute(send_f, "batch", [(3, 1)])
    own_inputs = (send_f, far_keys, far_query, seg, normed, weight_of(0, near), weight_of(0, far))
    own_outs = [((2, rows, group), F32), ((2, rows, group), BF16)]
    send_a, *own = call(
        project_near_kernel,
        [VMEM] * 9,
        [((tall, 2 * group), BF16)] + own_outs,
        (*own_inputs, weight_of(3, near), weight_of(1, near)),
        2 * rows * features * 2 * group,
    )
    got_a = lax.ppermute(send_a, "batch", [(0, 2)])
    sorted_outs = [((tall, 2 * group), BF16), ((tall, group), BF16)]
    got_b, got_c = call(sort_first_kernel, [VMEM], sorted_outs, (got_1,), 1 << 30)
    got_b, got_c = call(
        sort_second_kernel, [VMEM] * 3, sorted_outs, (got_2, got_b, got_c), rows,
        aliases={1: 0, 2: 1},
    )
    early_1, early_2 = call(
        early_kernel,
        [VMEM] * 3,
        [((rows, group), BF16), ((rows, group), F32)],
        (got_b, got_c, send_a),
        1 << 30,
    )
    send_e, send_g = call(
        far_kernel,
        [VMEM] * 5,
        [((rows, group), BF16)] * 2,
        (got_b, got_c, got_f, send_a, early_1),
        1 << 30,
    )
    got_e = lax.ppermute(send_e, "batch", [(1, 3), (0, 1)])
    got_g = closed(send_g, {1: 2, 2: 1})
    (send_d,) = call(
        far_d_kernel,
        [VMEM] * 3,
        [((rows, group), BF16)],
        (early_2, got_c, got_a),
        rows,
        [pltpu.VMEM((rows, group), F32)],
    )
    got_d = closed(send_d, {2: 3, 3: 2})
    mixed, gate = call(
        near_kernel,
        [VMEM] * 12,
        own_outs,
        (got_a, got_b, send_a, *own_inputs, *own),
        rows,
        aliases={10: 0, 11: 1},
    )
    (out,) = call(
        finish_kernel,
        [VMEM] * 6,
        [((rows, features), BF16)],
        (mixed, got_d, got_e + got_g, gate, hidden, output_weight),
        rows,
    )
    return out


def solution(mesh):
    chain = mesh.shape["batch"] == 4 and mesh.shape["col"] == 4
    return jax.shard_map(
        chain_plan if chain else owners_plan,
        mesh=mesh,
        in_specs=(
            P(("rep", "batch"), "col"),
            P(),
            P(),
            P(),
            P(("rep", "batch", "col"), None),
            P(("rep", "batch", "col")),
        ),
        out_specs=P(("rep", "batch", "col"), None),
        check_vma=False,
    )
```

```python
import jax
import jax.numpy as jnp
from jax import lax
from jax.experimental import pallas as pl
from jax.experimental.pallas import tpu as pltpu
from jax.sharding import PartitionSpec as P

HEADS = 4
HEAD_DIM = 128
SEG_ROWS = 8
OUT_PARTS = 2

eps_norm = 1e-06

F32 = jnp.float32
BF16 = jnp.bfloat16


def layer_norm(values):
    row_mean = jnp.mean(values, axis=-1, keepdims=True)
    centered = values - row_mean
    row_var = jnp.mean(centered * centered, axis=-1, keepdims=True)
    return centered * lax.rsqrt(row_var + eps_norm)


def project(hidden_rows, joined_weight):
    normed = layer_norm(hidden_rows.astype(F32)).astype(BF16)
    return jax.nn.silu(jnp.dot(normed, joined_weight, preferred_element_type=F32)).astype(BF16)


def attend(joined_rows, seg_ids):
    width = HEADS * HEAD_DIM
    total = joined_rows.shape[0]
    gate_part = joined_rows[:, :width]
    value_part = joined_rows[:, width : 2 * width].reshape(total, HEADS, HEAD_DIM)
    query_part = joined_rows[:, 2 * width : 3 * width].reshape(total, HEADS, HEAD_DIM)
    key_part = joined_rows[:, 3 * width :].reshape(total, HEADS, HEAD_DIM)
    scores = jnp.einsum(
        "ihd,jhd->hij", query_part, key_part, preferred_element_type=F32
    ) * HEAD_DIM ** (-0.5)
    positions = jnp.arange(total, dtype=jnp.int32)
    allowed = (positions[None, :] <= positions[:, None]) & (seg_ids[None, :] == seg_ids[:, None])
    weights = jnp.where(allowed[None], jax.nn.silu(scores), 0.0).astype(BF16)
    mixed = jnp.einsum(
        "hij,jhd->ihd", weights, value_part, preferred_element_type=F32
    ).reshape(total, width)
    return (layer_norm(mixed) * gate_part.astype(F32)).astype(BF16)


def owners_plan(lookups, input_weight, joined_weight, output_weight, owner_counts, user_index):
    token_block = lax.all_to_all(lookups, "col", split_axis=0, concat_axis=1, tiled=True)
    hidden = jnp.dot(token_block, input_weight, preferred_element_type=F32).astype(BF16)
    local_rows = hidden.shape[0]
    owners = lax.axis_size("batch")
    capacity = local_rows // owners + local_rows // (2 * owners)
    counts = owner_counts[0]
    bin_ends = jnp.cumsum(counts)
    bin_starts = bin_ends - counts
    slot_ids = jnp.arange(capacity, dtype=jnp.int32)
    filled = slot_ids[None, :] < counts[:, None]
    gather_rows = jnp.where(filled, bin_starts[:, None] + slot_ids[None, :], 0).reshape(-1)
    seg_send = jnp.where(filled.reshape(-1), user_index[gather_rows], -1).reshape(owners, capacity)
    payload = hidden[gather_rows].reshape(owners, capacity, -1)
    received, seg_ids = (
        lax.all_to_all(payload, "batch", split_axis=0, concat_axis=0, tiled=True),
        lax.all_to_all(seg_send, "batch", split_axis=0, concat_axis=0, tiled=True),
    )
    joined_rows = project(received.reshape(owners * capacity, -1), joined_weight)
    gated_rows = attend(joined_rows, seg_ids.reshape(-1))
    token_pos = jnp.arange(local_rows, dtype=jnp.int32)
    owner_ids = jnp.arange(owners, dtype=jnp.int32)
    dest_owner = jnp.sum((token_pos[:, None] >= bin_ends[None, :]).astype(jnp.int32), axis=1)
    onehot = dest_owner[:, None] == owner_ids[None, :]
    first_slot = jnp.sum(jnp.where(onehot, bin_starts[None, :], 0), axis=1)
    back_rows = dest_owner * capacity + token_pos - first_slot
    returned = lax.all_to_all(
        gated_rows.reshape(owners, capacity, -1), "batch", split_axis=0, concat_axis=0, tiled=True
    )
    own_gated = returned.reshape(owners * capacity, -1)[back_rows]
    branch_rows = jnp.dot(own_gated, output_weight, preferred_element_type=F32).astype(BF16)
    return (hidden.astype(F32) + branch_rows.astype(F32)).astype(BF16)


def batch_index():
    return lax.axis_index("batch")


def is_last():
    return lax.axis_index("batch") == lax.axis_size("batch") - 1


def silu_of(values):
    half = 0.5 * values
    return half + half * jnp.tanh(half)


def head_weights(query, key, allowed):
    scores = lax.dot_general(query, key, (((1,), (1,)), ((), ())), preferred_element_type=F32)
    half = scores * (0.5 * HEAD_DIM ** (-0.5))
    return jnp.where(allowed, half + half * jnp.tanh(half), 0.0).astype(BF16)


def seg_column(seg_row):
    wide = jnp.broadcast_to(seg_row, (128, seg_row.shape[1]))
    return wide.T[:, :1]


def segments_kernel(counts, users, seg_out):
    rows = users.shape[1]
    owners = counts.shape[1]
    position = lax.broadcasted_iota(jnp.int32, (1, rows), 1)
    end = counts[:, :1]
    owner = (position >= end).astype(jnp.int32)
    for d in range(1, owners - 1):
        end = end + counts[:, d : d + 1]
        owner = owner + (position >= end).astype(jnp.int32)
    seg_out[...] = jnp.broadcast_to((owner + owners * users[...]).astype(F32), seg_out.shape)


def put_seg(ref, seg):
    rows = seg.shape[1]
    for at in range(0, ref.shape[1], rows):
        ref[rows:, at : at + rows] = seg.astype(BF16)


def silu_dot(normed, weight):
    return silu_of(jnp.dot(normed[...], weight[...], preferred_element_type=F32)).astype(BF16)


def is_upward():
    return lax.axis_index("col") % 2 == 0


def put_keys(normed, w_key, w_value, out):
    rows = normed.shape[0]
    group = w_key.shape[1]
    out[:rows, :group] = silu_dot(normed, w_key)
    out[:rows, group : 2 * group] = silu_dot(normed, w_value)


def put_query(normed, w_query, out):
    rows = normed.shape[0]
    group = w_query.shape[1]
    out[:rows, :group] = silu_dot(normed, w_query)
    out[:rows, group:] = jnp.zeros((rows, group), BF16)


def add_pieces(pieces, w_in, total):
    for shift, piece in pieces.items():
        width = piece.shape[1]
        start = pl.multiple_of((lax.axis_index("col") ^ shift) * width, width)
        term = jnp.dot(piece[...], w_in[pl.ds(start, width), :], preferred_element_type=F32)
        total = term if total is None else total + term
    return total


def partial_kernel(part2, part1, own, w_in, partial):
    partial[...] = add_pieces({0: own, 1: part1, 2: part2}, w_in, None)


def project_first_kernel(
    part3, partial, w_in, w_key, w_value, w_query, seg, hidden_out, normed, send_1
):
    total = add_pieces({3: part3}, w_in, partial[...])
    hidden = total.astype(BF16)
    hidden_out[...] = hidden
    normed[...] = layer_norm(hidden.astype(F32)).astype(BF16)
    put_seg(send_1, seg[...])

    @pl.when(is_upward())
    def _():
        put_keys(normed, w_key, w_value, send_1)

    @pl.when(~is_upward())
    def _():
        put_query(normed, w_query, send_1)


def project_second_kernel(
    normed, send_1, w_key, w_value, w_query, seg, send_2, far_keys, far_query
):
    rows = normed.shape[0]
    group = w_query.shape[1]
    put_seg(send_2, seg[...])

    @pl.when(is_upward())
    def _():
        put_query(normed, w_query, send_2)
        far_query[...] = send_2[:rows, :group]
        far_keys[...] = send_1[:rows, :]

    @pl.when(~is_upward())
    def _():
        put_keys(normed, w_key, w_value, send_2)
        far_query[...] = send_1[:rows, :group]
        far_keys[...] = send_2[:rows, :]


def sort_first_kernel(got_1, got_b, got_c):
    @pl.when(is_upward())
    def _():
        got_b[...] = got_1[...]

    @pl.when(~is_upward())
    def _():
        got_c[...] = got_1[:, : got_c.shape[1]]


def sort_second_kernel(got_2, up_in, down_in, got_b, got_c):
    @pl.when(is_upward())
    def _():
        got_c[...] = got_2[:, : got_c.shape[1]]

    @pl.when(~is_upward())
    def _():
        got_b[...] = got_2[...]


def project_query_kernel(normed, w_near, seg, send_2, send_f):
    rows = normed.shape[0]
    send_f[:rows, :] = silu_dot(normed, w_near)
    put_seg(send_f, seg[...])


def attend_own(send_a, send_f, far_keys, far_query, seg, normed, w_near, w_far, mixed, gate):
    rows, group = mixed.shape[1:]
    seg_row = seg[0:1, :]
    allowed = (seg_column(seg_row) == seg_row) & (
        lax.broadcasted_iota(jnp.int32, (rows, rows), 1)
        <= lax.broadcasted_iota(jnp.int32, (rows, rows), 0)
    )
    for side, (query, key_value) in enumerate(((send_f, send_a), (far_query, far_keys))):
        for lo in range(0, group, HEAD_DIM):
            hi = lo + HEAD_DIM
            weights = head_weights(query[:rows, lo:hi], key_value[:rows, lo:hi], allowed)
            mixed[side, :, lo:hi] = jnp.dot(
                weights, key_value[:rows, group + lo : group + hi], preferred_element_type=F32
            )
    gate[0] = silu_dot(normed, w_near)
    gate[1] = silu_dot(normed, w_far)


def project_near_kernel(
    send_f, far_keys, far_query, seg, normed, w_near, w_far, w_key, w_value, send_a, mixed, gate
):
    put_keys(normed, w_key, w_value, send_a)
    put_seg(send_a, seg[...])

    @pl.when(~is_last())
    def _():
        attend_own(send_a, send_f, far_keys, far_query, seg, normed, w_near, w_far, mixed, gate)


def seg_row_of(ref, rows):
    return ref[rows : rows + SEG_ROWS, :rows].astype(F32)[0:1, :]


def add_blocks(query, key_values, out):
    group = query.shape[1]
    rows = query.shape[0] - SEG_ROWS
    column = seg_column(seg_row_of(query, rows))
    masks = [column == seg_row_of(ref, rows) for ref in key_values]
    for lo in range(0, group, HEAD_DIM):
        hi = lo + HEAD_DIM
        total = None
        for ref, allowed in zip(key_values, masks):
            weights = head_weights(query[:rows, lo:hi], ref[:rows, lo:hi], allowed)
            term = jnp.dot(
                weights, ref[:rows, group + lo : group + hi], preferred_element_type=F32
            )
            total = term if total is None else total + term
        out[:, lo:hi] = total.astype(out.dtype)


def add_near(query, column, key_value, mixed):
    rows, group = mixed.shape
    allowed = column == seg_row_of(key_value, rows)
    for lo in range(0, group, HEAD_DIM):
        hi = lo + HEAD_DIM
        weights = head_weights(query[:rows, lo:hi], key_value[:rows, lo:hi], allowed)
        mixed[:, lo:hi] += jnp.dot(
            weights, key_value[:rows, group + lo : group + hi], preferred_element_type=F32
        )


def early_kernel(got_b, got_c, send_a, early_1, early_2):
    @pl.when(batch_index() == 1)
    def _():
        add_blocks(got_c, [send_a, got_b], early_1)

    @pl.when(batch_index() == 2)
    def _():
        add_blocks(got_c, [send_a, got_b], early_2)


def far_kernel(got_b, got_c, got_f, send_a, early_1, send_e, send_g):
    @pl.when(batch_index() == 0)
    def _():
        add_blocks(got_c, [send_a], send_e)

    @pl.when(batch_index() == 1)
    def _():
        add_blocks(got_f, [send_a, got_b], send_e)
        send_g[...] = early_1[...]

    @pl.when(batch_index() > 1)
    def _():
        send_e[...] = jnp.zeros_like(send_e)

    @pl.when(batch_index() != 1)
    def _():
        send_g[...] = jnp.zeros_like(send_g)


def far_d_kernel(early_2, got_c, got_a, send_d, total):
    @pl.when(batch_index() == 2)
    def _():
        rows = total.shape[0]
        total[...] = early_2[...]
        add_near(got_c, seg_column(seg_row_of(got_c, rows)), got_a, total)
        send_d[...] = total[...].astype(BF16)

    @pl.when(batch_index() != 2)
    def _():
        send_d[...] = jnp.zeros_like(send_d)


def near_kernel(
    got_a, got_b, send_a, send_f, far_keys, far_query, seg, normed, w_near, w_far,
    mixed_in, gate_in, mixed, gate,
):
    column = seg_column(seg[0:1, :])

    @pl.when(is_last())
    def _():
        attend_own(send_a, send_f, far_keys, far_query, seg, normed, w_near, w_far, mixed, gate)

    @pl.when(batch_index() > 0)
    def _():
        add_near(send_f, column, got_b, mixed.at[0])

    @pl.when(batch_index() == 2)
    def _():
        add_near(send_f, column, got_a, mixed.at[0])


def finish_kernel(mixed, got_d, got_eg, gate, hidden, w_out, out, staged, sems):
    near = batch_index() % 2
    last = is_last()
    got = got_eg[...].astype(F32)
    group = mixed.shape[2]
    sides = (
        mixed[0] + jnp.where(last, got, 0.0),
        mixed[1] + got_d[...].astype(F32) + jnp.where(last, 0.0, got),
    )
    total = sum(jnp.sum(side, axis=-1, keepdims=True) for side in sides)
    sides = [side - total / (2 * group) for side in sides]
    total = sum(jnp.sum(side * side, axis=-1, keepdims=True) for side in sides)
    scale = lax.rsqrt(total / (2 * group) + eps_norm)
    gates = [(side * scale * gate[i].astype(F32)).astype(BF16) for i, side in enumerate(sides)]
    columns = hidden.shape[1] // OUT_PARTS
    copies = []
    for part in range(OUT_PARTS):
        at = slice(part * columns, (part + 1) * columns)
        branch = None
        for which, gated in zip((near, 1 - near), gates):
            start = pl.multiple_of(which * group, group)
            term = jnp.dot(gated, w_out[pl.ds(start, group), at], preferred_element_type=F32)
            branch = term if branch is None else branch + term
        total = hidden[:, at].astype(F32) + branch.astype(BF16).astype(F32)
        staged[:, at] = total.astype(BF16)
        copies.append(pltpu.make_async_copy(staged.at[:, at], out.at[:, at], sems.at[part]))
        copies[-1].start()
    for copy in copies:
        copy.wait()


VMEM = pl.BlockSpec(memory_space=pltpu.VMEM)


def call(kernel, in_specs, outs, operands, flops, scratch=(), limit=32 << 20, aliases=()):
    return pl.pallas_call(
        kernel,
        out_shape=[jax.ShapeDtypeStruct(shape, dtype) for shape, dtype in outs],
        in_specs=in_specs,
        out_specs=[VMEM] * len(outs),
        scratch_shapes=list(scratch),
        input_output_aliases=dict(aliases),
        compiler_params=pltpu.CompilerParams(vmem_limit_bytes=limit),
        cost_estimate=pl.CostEstimate(flops=flops, bytes_accessed=0, transcendentals=0),
    )(*operands)


def chain_plan(lookups, input_weight, joined_weight, output_weight, owner_counts, user_index):
    cols = lax.axis_size("col")
    batch_at = lax.axis_index("batch").astype(jnp.int32)
    col_at = lax.axis_index("col").astype(jnp.int32)
    pieces = lookups.reshape(cols, lookups.shape[0] // cols, lookups.shape[1])
    rows = pieces.shape[1]

    def piece(source, shift):
        return lax.dynamic_index_in_dim(source, col_at ^ shift, 0, keepdims=False)

    def exchange(block, shift):
        return lax.ppermute(block, "col", [(i, i ^ shift) for i in range(cols)])

    across = piece(pieces, 2)
    pieces, across = lax.optimization_barrier((pieces, across))
    parts = [piece(pieces, 0)] + [
        exchange(across if shift == 2 else piece(pieces, shift), shift)
        for shift in range(1, cols)
    ]
    width = HEADS * HEAD_DIM
    group = width // 2
    features = input_weight.shape[1]
    tall = rows + SEG_ROWS
    (seg,) = call(
        segments_kernel,
        [VMEM] * 2,
        [((SEG_ROWS, rows), F32)],
        (owner_counts, user_index.reshape(1, rows)),
        1 << 30,
    )
    near = batch_at % 2
    far = 1 - near

    def weight_of(block, index):
        return lax.dynamic_slice_in_dim(joined_weight, block * width + index * group, group, 1)

    last = lax.axis_size("batch") - 1

    def up_and_down(block, parity):
        perm = []
        for at in range(cols):
            step = 1 if at % 2 == parity else -1
            for source in range(last + 1):
                inside = 0 <= source + step <= last
                target = (source + step, at) if inside else (source, at ^ 1)
                perm.append((source * cols + at, target[0] * cols + target[1]))
        return lax.ppermute(block, ("batch", "col"), perm)

    def closed(block, legs):
        perm = []
        for at in range(cols):
            for source in range(last + 1):
                target = (legs[source], at) if source in legs else (source, at ^ 1)
                perm.append((source * cols + at, target[0] * cols + target[1]))
        return lax.ppermute(block, ("batch", "col"), perm)

    far_weights = (weight_of(3, far), weight_of(1, far), weight_of(2, far))
    (partial,) = call(
        partial_kernel,
        [VMEM] * 4,
        [((rows, features), F32)],
        (parts[2], parts[1], parts[0], input_weight),
        rows,
    )
    hidden, normed, send_1 = call(
        project_first_kernel,
        [VMEM] * 7,
        [((rows, features), BF16), ((rows, features), BF16), ((tall, 2 * group), BF16)],
        (parts[3], partial, input_weight, *far_weights, seg),
        2 * rows * features * (features + 2 * group),
    )
    got_1 = up_and_down(send_1, 0)
    send_2, far_keys, far_query = call(
        project_second_kernel,
        [VMEM] * 6,
        [((tall, 2 * group), BF16), ((rows, 2 * group), BF16), ((rows, group), BF16)],
        (normed, send_1, *far_weights, seg),
        2 * rows * features * 2 * group,
    )
    got_2 = up_and_down(send_2, 1)
    (send_f,) = call(
        project_query_kernel,
        [VMEM] * 4,
        [((tall, group), BF16)],
        (normed, weight_of(2, near), seg, send_2),
        2 * rows * features * group,
    )
    got_f = lax.ppermute(send_f, "batch", [(3, 1)])
    own_inputs = (send_f, far_keys, far_query, seg, normed, weight_of(0, near), weight_of(0, far))
    own_outs = [((2, rows, group), F32), ((2, rows, group), BF16)]
    send_a, *own = call(
        project_near_kernel,
        [VMEM] * 9,
        [((tall, 2 * group), BF16)] + own_outs,
        (*own_inputs, weight_of(3, near), weight_of(1, near)),
        2 * rows * features * 2 * group,
    )
    got_a = lax.ppermute(send_a, "batch", [(0, 2)])
    sorted_outs = [((tall, 2 * group), BF16), ((tall, group), BF16)]
    got_b, got_c = call(sort_first_kernel, [VMEM], sorted_outs, (got_1,), 1 << 30)
    got_b, got_c = call(
        sort_second_kernel, [VMEM] * 3, sorted_outs, (got_2, got_b, got_c), rows,
        aliases={1: 0, 2: 1},
    )
    early_1, early_2 = call(
        early_kernel,
        [VMEM] * 3,
        [((rows, group), BF16), ((rows, group), F32)],
        (got_b, got_c, send_a),
        1 << 30,
    )
    send_e, send_g = call(
        far_kernel,
        [VMEM] * 5,
        [((rows, group), BF16)] * 2,
        (got_b, got_c, got_f, send_a, early_1),
        1 << 30,
    )
    got_e = lax.ppermute(send_e, "batch", [(1, 3), (0, 1)])
    got_g = closed(send_g, {1: 2, 2: 1})
    (send_d,) = call(
        far_d_kernel,
        [VMEM] * 3,
        [((rows, group), BF16)],
        (early_2, got_c, got_a),
        rows,
        [pltpu.VMEM((rows, group), F32)],
    )
    got_d = closed(send_d, {2: 3, 3: 2})
    mixed, gate = call(
        near_kernel,
        [VMEM] * 12,
        own_outs,
        (got_a, got_b, send_a, *own_inputs, *own),
        rows,
        aliases={10: 0, 11: 1},
    )
    return pl.pallas_call(
        finish_kernel,
        out_shape=jax.ShapeDtypeStruct((rows, features), BF16),
        in_specs=[VMEM] * 6,
        out_specs=pl.BlockSpec(memory_space=pl.ANY),
        scratch_shapes=[
            pltpu.VMEM((rows, features), BF16),
            pltpu.SemaphoreType.DMA((OUT_PARTS,)),
        ],
        compiler_params=pltpu.CompilerParams(vmem_limit_bytes=32 << 20),
        cost_estimate=pl.CostEstimate(flops=rows, bytes_accessed=0, transcendentals=0),
    )(mixed, got_d, got_e + got_g, gate, hidden, output_weight)


def solution(mesh):
    chain = mesh.shape["batch"] == 4 and mesh.shape["col"] == 4
    return jax.shard_map(
        chain_plan if chain else owners_plan,
        mesh=mesh,
        in_specs=(
            P(("rep", "batch"), "col"),
            P(),
            P(),
            P(),
            P(("rep", "batch", "col"), None),
            P(("rep", "batch", "col")),
        ),
        out_specs=P(("rep", "batch", "col"), None),
        check_vma=False,
    )
```

```python
import jax
import jax.numpy as jnp
from jax import lax
from jax.experimental import pallas as pl
from jax.experimental.pallas import tpu as pltpu
from jax.sharding import PartitionSpec as P

HEADS = 4
HEAD_DIM = 128
SEG_ROWS = 8
OUT_PARTS = 2

eps_norm = 1e-06

F32 = jnp.float32
BF16 = jnp.bfloat16


def layer_norm(values):
    row_mean = jnp.mean(values, axis=-1, keepdims=True)
    centered = values - row_mean
    row_var = jnp.mean(centered * centered, axis=-1, keepdims=True)
    return centered * lax.rsqrt(row_var + eps_norm)


def project(hidden_rows, joined_weight):
    normed = layer_norm(hidden_rows.astype(F32)).astype(BF16)
    return jax.nn.silu(jnp.dot(normed, joined_weight, preferred_element_type=F32)).astype(BF16)


def attend(joined_rows, seg_ids):
    width = HEADS * HEAD_DIM
    total = joined_rows.shape[0]
    gate_part = joined_rows[:, :width]
    value_part = joined_rows[:, width : 2 * width].reshape(total, HEADS, HEAD_DIM)
    query_part = joined_rows[:, 2 * width : 3 * width].reshape(total, HEADS, HEAD_DIM)
    key_part = joined_rows[:, 3 * width :].reshape(total, HEADS, HEAD_DIM)
    scores = jnp.einsum(
        "ihd,jhd->hij", query_part, key_part, preferred_element_type=F32
    ) * HEAD_DIM ** (-0.5)
    positions = jnp.arange(total, dtype=jnp.int32)
    allowed = (positions[None, :] <= positions[:, None]) & (seg_ids[None, :] == seg_ids[:, None])
    weights = jnp.where(allowed[None], jax.nn.silu(scores), 0.0).astype(BF16)
    mixed = jnp.einsum(
        "hij,jhd->ihd", weights, value_part, preferred_element_type=F32
    ).reshape(total, width)
    return (layer_norm(mixed) * gate_part.astype(F32)).astype(BF16)


def owners_plan(lookups, input_weight, joined_weight, output_weight, owner_counts, user_index):
    token_block = lax.all_to_all(lookups, "col", split_axis=0, concat_axis=1, tiled=True)
    hidden = jnp.dot(token_block, input_weight, preferred_element_type=F32).astype(BF16)
    local_rows = hidden.shape[0]
    owners = lax.axis_size("batch")
    capacity = local_rows // owners + local_rows // (2 * owners)
    counts = owner_counts[0]
    bin_ends = jnp.cumsum(counts)
    bin_starts = bin_ends - counts
    slot_ids = jnp.arange(capacity, dtype=jnp.int32)
    filled = slot_ids[None, :] < counts[:, None]
    gather_rows = jnp.where(filled, bin_starts[:, None] + slot_ids[None, :], 0).reshape(-1)
    seg_send = jnp.where(filled.reshape(-1), user_index[gather_rows], -1).reshape(owners, capacity)
    payload = hidden[gather_rows].reshape(owners, capacity, -1)
    received, seg_ids = (
        lax.all_to_all(payload, "batch", split_axis=0, concat_axis=0, tiled=True),
        lax.all_to_all(seg_send, "batch", split_axis=0, concat_axis=0, tiled=True),
    )
    joined_rows = project(received.reshape(owners * capacity, -1), joined_weight)
    gated_rows = attend(joined_rows, seg_ids.reshape(-1))
    token_pos = jnp.arange(local_rows, dtype=jnp.int32)
    owner_ids = jnp.arange(owners, dtype=jnp.int32)
    dest_owner = jnp.sum((token_pos[:, None] >= bin_ends[None, :]).astype(jnp.int32), axis=1)
    onehot = dest_owner[:, None] == owner_ids[None, :]
    first_slot = jnp.sum(jnp.where(onehot, bin_starts[None, :], 0), axis=1)
    back_rows = dest_owner * capacity + token_pos - first_slot
    returned = lax.all_to_all(
        gated_rows.reshape(owners, capacity, -1), "batch", split_axis=0, concat_axis=0, tiled=True
    )
    own_gated = returned.reshape(owners * capacity, -1)[back_rows]
    branch_rows = jnp.dot(own_gated, output_weight, preferred_element_type=F32).astype(BF16)
    return (hidden.astype(F32) + branch_rows.astype(F32)).astype(BF16)


def batch_index():
    return lax.axis_index("batch")


def is_last():
    return lax.axis_index("batch") == lax.axis_size("batch") - 1


def silu_of(values):
    half = 0.5 * values
    return half + half * jnp.tanh(half)


def head_weights(query, key, allowed):
    scores = lax.dot_general(query, key, (((1,), (1,)), ((), ())), preferred_element_type=F32)
    half = scores * (0.5 * HEAD_DIM ** (-0.5))
    return jnp.where(allowed, half + half * jnp.tanh(half), 0.0).astype(BF16)


def seg_column(seg_row):
    wide = jnp.broadcast_to(seg_row, (128, seg_row.shape[1]))
    return wide.T[:, :1]


def segments_kernel(counts, users, seg_out):
    rows = users.shape[1]
    owners = counts.shape[1]
    position = lax.broadcasted_iota(jnp.int32, (1, rows), 1)
    end = counts[:, :1]
    owner = (position >= end).astype(jnp.int32)
    for d in range(1, owners - 1):
        end = end + counts[:, d : d + 1]
        owner = owner + (position >= end).astype(jnp.int32)
    seg_out[...] = jnp.broadcast_to((owner + owners * users[...]).astype(F32), seg_out.shape)


def put_seg(ref, seg):
    rows = seg.shape[1]
    for at in range(0, ref.shape[1], rows):
        ref[rows:, at : at + rows] = seg.astype(BF16)


def silu_dot(normed, weight):
    return silu_of(jnp.dot(normed[...], weight[...], preferred_element_type=F32)).astype(BF16)


def is_upward():
    return lax.axis_index("col") % 2 == 0


def put_keys(normed, w_key, w_value, out):
    rows = normed.shape[0]
    group = w_key.shape[1]
    out[:rows, :group] = silu_dot(normed, w_key)
    out[:rows, group : 2 * group] = silu_dot(normed, w_value)


def put_query(normed, w_query, out):
    rows = normed.shape[0]
    group = w_query.shape[1]
    out[:rows, :group] = silu_dot(normed, w_query)
    out[:rows, group:] = jnp.zeros((rows, group), BF16)


def add_pieces(pieces, w_in, total):
    for shift, piece in pieces.items():
        width = piece.shape[1]
        start = pl.multiple_of((lax.axis_index("col") ^ shift) * width, width)
        term = jnp.dot(piece[...], w_in[pl.ds(start, width), :], preferred_element_type=F32)
        total = term if total is None else total + term
    return total


def partial_kernel(part2, part1, own, w_in, partial):
    partial[...] = add_pieces({0: own, 1: part1, 2: part2}, w_in, None)


def project_first_kernel(
    part3, partial, w_in, w_key, w_value, w_query, seg, hidden_out, normed, send_1
):
    total = add_pieces({3: part3}, w_in, partial[...])
    hidden = total.astype(BF16)
    hidden_out[...] = hidden
    normed[...] = layer_norm(hidden.astype(F32)).astype(BF16)
    put_seg(send_1, seg[...])

    @pl.when(is_upward())
    def _():
        put_keys(normed, w_key, w_value, send_1)

    @pl.when(~is_upward())
    def _():
        put_query(normed, w_query, send_1)


def project_second_kernel(
    normed, send_1, w_key, w_value, w_query, seg, send_2, far_keys, far_query
):
    rows = normed.shape[0]
    group = w_query.shape[1]
    put_seg(send_2, seg[...])

    @pl.when(is_upward())
    def _():
        put_query(normed, w_query, send_2)
        far_query[...] = send_2[:rows, :group]
        far_keys[...] = send_1[:rows, :]

    @pl.when(~is_upward())
    def _():
        put_keys(normed, w_key, w_value, send_2)
        far_query[...] = send_1[:rows, :group]
        far_keys[...] = send_2[:rows, :]


def sort_first_kernel(got_1, got_b, got_c):
    @pl.when(is_upward())
    def _():
        got_b[...] = got_1[...]

    @pl.when(~is_upward())
    def _():
        got_c[...] = got_1[:, : got_c.shape[1]]


def sort_second_kernel(got_2, up_in, down_in, got_b, got_c):
    @pl.when(is_upward())
    def _():
        got_c[...] = got_2[:, : got_c.shape[1]]

    @pl.when(~is_upward())
    def _():
        got_b[...] = got_2[...]


def project_query_kernel(normed, w_near, seg, send_2, send_f):
    rows = normed.shape[0]
    send_f[:rows, :] = silu_dot(normed, w_near)
    put_seg(send_f, seg[...])


def attend_own(send_a, send_f, far_keys, far_query, seg, normed, w_near, w_far, mixed, gate):
    rows, group = mixed.shape[1:]
    seg_row = seg[0:1, :]
    allowed = (seg_column(seg_row) == seg_row) & (
        lax.broadcasted_iota(jnp.int32, (rows, rows), 1)
        <= lax.broadcasted_iota(jnp.int32, (rows, rows), 0)
    )
    for side, (query, key_value) in enumerate(((send_f, send_a), (far_query, far_keys))):
        for lo in range(0, group, HEAD_DIM):
            hi = lo + HEAD_DIM
            weights = head_weights(query[:rows, lo:hi], key_value[:rows, lo:hi], allowed)
            mixed[side, :, lo:hi] = jnp.dot(
                weights, key_value[:rows, group + lo : group + hi], preferred_element_type=F32
            )


def project_near_kernel(
    send_f, far_keys, far_query, seg, normed, w_near, w_far, w_key, w_value, send_a, mixed, gate
):
    put_keys(normed, w_key, w_value, send_a)
    put_seg(send_a, seg[...])

    @pl.when(~is_last())
    def _():
        attend_own(send_a, send_f, far_keys, far_query, seg, normed, w_near, w_far, mixed, gate)


def seg_row_of(ref, rows):
    return ref[rows : rows + SEG_ROWS, :rows].astype(F32)[0:1, :]


def add_blocks(query, key_values, out):
    group = query.shape[1]
    rows = query.shape[0] - SEG_ROWS
    column = seg_column(seg_row_of(query, rows))
    masks = [column == seg_row_of(ref, rows) for ref in key_values]
    for lo in range(0, group, HEAD_DIM):
        hi = lo + HEAD_DIM
        total = None
        for ref, allowed in zip(key_values, masks):
            weights = head_weights(query[:rows, lo:hi], ref[:rows, lo:hi], allowed)
            term = jnp.dot(
                weights, ref[:rows, group + lo : group + hi], preferred_element_type=F32
            )
            total = term if total is None else total + term
        out[:, lo:hi] = total.astype(out.dtype)


def add_near(query, column, key_value, mixed):
    rows, group = mixed.shape
    allowed = column == seg_row_of(key_value, rows)
    for lo in range(0, group, HEAD_DIM):
        hi = lo + HEAD_DIM
        weights = head_weights(query[:rows, lo:hi], key_value[:rows, lo:hi], allowed)
        mixed[:, lo:hi] += jnp.dot(
            weights, key_value[:rows, group + lo : group + hi], preferred_element_type=F32
        )


def early_kernel(got_b, got_c, send_a, early_1, early_2):
    @pl.when(batch_index() == 1)
    def _():
        add_blocks(got_c, [send_a, got_b], early_1)

    @pl.when(batch_index() == 2)
    def _():
        add_blocks(got_c, [send_a, got_b], early_2)


def far_kernel(got_b, got_c, got_f, send_a, early_1, send_e, send_g):
    @pl.when(batch_index() == 0)
    def _():
        add_blocks(got_c, [send_a], send_e)

    @pl.when(batch_index() == 1)
    def _():
        add_blocks(got_f, [send_a, got_b], send_e)
        send_g[...] = early_1[...]

    @pl.when(batch_index() > 1)
    def _():
        send_e[...] = jnp.zeros_like(send_e)

    @pl.when(batch_index() != 1)
    def _():
        send_g[...] = jnp.zeros_like(send_g)


def far_d_kernel(early_2, got_c, got_a, send_d, total):
    @pl.when(batch_index() == 2)
    def _():
        rows = total.shape[0]
        total[...] = early_2[...]
        add_near(got_c, seg_column(seg_row_of(got_c, rows)), got_a, total)
        send_d[...] = total[...].astype(BF16)

    @pl.when(batch_index() != 2)
    def _():
        send_d[...] = jnp.zeros_like(send_d)


def near_kernel(
    got_a, got_b, send_a, send_f, far_keys, far_query, seg, normed, w_near, w_far,
    mixed_in, gate_in, mixed, gate,
):
    column = seg_column(seg[0:1, :])
    gate[0] = silu_dot(normed, w_near)
    gate[1] = silu_dot(normed, w_far)

    @pl.when(is_last())
    def _():
        attend_own(send_a, send_f, far_keys, far_query, seg, normed, w_near, w_far, mixed, gate)

    @pl.when(batch_index() > 0)
    def _():
        add_near(send_f, column, got_b, mixed.at[0])

    @pl.when(batch_index() == 2)
    def _():
        add_near(send_f, column, got_a, mixed.at[0])


def finish_kernel(mixed, got_d, got_eg, gate, hidden, w_out, out, staged, sems):
    near = batch_index() % 2
    last = is_last()
    got = got_eg[...].astype(F32)
    group = mixed.shape[2]
    sides = (
        mixed[0] + jnp.where(last, got, 0.0),
        mixed[1] + got_d[...].astype(F32) + jnp.where(last, 0.0, got),
    )
    total = sum(jnp.sum(side, axis=-1, keepdims=True) for side in sides)
    sides = [side - total / (2 * group) for side in sides]
    total = sum(jnp.sum(side * side, axis=-1, keepdims=True) for side in sides)
    scale = lax.rsqrt(total / (2 * group) + eps_norm)
    gates = [(side * scale * gate[i].astype(F32)).astype(BF16) for i, side in enumerate(sides)]
    columns = hidden.shape[1] // OUT_PARTS
    copies = []
    for part in range(OUT_PARTS):
        at = slice(part * columns, (part + 1) * columns)
        branch = None
        for which, gated in zip((near, 1 - near), gates):
            start = pl.multiple_of(which * group, group)
            term = jnp.dot(gated, w_out[pl.ds(start, group), at], preferred_element_type=F32)
            branch = term if branch is None else branch + term
        total = hidden[:, at].astype(F32) + branch.astype(BF16).astype(F32)
        staged[:, at] = total.astype(BF16)
        copies.append(pltpu.make_async_copy(staged.at[:, at], out.at[:, at], sems.at[part]))
        copies[-1].start()
    for copy in copies:
        copy.wait()


VMEM = pl.BlockSpec(memory_space=pltpu.VMEM)


def call(kernel, in_specs, outs, operands, flops, scratch=(), limit=32 << 20, aliases=()):
    return pl.pallas_call(
        kernel,
        out_shape=[jax.ShapeDtypeStruct(shape, dtype) for shape, dtype in outs],
        in_specs=in_specs,
        out_specs=[VMEM] * len(outs),
        scratch_shapes=list(scratch),
        input_output_aliases=dict(aliases),
        compiler_params=pltpu.CompilerParams(vmem_limit_bytes=limit),
        cost_estimate=pl.CostEstimate(flops=flops, bytes_accessed=0, transcendentals=0),
    )(*operands)


def chain_plan(lookups, input_weight, joined_weight, output_weight, owner_counts, user_index):
    cols = lax.axis_size("col")
    batch_at = lax.axis_index("batch").astype(jnp.int32)
    col_at = lax.axis_index("col").astype(jnp.int32)
    pieces = lookups.reshape(cols, lookups.shape[0] // cols, lookups.shape[1])
    rows = pieces.shape[1]

    def piece(source, shift):
        return lax.dynamic_index_in_dim(source, col_at ^ shift, 0, keepdims=False)

    def exchange(block, shift):
        return lax.ppermute(block, "col", [(i, i ^ shift) for i in range(cols)])

    across = piece(pieces, 2)
    pieces, across = lax.optimization_barrier((pieces, across))
    parts = [piece(pieces, 0)] + [
        exchange(across if shift == 2 else piece(pieces, shift), shift)
        for shift in range(1, cols)
    ]
    width = HEADS * HEAD_DIM
    group = width // 2
    features = input_weight.shape[1]
    tall = rows + SEG_ROWS
    (seg,) = call(
        segments_kernel,
        [VMEM] * 2,
        [((SEG_ROWS, rows), F32)],
        (owner_counts, user_index.reshape(1, rows)),
        1 << 30,
    )
    near = batch_at % 2
    far = 1 - near

    def weight_of(block, index):
        return lax.dynamic_slice_in_dim(joined_weight, block * width + index * group, group, 1)

    last = lax.axis_size("batch") - 1

    def up_and_down(block, parity):
        perm = []
        for at in range(cols):
            step = 1 if at % 2 == parity else -1
            for source in range(last + 1):
                inside = 0 <= source + step <= last
                target = (source + step, at) if inside else (source, at ^ 1)
                perm.append((source * cols + at, target[0] * cols + target[1]))
        return lax.ppermute(block, ("batch", "col"), perm)

    def closed(block, legs):
        perm = []
        for at in range(cols):
            for source in range(last + 1):
                target = (legs[source], at) if source in legs else (source, at ^ 1)
                perm.append((source * cols + at, target[0] * cols + target[1]))
        return lax.ppermute(block, ("batch", "col"), perm)

    far_weights = (weight_of(3, far), weight_of(1, far), weight_of(2, far))
    (partial,) = call(
        partial_kernel,
        [VMEM] * 4,
        [((rows, features), F32)],
        (parts[2], parts[1], parts[0], input_weight),
        rows,
    )
    hidden, normed, send_1 = call(
        project_first_kernel,
        [VMEM] * 7,
        [((rows, features), BF16), ((rows, features), BF16), ((tall, 2 * group), BF16)],
        (parts[3], partial, input_weight, *far_weights, seg),
        2 * rows * features * (features + 2 * group),
    )
    got_1 = up_and_down(send_1, 0)
    send_2, far_keys, far_query = call(
        project_second_kernel,
        [VMEM] * 6,
        [((tall, 2 * group), BF16), ((rows, 2 * group), BF16), ((rows, group), BF16)],
        (normed, send_1, *far_weights, seg),
        2 * rows * features * 2 * group,
    )
    got_2 = up_and_down(send_2, 1)
    (send_f,) = call(
        project_query_kernel,
        [VMEM] * 4,
        [((tall, group), BF16)],
        (normed, weight_of(2, near), seg, send_2),
        2 * rows * features * group,
    )
    got_f = lax.ppermute(send_f, "batch", [(3, 1)])
    own_inputs = (send_f, far_keys, far_query, seg, normed, weight_of(0, near), weight_of(0, far))
    own_outs = [((2, rows, group), F32), ((2, rows, group), BF16)]
    send_a, *own = call(
        project_near_kernel,
        [VMEM] * 9,
        [((tall, 2 * group), BF16)] + own_outs,
        (*own_inputs, weight_of(3, near), weight_of(1, near)),
        2 * rows * features * 2 * group,
    )
    got_a = lax.ppermute(send_a, "batch", [(0, 2)])
    sorted_outs = [((tall, 2 * group), BF16), ((tall, group), BF16)]
    got_b, got_c = call(sort_first_kernel, [VMEM], sorted_outs, (got_1,), 1 << 30)
    got_b, got_c = call(
        sort_second_kernel, [VMEM] * 3, sorted_outs, (got_2, got_b, got_c), rows,
        aliases={1: 0, 2: 1},
    )
    early_1, early_2 = call(
        early_kernel,
        [VMEM] * 3,
        [((rows, group), BF16), ((rows, group), F32)],
        (got_b, got_c, send_a),
        1 << 30,
    )
    send_e, send_g = call(
        far_kernel,
        [VMEM] * 5,
        [((rows, group), BF16)] * 2,
        (got_b, got_c, got_f, send_a, early_1),
        1 << 30,
    )
    got_e = lax.ppermute(send_e, "batch", [(1, 3), (0, 1)])
    got_g = closed(send_g, {1: 2, 2: 1})
    (send_d,) = call(
        far_d_kernel,
        [VMEM] * 3,
        [((rows, group), BF16)],
        (early_2, got_c, got_a),
        rows,
        [pltpu.VMEM((rows, group), F32)],
    )
    got_d = closed(send_d, {2: 3, 3: 2})
    mixed, gate = call(
        near_kernel,
        [VMEM] * 12,
        own_outs,
        (got_a, got_b, send_a, *own_inputs, *own),
        rows,
        aliases={10: 0, 11: 1},
    )
    return pl.pallas_call(
        finish_kernel,
        out_shape=jax.ShapeDtypeStruct((rows, features), BF16),
        in_specs=[VMEM] * 6,
        out_specs=pl.BlockSpec(memory_space=pl.ANY),
        scratch_shapes=[
            pltpu.VMEM((rows, features), BF16),
            pltpu.SemaphoreType.DMA((OUT_PARTS,)),
        ],
        compiler_params=pltpu.CompilerParams(vmem_limit_bytes=32 << 20),
        cost_estimate=pl.CostEstimate(flops=rows, bytes_accessed=0, transcendentals=0),
    )(mixed, got_d, got_e + got_g, gate, hidden, output_weight)


def solution(mesh):
    chain = mesh.shape["batch"] == 4 and mesh.shape["col"] == 4
    return jax.shard_map(
        chain_plan if chain else owners_plan,
        mesh=mesh,
        in_specs=(
            P(("rep", "batch"), "col"),
            P(),
            P(),
            P(),
            P(("rep", "batch", "col"), None),
            P(("rep", "batch", "col")),
        ),
        out_specs=P(("rep", "batch", "col"), None),
        check_vma=False,
    )
```

```python
import jax
import jax.numpy as jnp
from jax import lax
from jax.experimental import pallas as pl
from jax.experimental.pallas import tpu as pltpu
from jax.sharding import PartitionSpec as P

HEADS = 4
HEAD_DIM = 128
SEG_ROWS = 8
OUT_PARTS = 2

eps_norm = 1e-06

F32 = jnp.float32
BF16 = jnp.bfloat16


def layer_norm(values):
    row_mean = jnp.mean(values, axis=-1, keepdims=True)
    centered = values - row_mean
    row_var = jnp.mean(centered * centered, axis=-1, keepdims=True)
    return centered * lax.rsqrt(row_var + eps_norm)


def project(hidden_rows, joined_weight):
    normed = layer_norm(hidden_rows.astype(F32)).astype(BF16)
    return jax.nn.silu(jnp.dot(normed, joined_weight, preferred_element_type=F32)).astype(BF16)


def attend(joined_rows, seg_ids):
    width = HEADS * HEAD_DIM
    total = joined_rows.shape[0]
    gate_part = joined_rows[:, :width]
    value_part = joined_rows[:, width : 2 * width].reshape(total, HEADS, HEAD_DIM)
    query_part = joined_rows[:, 2 * width : 3 * width].reshape(total, HEADS, HEAD_DIM)
    key_part = joined_rows[:, 3 * width :].reshape(total, HEADS, HEAD_DIM)
    scores = jnp.einsum(
        "ihd,jhd->hij", query_part, key_part, preferred_element_type=F32
    ) * HEAD_DIM ** (-0.5)
    positions = jnp.arange(total, dtype=jnp.int32)
    allowed = (positions[None, :] <= positions[:, None]) & (seg_ids[None, :] == seg_ids[:, None])
    weights = jnp.where(allowed[None], jax.nn.silu(scores), 0.0).astype(BF16)
    mixed = jnp.einsum(
        "hij,jhd->ihd", weights, value_part, preferred_element_type=F32
    ).reshape(total, width)
    return (layer_norm(mixed) * gate_part.astype(F32)).astype(BF16)


def owners_plan(lookups, input_weight, joined_weight, output_weight, owner_counts, user_index):
    token_block = lax.all_to_all(lookups, "col", split_axis=0, concat_axis=1, tiled=True)
    hidden = jnp.dot(token_block, input_weight, preferred_element_type=F32).astype(BF16)
    local_rows = hidden.shape[0]
    owners = lax.axis_size("batch")
    capacity = local_rows // owners + local_rows // (2 * owners)
    counts = owner_counts[0]
    bin_ends = jnp.cumsum(counts)
    bin_starts = bin_ends - counts
    slot_ids = jnp.arange(capacity, dtype=jnp.int32)
    filled = slot_ids[None, :] < counts[:, None]
    gather_rows = jnp.where(filled, bin_starts[:, None] + slot_ids[None, :], 0).reshape(-1)
    seg_send = jnp.where(filled.reshape(-1), user_index[gather_rows], -1).reshape(owners, capacity)
    payload = hidden[gather_rows].reshape(owners, capacity, -1)
    received, seg_ids = (
        lax.all_to_all(payload, "batch", split_axis=0, concat_axis=0, tiled=True),
        lax.all_to_all(seg_send, "batch", split_axis=0, concat_axis=0, tiled=True),
    )
    joined_rows = project(received.reshape(owners * capacity, -1), joined_weight)
    gated_rows = attend(joined_rows, seg_ids.reshape(-1))
    token_pos = jnp.arange(local_rows, dtype=jnp.int32)
    owner_ids = jnp.arange(owners, dtype=jnp.int32)
    dest_owner = jnp.sum((token_pos[:, None] >= bin_ends[None, :]).astype(jnp.int32), axis=1)
    onehot = dest_owner[:, None] == owner_ids[None, :]
    first_slot = jnp.sum(jnp.where(onehot, bin_starts[None, :], 0), axis=1)
    back_rows = dest_owner * capacity + token_pos - first_slot
    returned = lax.all_to_all(
        gated_rows.reshape(owners, capacity, -1), "batch", split_axis=0, concat_axis=0, tiled=True
    )
    own_gated = returned.reshape(owners * capacity, -1)[back_rows]
    branch_rows = jnp.dot(own_gated, output_weight, preferred_element_type=F32).astype(BF16)
    return (hidden.astype(F32) + branch_rows.astype(F32)).astype(BF16)


def batch_index():
    return lax.axis_index("batch")


def is_last():
    return lax.axis_index("batch") == lax.axis_size("batch") - 1


def silu_of(values):
    half = 0.5 * values
    return half + half * jnp.tanh(half)


def head_weights(query, key, allowed):
    scores = lax.dot_general(query, key, (((1,), (1,)), ((), ())), preferred_element_type=F32)
    half = scores * (0.5 * HEAD_DIM ** (-0.5))
    return jnp.where(allowed, half + half * jnp.tanh(half), 0.0).astype(BF16)


def seg_column(seg_row):
    wide = jnp.broadcast_to(seg_row, (128, seg_row.shape[1]))
    return wide.T[:, :1]


def segments_kernel(counts, users, seg_out):
    rows = users.shape[1]
    owners = counts.shape[1]
    position = lax.broadcasted_iota(jnp.int32, (1, rows), 1)
    end = counts[:, :1]
    owner = (position >= end).astype(jnp.int32)
    for d in range(1, owners - 1):
        end = end + counts[:, d : d + 1]
        owner = owner + (position >= end).astype(jnp.int32)
    seg_out[...] = jnp.broadcast_to((owner + owners * users[...]).astype(F32), seg_out.shape)


def put_seg(ref, seg):
    rows = seg.shape[1]
    for at in range(0, ref.shape[1], rows):
        ref[rows:, at : at + rows] = seg.astype(BF16)


def silu_dot(normed, weight):
    return silu_of(jnp.dot(normed[...], weight[...], preferred_element_type=F32)).astype(BF16)


def is_upward():
    return lax.axis_index("col") % 2 == 0


def put_keys(normed, w_key, w_value, out):
    rows = normed.shape[0]
    group = w_key.shape[1]
    out[:rows, :group] = silu_dot(normed, w_key)
    out[:rows, group : 2 * group] = silu_dot(normed, w_value)


def put_query(normed, w_query, out):
    rows = normed.shape[0]
    group = w_query.shape[1]
    out[:rows, :group] = silu_dot(normed, w_query)
    out[:rows, group:] = jnp.zeros((rows, group), BF16)


def add_pieces(pieces, w_in, total):
    for shift, piece in pieces.items():
        width = piece.shape[1]
        start = pl.multiple_of((lax.axis_index("col") ^ shift) * width, width)
        term = jnp.dot(piece[...], w_in[pl.ds(start, width), :], preferred_element_type=F32)
        total = term if total is None else total + term
    return total


def partial_kernel(part2, part1, own, w_in, partial):
    partial[...] = add_pieces({0: own, 1: part1, 2: part2}, w_in, None)


def project_first_kernel(
    part3, partial, w_in, w_key, w_value, w_query, seg, hidden_out, normed, send_1
):
    total = add_pieces({3: part3}, w_in, partial[...])
    hidden = total.astype(BF16)
    hidden_out[...] = hidden
    normed[...] = layer_norm(hidden.astype(F32)).astype(BF16)
    put_seg(send_1, seg[...])

    @pl.when(is_upward())
    def _():
        put_keys(normed, w_key, w_value, send_1)

    @pl.when(~is_upward())
    def _():
        put_query(normed, w_query, send_1)


def project_second_kernel(
    normed, send_1, w_key, w_value, w_query, seg, send_2, far_keys, far_query
):
    rows = normed.shape[0]
    group = w_query.shape[1]
    put_seg(send_2, seg[...])

    @pl.when(is_upward())
    def _():
        put_query(normed, w_query, send_2)
        far_query[...] = send_2[:rows, :group]
        far_keys[...] = send_1[:rows, :]

    @pl.when(~is_upward())
    def _():
        put_keys(normed, w_key, w_value, send_2)
        far_query[...] = send_1[:rows, :group]
        far_keys[...] = send_2[:rows, :]


def sort_first_kernel(got_1, got_b, got_c):
    @pl.when(is_upward())
    def _():
        got_b[...] = got_1[...]

    @pl.when(~is_upward())
    def _():
        got_c[...] = got_1[:, : got_c.shape[1]]


def sort_second_kernel(got_2, up_in, down_in, got_b, got_c):
    @pl.when(is_upward())
    def _():
        got_c[...] = got_2[:, : got_c.shape[1]]

    @pl.when(~is_upward())
    def _():
        got_b[...] = got_2[...]


def project_query_kernel(normed, w_near, seg, send_2, send_f):
    rows = normed.shape[0]
    send_f[:rows, :] = silu_dot(normed, w_near)
    put_seg(send_f, seg[...])


def attend_own(send_a, send_f, far_keys, far_query, seg, normed, w_near, w_far, mixed, gate):
    rows, group = mixed.shape[1:]
    seg_row = seg[0:1, :]
    allowed = (seg_column(seg_row) == seg_row) & (
        lax.broadcasted_iota(jnp.int32, (rows, rows), 1)
        <= lax.broadcasted_iota(jnp.int32, (rows, rows), 0)
    )
    for side, (query, key_value) in enumerate(((send_f, send_a), (far_query, far_keys))):
        for lo in range(0, group, HEAD_DIM):
            hi = lo + HEAD_DIM
            weights = head_weights(query[:rows, lo:hi], key_value[:rows, lo:hi], allowed)
            mixed[side, :, lo:hi] = jnp.dot(
                weights, key_value[:rows, group + lo : group + hi], preferred_element_type=F32
            )


def project_near_kernel(
    send_f, far_keys, far_query, seg, normed, w_near, w_far, w_key, w_value, send_a, mixed, gate
):
    put_keys(normed, w_key, w_value, send_a)
    put_seg(send_a, seg[...])

    @pl.when(~is_last())
    def _():
        attend_own(send_a, send_f, far_keys, far_query, seg, normed, w_near, w_far, mixed, gate)


def seg_row_of(ref, rows):
    return ref[rows : rows + SEG_ROWS, :rows].astype(F32)[0:1, :]


def add_blocks(query, key_values, out):
    group = query.shape[1]
    rows = query.shape[0] - SEG_ROWS
    column = seg_column(seg_row_of(query, rows))
    masks = [column == seg_row_of(ref, rows) for ref in key_values]
    for lo in range(0, group, HEAD_DIM):
        hi = lo + HEAD_DIM
        total = None
        for ref, allowed in zip(key_values, masks):
            weights = head_weights(query[:rows, lo:hi], ref[:rows, lo:hi], allowed)
            term = jnp.dot(
                weights, ref[:rows, group + lo : group + hi], preferred_element_type=F32
            )
            total = term if total is None else total + term
        out[:, lo:hi] = total.astype(out.dtype)


def add_near(query, column, key_value, mixed):
    rows, group = mixed.shape
    allowed = column == seg_row_of(key_value, rows)
    for lo in range(0, group, HEAD_DIM):
        hi = lo + HEAD_DIM
        weights = head_weights(query[:rows, lo:hi], key_value[:rows, lo:hi], allowed)
        mixed[:, lo:hi] += jnp.dot(
            weights, key_value[:rows, group + lo : group + hi], preferred_element_type=F32
        )


def early_kernel(got_b, got_c, send_a, early_1, early_2):
    @pl.when(batch_index() == 0)
    def _():
        add_blocks(got_c, [send_a], early_1)

    @pl.when(batch_index() == 1)
    def _():
        add_blocks(got_c, [send_a, got_b], early_1)

    @pl.when(batch_index() == 2)
    def _():
        add_blocks(got_c, [send_a, got_b], early_2)


def far_kernel(got_b, got_c, got_f, send_a, early_1, send_e, send_g):
    @pl.when(batch_index() == 1)
    def _():
        add_blocks(got_f, [send_a, got_b], send_e)
        send_g[...] = early_1[...]

    @pl.when(batch_index() != 1)
    def _():
        send_e[...] = jnp.zeros_like(send_e)
        send_g[...] = jnp.zeros_like(send_g)


def far_d_kernel(early_1, early_2, got_c, got_a, send_d, total):
    @pl.when(batch_index() == 0)
    def _():
        send_d[...] = early_1[...]

    @pl.when(batch_index() == 2)
    def _():
        rows = total.shape[0]
        total[...] = early_2[...]
        add_near(got_c, seg_column(seg_row_of(got_c, rows)), got_a, total)
        send_d[...] = total[...].astype(BF16)

    @pl.when((batch_index() != 0) & (batch_index() != 2))
    def _():
        send_d[...] = jnp.zeros_like(send_d)


def near_kernel(
    got_a, got_b, send_a, send_f, far_keys, far_query, seg, normed, w_near, w_far,
    mixed_in, gate_in, mixed, gate,
):
    column = seg_column(seg[0:1, :])
    gate[0] = silu_dot(normed, w_near)
    gate[1] = silu_dot(normed, w_far)

    @pl.when(is_last())
    def _():
        attend_own(send_a, send_f, far_keys, far_query, seg, normed, w_near, w_far, mixed, gate)

    @pl.when(batch_index() > 0)
    def _():
        add_near(send_f, column, got_b, mixed.at[0])

    @pl.when(batch_index() == 2)
    def _():
        add_near(send_f, column, got_a, mixed.at[0])


def finish_kernel(mixed, got_d, got_eg, gate, hidden, w_out, out, staged, sems):
    near = batch_index() % 2
    last = is_last()
    got = got_eg[...].astype(F32)
    group = mixed.shape[2]
    sides = (
        mixed[0] + jnp.where(last, got, 0.0),
        mixed[1] + got_d[...].astype(F32) + jnp.where(last, 0.0, got),
    )
    total = sum(jnp.sum(side, axis=-1, keepdims=True) for side in sides)
    sides = [side - total / (2 * group) for side in sides]
    total = sum(jnp.sum(side * side, axis=-1, keepdims=True) for side in sides)
    scale = lax.rsqrt(total / (2 * group) + eps_norm)
    gates = [(side * scale * gate[i].astype(F32)).astype(BF16) for i, side in enumerate(sides)]
    columns = hidden.shape[1] // OUT_PARTS
    copies = []
    for part in range(OUT_PARTS):
        at = slice(part * columns, (part + 1) * columns)
        branch = None
        for which, gated in zip((near, 1 - near), gates):
            start = pl.multiple_of(which * group, group)
            term = jnp.dot(gated, w_out[pl.ds(start, group), at], preferred_element_type=F32)
            branch = term if branch is None else branch + term
        total = hidden[:, at].astype(F32) + branch.astype(BF16).astype(F32)
        staged[:, at] = total.astype(BF16)
        copies.append(pltpu.make_async_copy(staged.at[:, at], out.at[:, at], sems.at[part]))
        copies[-1].start()
    for copy in copies:
        copy.wait()


VMEM = pl.BlockSpec(memory_space=pltpu.VMEM)


def call(kernel, in_specs, outs, operands, flops, scratch=(), limit=32 << 20, aliases=()):
    return pl.pallas_call(
        kernel,
        out_shape=[jax.ShapeDtypeStruct(shape, dtype) for shape, dtype in outs],
        in_specs=in_specs,
        out_specs=[VMEM] * len(outs),
        scratch_shapes=list(scratch),
        input_output_aliases=dict(aliases),
        compiler_params=pltpu.CompilerParams(vmem_limit_bytes=limit),
        cost_estimate=pl.CostEstimate(flops=flops, bytes_accessed=0, transcendentals=0),
    )(*operands)


def chain_plan(lookups, input_weight, joined_weight, output_weight, owner_counts, user_index):
    cols = lax.axis_size("col")
    batch_at = lax.axis_index("batch").astype(jnp.int32)
    col_at = lax.axis_index("col").astype(jnp.int32)
    pieces = lookups.reshape(cols, lookups.shape[0] // cols, lookups.shape[1])
    rows = pieces.shape[1]

    def piece(source, shift):
        return lax.dynamic_index_in_dim(source, col_at ^ shift, 0, keepdims=False)

    def exchange(block, shift):
        return lax.ppermute(block, "col", [(i, i ^ shift) for i in range(cols)])

    across = piece(pieces, 2)
    pieces, across = lax.optimization_barrier((pieces, across))
    parts = [piece(pieces, 0)] + [
        exchange(across if shift == 2 else piece(pieces, shift), shift)
        for shift in range(1, cols)
    ]
    width = HEADS * HEAD_DIM
    group = width // 2
    features = input_weight.shape[1]
    tall = rows + SEG_ROWS
    (seg,) = call(
        segments_kernel,
        [VMEM] * 2,
        [((SEG_ROWS, rows), F32)],
        (owner_counts, user_index.reshape(1, rows)),
        1 << 30,
    )
    near = batch_at % 2
    far = 1 - near

    def weight_of(block, index):
        return lax.dynamic_slice_in_dim(joined_weight, block * width + index * group, group, 1)

    last = lax.axis_size("batch") - 1

    def up_and_down(block, parity):
        perm = []
        for at in range(cols):
            step = 1 if at % 2 == parity else -1
            for source in range(last + 1):
                inside = 0 <= source + step <= last
                target = (source + step, at) if inside else (source, at ^ 1)
                perm.append((source * cols + at, target[0] * cols + target[1]))
        return lax.ppermute(block, ("batch", "col"), perm)

    def closed(block, legs):
        perm = []
        for at in range(cols):
            for source in range(last + 1):
                target = (legs[source], at) if source in legs else (source, at ^ 1)
                perm.append((source * cols + at, target[0] * cols + target[1]))
        return lax.ppermute(block, ("batch", "col"), perm)

    far_weights = (weight_of(3, far), weight_of(1, far), weight_of(2, far))
    (partial,) = call(
        partial_kernel,
        [VMEM] * 4,
        [((rows, features), F32)],
        (parts[2], parts[1], parts[0], input_weight),
        rows,
    )
    hidden, normed, send_1 = call(
        project_first_kernel,
        [VMEM] * 7,
        [((rows, features), BF16), ((rows, features), BF16), ((tall, 2 * group), BF16)],
        (parts[3], partial, input_weight, *far_weights, seg),
        2 * rows * features * (features + 2 * group),
    )
    got_1 = up_and_down(send_1, 0)
    send_2, far_keys, far_query = call(
        project_second_kernel,
        [VMEM] * 6,
        [((tall, 2 * group), BF16), ((rows, 2 * group), BF16), ((rows, group), BF16)],
        (normed, send_1, *far_weights, seg),
        2 * rows * features * 2 * group,
    )
    got_2 = up_and_down(send_2, 1)
    (send_f,) = call(
        project_query_kernel,
        [VMEM] * 4,
        [((tall, group), BF16)],
        (normed, weight_of(2, near), seg, send_2),
        2 * rows * features * group,
    )
    got_f = lax.ppermute(send_f, "batch", [(3, 1)])
    own_inputs = (send_f, far_keys, far_query, seg, normed, weight_of(0, near), weight_of(0, far))
    own_outs = [((2, rows, group), F32), ((2, rows, group), BF16)]
    send_a, *own = call(
        project_near_kernel,
        [VMEM] * 9,
        [((tall, 2 * group), BF16)] + own_outs,
        (*own_inputs, weight_of(3, near), weight_of(1, near)),
        2 * rows * features * 2 * group,
    )
    got_a = lax.ppermute(send_a, "batch", [(0, 2)])
    sorted_outs = [((tall, 2 * group), BF16), ((tall, group), BF16)]
    got_b, got_c = call(sort_first_kernel, [VMEM], sorted_outs, (got_1,), 1 << 30)
    got_b, got_c = call(
        sort_second_kernel, [VMEM] * 3, sorted_outs, (got_2, got_b, got_c), rows,
        aliases={1: 0, 2: 1},
    )
    early_1, early_2 = call(
        early_kernel,
        [VMEM] * 3,
        [((rows, group), BF16), ((rows, group), F32)],
        (got_b, got_c, send_a),
        1 << 30,
    )
    send_e, send_g = call(
        far_kernel,
        [VMEM] * 5,
        [((rows, group), BF16)] * 2,
        (got_b, got_c, got_f, send_a, early_1),
        1 << 30,
    )
    got_e = lax.ppermute(send_e, "batch", [(1, 3)])
    got_g = closed(send_g, {1: 2, 2: 1})
    (send_d,) = call(
        far_d_kernel,
        [VMEM] * 4,
        [((rows, group), BF16)],
        (early_1, early_2, got_c, got_a),
        rows,
        [pltpu.VMEM((rows, group), F32)],
    )
    got_d = closed(send_d, {0: 1, 1: 0, 2: 3, 3: 2})
    mixed, gate = call(
        near_kernel,
        [VMEM] * 12,
        own_outs,
        (got_a, got_b, send_a, *own_inputs, *own),
        rows,
        aliases={10: 0, 11: 1},
    )
    return pl.pallas_call(
        finish_kernel,
        out_shape=jax.ShapeDtypeStruct((rows, features), BF16),
        in_specs=[VMEM] * 6,
        out_specs=pl.BlockSpec(memory_space=pl.ANY),
        scratch_shapes=[
            pltpu.VMEM((rows, features), BF16),
            pltpu.SemaphoreType.DMA((OUT_PARTS,)),
        ],
        compiler_params=pltpu.CompilerParams(vmem_limit_bytes=32 << 20),
        cost_estimate=pl.CostEstimate(flops=rows, bytes_accessed=0, transcendentals=0),
    )(mixed, got_d, got_e + got_g, gate, hidden, output_weight)


def solution(mesh):
    chain = mesh.shape["batch"] == 4 and mesh.shape["col"] == 4
    return jax.shard_map(
        chain_plan if chain else owners_plan,
        mesh=mesh,
        in_specs=(
            P(("rep", "batch"), "col"),
            P(),
            P(),
            P(),
            P(("rep", "batch", "col"), None),
            P(("rep", "batch", "col")),
        ),
        out_specs=P(("rep", "batch", "col"), None),
        check_vma=False,
    )
```
